32 devices in a mesh: fsdp: 8 (over y, x, core), ctx: 4 (over z).
Axes of the slice: x: 2, y: 2, z: 4, core: 2. Of those that a mesh axis runs over, the one named last changes fastest.
Arguments:
- hidden_in: bfloat16 [8192, 1024], P(('fsdp', 'ctx')), may hold values from -6 to 6
- segments: int32 [8192], P(('fsdp', 'ctx')), may hold values from 0 to 2, as said below
- cotangent: bfloat16 [8192, 1024], P(('fsdp', 'ctx')), may hold values from -6 to 6
- mixer_in: bfloat16 [1024, 4120], P(('fsdp', 'ctx')), may hold values from -0.1875 to 0.1875
- mixer_out: bfloat16 [2048, 1024], P(None, ('fsdp', 'ctx')), may hold values from -0.25 to 0.25
- gate_up: bfloat16 [1024, 4096], P(('fsdp', 'ctx')), may hold values from -0.1875 to 0.1875
- down_weight: bfloat16 [2048, 1024], P(None, ('fsdp', 'ctx')), may hold values from -0.125 to 0.125
- norm_gain: float32 [1024], replicated, may hold values from 0.5 to 1.5
- feed_gain: float32 [1024], replicated, may hold values from 0.5 to 1.5
- step_bias: float32 [24], replicated, may hold values from -6 to -2
- decay_log: float32 [24], replicated, may hold values from -3.5 to 1
- skip_gain: float32 [24], replicated, may hold values from 0.5 to 1.5
Outputs:
- layer_out: bfloat16 [8192, 1024], P(('fsdp', 'ctx'))
- input_grad: bfloat16 [8192, 1024], P(('fsdp', 'ctx'))
- mixer_in_grad: float32 [1024, 4120], P(('fsdp', 'ctx'))
- mixer_out_grad: float32 [2048, 1024], P(None, ('fsdp', 'ctx'))
- gate_up_grad: float32 [1024, 4096], P(('fsdp', 'ctx'))
- down_grad: float32 [2048, 1024], P(None, ('fsdp', 'ctx'))
- norm_gain_grad: float32 [1024], replicated
- feed_gain_grad: float32 [1024], replicated
- step_bias_grad: float32 [24], replicated
- decay_log_grad: float32 [24], replicated
- skip_gain_grad: float32 [24], replicated
The draws below stay inside these ranges and needn't reach their ends.
Inputs may be any that keep to these rules, and one draw needn't show every extreme that they name: `segments`: in each sequence of 1024 tokens the numbers start at 0 and never fall; they rise at two document starts (by two at once where both starts coincide), the first at one of the positions 1 to 256, the second at one of the positions 768 to 1023; a start may fall on the first token of a sequence piece.
All inputs are finite; a program needn't handle non-finite values.
Results may differ from the reference program's by a relative error of at most 0.012.
Values may be sent and summed in bfloat16 or wider, within the bound.
No kernel may reach another device: no remote copies, remote signals or barrier semaphores. Data moves between devices by JAX's collectives and lax.ppermute only.
A program may use at most 256 MiB of HBM per device.

```python
import jax
import jax.numpy as jnp
from jax import lax

D = 1024
FF = 2048
SH = 24
SP = 64
NS = 128
QUERY_HEADS = 8
KEY_VALUE_HEADS = 2
HEAD_SIZE = 64
SEQUENCE_LENGTH = 1024
SEQ_DEV = 256
TOKENS = 8192
CIN = 4120
CMID = 2048
N_CTX = 4


def draw_segments(key, part):
    key = jax.random.fold_in(key, 11)
    first_key, second_key = jax.random.split(key)
    sequence_batch = TOKENS // SEQUENCE_LENGTH
    opening = jax.random.randint(first_key, (sequence_batch, 1), 1, SEQ_DEV + 1)
    closing = SEQUENCE_LENGTH - jax.random.randint(second_key, (sequence_batch, 1), 1, SEQ_DEV + 1)
    token_position = jnp.arange(SEQUENCE_LENGTH)[None, :]
    numbers = (token_position >= opening).astype(jnp.int32) + (token_position >= closing).astype(jnp.int32)
    return numbers.reshape(TOKENS)


def shard_levels(rng, dims, cuts, smallest, top_value):
    def one(axis_at, parts):
        steps = jax.random.uniform(jax.random.fold_in(jax.random.fold_in(rng, 6), axis_at), (parts,), jnp.float32, smallest / len(cuts), top_value / len(cuts))
        return jnp.repeat(jnp.exp(steps), dims[axis_at] // parts).reshape((-1,) + (1,) * (len(dims) - axis_at - 1))

    gain = one(*cuts[0])
    for cut in cuts[1:]:
        gain = gain * one(*cut)
    return gain


def scatter_about(rng, extent, scale, bound, cuts=(), kind=jnp.bfloat16):
    array = jax.random.normal(rng, extent, jnp.float32) * scale
    if len(cuts) > 0:
        array = shard_levels(rng, extent, cuts, -0.22, 0.18) * array
    return jnp.clip(array, min=-bound, max=bound).astype(kind)


def setup_inputs(seed: int = 0) -> dict:
    key_list = jax.random.split(jax.random.key(seed), 13)
    hidden_in = scatter_about(key_list[0], (TOKENS, D), 1.0, 6.0, ((0, 32),))
    segments = draw_segments(jax.random.fold_in(key_list[12], 71), 0)
    cotangent = scatter_about(key_list[2], (TOKENS, D), 1.0, 6.0, ((0, 32),))
    mixer_in = scatter_about(key_list[3], (D, CIN), D ** -0.5, 0.1875, ((0, 32),))
    mixer_out = scatter_about(key_list[4], (CMID, D), (CMID // 4) ** -0.5, 0.25, ((1, 32),))
    gate_up = scatter_about(key_list[5], (D, 2 * FF), D ** -0.5, 0.1875, ((0, 32),))
    down_weight = scatter_about(key_list[6], (FF, D), FF ** -0.5, 0.125, ((1, 32),))
    norm_gain = jnp.clip(1.0 + 0.1 * jax.random.normal(key_list[7], (D,), jnp.float32), 0.5, 1.5)
    feed_gain = jnp.clip(1.0 + 0.1 * jax.random.normal(key_list[8], (D,), jnp.float32), 0.5, 1.5)
    step_bias = jnp.clip(jax.random.uniform(key_list[9], (SH,), jnp.float32, -6.0, -2.0), -6.0, -2.0)
    decay_log = jnp.clip(jax.random.uniform(key_list[10], (SH,), jnp.float32, -3.5, 1.0), -3.5, 1.0)
    skip_gain = jnp.clip(jax.random.uniform(key_list[11], (SH,), jnp.float32, 0.5, 1.5), 0.5, 1.5)
    return dict(hidden_in=hidden_in, segments=segments, cotangent=cotangent, mixer_in=mixer_in, mixer_out=mixer_out, gate_up=gate_up, down_weight=down_weight, norm_gain=norm_gain, feed_gain=feed_gain, step_bias=step_bias, decay_log=decay_log, skip_gain=skip_gain)


EPSILON = 1e-06
ROTARY_BASE = 100000000000.0
HIGHEST = lax.Precision.HIGHEST

@jax.custom_vjp
def lower_bound(v):
    return lax.optimization_barrier(v.astype(jnp.bfloat16)).astype(jnp.float32)

@jax.custom_vjp
def low_back(v):
    return v

def low_keep(v):
    return (lower_bound(v), None)

def low_pass(kept, grad):
    return (grad,)

def back_keep(v):
    return (v, None)

def back_low(kept, grad):
    return (lower_bound(grad),)
lower_bound.defvjp(low_keep, low_pass)
low_back.defvjp(back_keep, back_low)

def matmul(left, right):
    return jnp.dot(left, right, precision=HIGHEST, preferred_element_type=jnp.float32)

def apply_rotation(tensor, token_position):
    half_width = tensor.shape[-1] // 2
    exponent = jnp.arange(half_width, dtype=jnp.float32) * (-2.0 / tensor.shape[-1])
    frequency = ROTARY_BASE ** exponent
    angles = token_position[:, None] * frequency[None, :]
    cosine = jnp.cos(angles)[:, None, :]
    sine_part = jnp.sin(angles)[:, None, :]
    first_half = tensor[..., :half_width]
    second = tensor[..., half_width:]
    return jnp.concatenate([first_half * cosine - second * sine_part, second * cosine + first_half * sine_part], axis=-1)

def attention_sequence(query_rows, key_rows, value_rows, segment_label):
    document_length = query_rows.shape[0]
    scores = low_back(jnp.einsum('qgrd,kgd->grqk', query_rows, key_rows, precision=HIGHEST))
    indices = jnp.arange(document_length)
    allowed = (indices[:, None] >= indices[None, :]) & (segment_label[:, None] == segment_label[None, :])
    scores = jnp.where(allowed[None, None], scores, -1e+30)
    chance = jax.nn.softmax(scores, axis=-1)
    mixed = jnp.einsum('grqk,kgd->qgrd', lower_bound(chance), value_rows, precision=HIGHEST)
    return mixed.reshape(document_length, QUERY_HEADS * HEAD_SIZE)

def ssm_block(inputs_x, input_b, input_c, step_raw, segment_label, previous, carry_state, step_bias, decay_log, skip_gain):
    count_of_rows = inputs_x.shape[0]
    values_x = inputs_x.reshape(count_of_rows, SH, SP)
    step_size = jax.nn.softplus(step_raw + step_bias)
    decay_rate = -jnp.exp(decay_log) * step_size
    running = jnp.cumsum(decay_rate, axis=0)
    indices = jnp.arange(count_of_rows)
    allowed = (indices[:, None] >= indices[None, :]) & (segment_label[:, None] == segment_label[None, :])
    spread = jnp.minimum(running[:, None, :] - running[None, :, :], 0.0)
    weights = jnp.where(allowed[:, :, None], jnp.exp(spread), 0.0) * step_size[None, :, :]
    intersection = matmul(input_c, input_b.T)
    carried = jnp.where((segment_label == previous)[:, None], jnp.exp(running), 0.0)
    result = jnp.einsum('tsh,shp->thp', weights * intersection[:, :, None], values_x, precision=HIGHEST)
    result = result + skip_gain[None, :, None] * values_x
    result = result + carried[:, :, None] * jnp.einsum('tn,hpn->thp', input_c, carry_state, precision=HIGHEST)
    tail_weight = jnp.where((segment_label == segment_label[-1])[:, None], jnp.exp(running[-1][None, :] - running), 0.0) * step_size
    new_state = jnp.einsum('sh,shp,sn->hpn', tail_weight, values_x, input_b, precision=HIGHEST)
    new_state = new_state + carried[-1][:, None, None] * carry_state
    return (result.reshape(count_of_rows, SH * SP), new_state)

def ssm_sequence(inputs_x, input_b, input_c, step_raw, segment_label, step_bias, decay_log, skip_gain):
    block_rows = SEQUENCE_LENGTH // N_CTX
    pieces = tuple((source.reshape((N_CTX, block_rows) + source.shape[1:]) for source in (inputs_x, input_b, input_c, step_raw, segment_label)))

    def advance(carry, block):
        carry_state, previous = carry
        output, new_state = ssm_block(block[0], block[1], block[2], block[3], block[4], previous, carry_state, step_bias, decay_log, skip_gain)
        return ((new_state, block[4][-1]), output)
    start = (jnp.zeros((SH, SP, NS), jnp.float32), jnp.full((), -1.0, jnp.float32))
    unused, outputs = lax.scan(jax.checkpoint(advance), start, pieces)
    return outputs.reshape(SEQUENCE_LENGTH, SH * SP)

def layer(hidden, segment_label, mixer_in, mixer_out, gate_up, down_weight, norm_gain, feed_gain, step_bias, decay_log, skip_gain):
    count_of_tokens = hidden.shape[0]
    sequence_batch = count_of_tokens // SEQUENCE_LENGTH
    mixer_width = SH * SP
    inv_first = lax.rsqrt(lax.optimization_barrier(jnp.mean(hidden * hidden, axis=-1, keepdims=True)) + EPSILON)
    normed = lower_bound(hidden * inv_first * norm_gain)
    apply_projection = low_back(matmul(normed, mixer_in))
    gate_z = apply_projection[:, :mixer_width]
    inputs_x = apply_projection[:, mixer_width:2 * mixer_width]
    input_b = apply_projection[:, 2 * mixer_width:2 * mixer_width + NS]
    input_c = apply_projection[:, 2 * mixer_width + NS:2 * mixer_width + 2 * NS]
    token_offset = 2 * mixer_width + 2 * NS
    step_raw = apply_projection[:, token_offset:token_offset + SH]
    token_offset = token_offset + SH
    query_raw = apply_projection[:, token_offset:token_offset + QUERY_HEADS * HEAD_SIZE]
    unrotated_key = apply_projection[:, token_offset + QUERY_HEADS * HEAD_SIZE:token_offset + (QUERY_HEADS + KEY_VALUE_HEADS) * HEAD_SIZE]
    unprojected_value = apply_projection[:, token_offset + (QUERY_HEADS + KEY_VALUE_HEADS) * HEAD_SIZE:]
    token_position = (jnp.arange(count_of_tokens) % SEQUENCE_LENGTH).astype(jnp.float32)
    query_rows = lower_bound(apply_rotation(query_raw.reshape(count_of_tokens, QUERY_HEADS, HEAD_SIZE), token_position) * HEAD_SIZE ** (-0.5))
    key_rows = lower_bound(apply_rotation(unrotated_key.reshape(count_of_tokens, KEY_VALUE_HEADS, HEAD_SIZE), token_position))
    value_rows = lower_bound(unprojected_value.reshape(count_of_tokens, KEY_VALUE_HEADS, HEAD_SIZE))

    def attend_single(items):
        return attention_sequence(items[0], items[1], items[2], items[3])
    attention_result = lax.map(jax.checkpoint(attend_single), (query_rows.reshape(sequence_batch, SEQUENCE_LENGTH, KEY_VALUE_HEADS, QUERY_HEADS // KEY_VALUE_HEADS, HEAD_SIZE), key_rows.reshape(sequence_batch, SEQUENCE_LENGTH, KEY_VALUE_HEADS, HEAD_SIZE), value_rows.reshape(sequence_batch, SEQUENCE_LENGTH, KEY_VALUE_HEADS, HEAD_SIZE), segment_label.reshape(sequence_batch, SEQUENCE_LENGTH)))
    attention_result = lower_bound(low_back(attention_result.reshape(count_of_tokens, QUERY_HEADS * HEAD_SIZE)))

    def mix_one(items):
        return ssm_sequence(items[0], items[1], items[2], items[3], items[4], step_bias, decay_log, skip_gain)
    ssm_out = lax.map(mix_one, (inputs_x.reshape(sequence_batch, SEQUENCE_LENGTH, mixer_width), input_b.reshape(sequence_batch, SEQUENCE_LENGTH, NS), input_c.reshape(sequence_batch, SEQUENCE_LENGTH, NS), step_raw.reshape(sequence_batch, SEQUENCE_LENGTH, SH), segment_label.reshape(sequence_batch, SEQUENCE_LENGTH))).reshape(count_of_tokens, mixer_width)
    gated = lower_bound(ssm_out * jax.nn.silu(gate_z))
    middle = jnp.concatenate([gated, attention_result], axis=1)
    residual = hidden + low_back(matmul(middle, mixer_out))
    inv_second = lax.rsqrt(lax.optimization_barrier(jnp.mean(residual * residual, axis=-1, keepdims=True)) + EPSILON)
    normed_two = lower_bound(residual * inv_second * feed_gain)
    gate_both = low_back(matmul(normed_two, gate_up))
    active = lower_bound(jax.nn.silu(gate_both[:, :FF]) * gate_both[:, FF:])
    return residual + low_back(matmul(active, down_weight))

def reference(hidden_in, segments, cotangent, mixer_in, mixer_out, gate_up, down_weight, norm_gain, feed_gain, step_bias, decay_log, skip_gain):
    segment_label = segments.astype(jnp.float32)

    def forward(hidden, weight_in, weight_out, weight_gate, weight_down, gain_one, gain_two, bias_step, log_decay, gain_skip):
        return layer(hidden, segment_label, weight_in, weight_out, weight_gate, weight_down, gain_one, gain_two, bias_step, log_decay, gain_skip)
    layer_out, pullback = jax.vjp(forward, hidden_in.astype(jnp.float32), mixer_in.astype(jnp.float32), mixer_out.astype(jnp.float32), gate_up.astype(jnp.float32), down_weight.astype(jnp.float32), norm_gain, feed_gain, step_bias, decay_log, skip_gain)
    grads = pullback(cotangent.astype(jnp.float32))
    return (layer_out.astype(jnp.bfloat16), grads[0].astype(jnp.bfloat16), grads[1], grads[2], grads[3], grads[4], grads[5], grads[6], grads[7], grads[8], grads[9])
```

```python
import jax
import jax.numpy as jnp
from jax import lax
from jax.sharding import PartitionSpec as P

FF = 2048
SH = 24
SP = 64
NS = 128
QUERY_HEADS = 8
KEY_VALUE_HEADS = 2
HEAD_SIZE = 64


EPSILON = 1e-06
ROTARY_BASE = 100000000000.0


def swap(value, mask):
    size = lax.axis_size("fsdp")
    return lax.ppermute(value, "fsdp", [(i, i ^ mask) for i in range(size)])


def swap_ctx(value, mask):
    size = lax.axis_size("ctx")
    return lax.ppermute(value, "ctx", [(i, i ^ mask) for i in range(size)])


def chip_masks():
    bits = lax.axis_size("fsdp").bit_length() - 2
    masks = [2 << i for i in range(bits)]
    x_masks, y_masks = masks[: bits // 2], masks[bits // 2 :]
    return (y_masks + x_masks, x_masks + y_masks)


def gather_weight(shard):
    part = lax.all_gather(shard, "ctx", axis=0, tiled=True)
    half = part.shape[0] // 2
    own = []
    for piece, masks in zip((part[:half], part[half:]), chip_masks()):
        for mask in masks:
            piece = jnp.concatenate([piece, swap(piece, mask)], axis=0)
        own.append(piece)
    other = [swap(piece, 1) for piece in own]
    return jnp.concatenate(own + other, axis=0)


def plus(left, right):
    return (left.astype(jnp.float32) + right.astype(jnp.float32)).astype(jnp.bfloat16)


def scatter_weight(kept, sent):
    arrived = swap(sent, 1)
    quarter = kept.shape[0] // 2
    ends = []
    for h, masks in enumerate(chip_masks()):
        rows = slice(h * quarter, (h + 1) * quarter)
        piece = plus(kept[rows], arrived[rows])
        for mask in reversed(masks):
            n = piece.shape[0] // 2
            piece = plus(piece[:n], swap(piece[n:], mask))
        ends.append(piece)
    return lax.psum_scatter(
        jnp.concatenate(ends, axis=0), "ctx", scatter_dimension=0, tiled=True
    ).astype(jnp.float32)


def weight_half(rows, columns, half):
    n = rows.shape[1] // 2
    return jnp.einsum(
        "td,tc->dc",
        rows[:, half * n : (half + 1) * n],
        columns,
        preferred_element_type=jnp.float32,
    ).astype(jnp.bfloat16)


def weight_grad(rows, columns):
    return scatter_weight(weight_half(rows, columns, 0), weight_half(rows, columns, 1))


def width_order(width):
    devices, pieces = lax.axis_size("fsdp"), lax.axis_size("ctx")
    rows = width // (devices * pieces)
    place = jnp.arange(width)
    core = place // (width // 2)
    half = (place // (width // 4)) % 2
    inner = place % (width // 4)
    along = (inner // rows) % (pieces // 2) + half * (pieces // 2)
    chip = inner // (rows * (pieces // 2))
    offset = core
    for i, (mask_a, mask_b) in enumerate(zip(*chip_masks())):
        bit = (chip >> i) & 1
        offset = offset + bit * jnp.where(half == 0, mask_a, mask_b)
    device = lax.axis_index("fsdp") ^ offset
    return (device * pieces + along) * rows + inner % rows


def gather_ctx(value):
    size = lax.axis_size("ctx")
    blocks = [value]
    if size == 4:
        one, two = swap_ctx(value, 1), swap_ctx(value, 2)
        return [value, one, two, swap_ctx(two, 1)]
    mask = 1
    while mask < size:
        blocks = blocks + [swap_ctx(block, mask) for block in blocks]
        mask *= 2
    return blocks


def scatter_ctx(blocks):
    size = lax.axis_size("ctx")
    if size == 4:
        two = plus(blocks[2], swap_ctx(blocks[3], 1))
        one = swap_ctx(blocks[1], 1)
        total = blocks[0].astype(jnp.float32) + one.astype(jnp.float32)
        return total + swap_ctx(two, 2).astype(jnp.float32)
    while size > 1:
        size //= 2
        blocks = [plus(blocks[j], swap_ctx(blocks[j + size], size)) for j in range(size)]
    return blocks[0].astype(jnp.float32)


def total_over_all(value):
    for axis in ("fsdp", "ctx"):
        size, mask = lax.axis_size(axis), 1
        while mask < size:
            pairs = [(i, i ^ mask) for i in range(size)]
            value = value + lax.ppermute(value, axis, pairs)
            mask *= 2
    return value


def entering(decay, state, reverse):
    heads, channels, size = state.shape
    devices, position = (lax.axis_size("ctx"), lax.axis_index("ctx"))
    rows = heads * channels
    packed = jnp.concatenate(
        [
            state.reshape(rows, size).astype(jnp.bfloat16),
            jnp.broadcast_to(
                jnp.pad(decay, (0, size - heads)).astype(jnp.bfloat16)[None], (16, size)
            ),
        ],
        axis=0,
    )
    everything = lax.all_gather(packed, "ctx")
    total = jnp.zeros((heads, channels, size), jnp.float32)
    for k in range(devices):
        at = devices - 1 - k if reverse else k
        reached = at > position if reverse else at < position
        rate = everything[at, rows, :heads].astype(jnp.float32)
        part = everything[at, :rows].astype(jnp.float32).reshape(heads, channels, size)
        total = jnp.where(reached, rate[:, None, None] * total + part, total)
    return total


def apply_rotation(tensor, token_position):
    half_width = tensor.shape[-1] // 2
    exponent = jnp.arange(half_width, dtype=jnp.float32) * (-2.0 / tensor.shape[-1])
    frequency = ROTARY_BASE**exponent
    angles = token_position[:, None] * frequency[None, :]
    cosine = jnp.cos(angles)[:, None, :]
    sine_part = jnp.sin(angles)[:, None, :]
    first_half = tensor[..., :half_width]
    second = tensor[..., half_width:]
    return jnp.concatenate(
        [first_half * cosine - second * sine_part, second * cosine + first_half * sine_part],
        axis=-1,
    )


def silu_slope(value_rows):
    logistic = jax.nn.sigmoid(value_rows)
    return logistic * (1.0 + value_rows * (1.0 - logistic))


def block_terms(
    inputs_x, input_b, input_c, step_raw, segment_label, previous, step_bias, decay_log, skip_gain
):
    count_of_rows = inputs_x.shape[0]
    values_x = inputs_x.reshape(count_of_rows, SH, SP)
    step_size = jax.nn.softplus(step_raw + step_bias)
    decay_rate = -jnp.exp(decay_log) * step_size
    running = jnp.cumsum(decay_rate, axis=0)
    indices = jnp.arange(count_of_rows)
    allowed = (indices[:, None] >= indices[None, :]) & (
        segment_label[:, None] == segment_label[None, :]
    )
    spread = jnp.minimum(running[:, None, :] - running[None, :, :], 0.0)
    weights = jnp.where(allowed[:, :, None], jnp.exp(spread), 0.0) * step_size[None, :, :]
    intersection = jnp.dot(
        input_c, input_b.T, preferred_element_type=jnp.float32
    )
    carried = jnp.where((segment_label == previous)[:, None], jnp.exp(running), 0.0)
    own_part = jnp.einsum(
        "tsh,shp->thp", weights * intersection[:, :, None], values_x
    )
    own_part = own_part + skip_gain[None, :, None] * values_x
    tail_weight = (
        jnp.where(
            (segment_label == segment_label[-1])[:, None],
            jnp.exp(running[-1][None, :] - running),
            0.0,
        )
        * step_size
    )
    end_state = jnp.einsum("sh,shp,sn->hpn", tail_weight, values_x, input_b)
    return (own_part, end_state, carried)


def local(
    hidden_in,
    segments,
    cotangent,
    mixer_in,
    mixer_out,
    gate_up,
    down_weight,
    norm_gain,
    feed_gain,
    step_bias,
    decay_log,
    skip_gain,
):
    mixer_width = SH * SP
    width = hidden_in.shape[1]
    edges = [mixer_width, 2 * mixer_width, 2 * mixer_width + 2 * NS]
    edges += [edges[-1] + SH, mixer_in.shape[1]]
    in_z = mixer_in[:, : edges[0]]
    in_mix = jnp.concatenate(
        [
            mixer_in[:, edges[0] : edges[2]],
            mixer_in[:, edges[3] : edges[4]],
            mixer_in[:, edges[2] : edges[3]],
        ],
        axis=1,
    )
    full_mix = gather_weight(in_mix)
    full_mid = gather_weight(jnp.concatenate([in_z, mixer_out.T], axis=1))
    full_z, out_turned = full_mid[:, :mixer_width], full_mid[:, mixer_width:]
    full_gate_up = gather_weight(gate_up)
    down_turned = gather_weight(down_weight.T)
    order = width_order(width)
    turn = (jnp.arange(width)[:, None] == order[None, :]).astype(jnp.bfloat16)
    hidden_in, cotangent = (
        jnp.dot(v, turn, preferred_element_type=jnp.float32).astype(jnp.bfloat16)
        for v in (hidden_in, cotangent)
    )
    gains = jnp.dot(
        jnp.stack([norm_gain, feed_gain]),
        turn.astype(jnp.float32),
        precision=lax.Precision.HIGHEST,
    )
    norm_gain, feed_gain = gains[0], gains[1]
    count_of_rows = hidden_in.shape[0]
    mixer_width = SH * SP
    repeat_heads = QUERY_HEADS // KEY_VALUE_HEADS
    hidden = hidden_in.astype(jnp.float32)
    inv_first = lax.rsqrt(jnp.mean(hidden * hidden, axis=-1, keepdims=True) + EPSILON)
    normed = (hidden * inv_first * norm_gain).astype(jnp.bfloat16)
    gate_z = jnp.dot(normed, full_z, preferred_element_type=jnp.float32)
    apply_projection = jnp.dot(normed, full_mix, preferred_element_type=jnp.float32)
    inputs_x = apply_projection[:, :mixer_width]
    input_b = apply_projection[:, mixer_width : mixer_width + NS]
    input_c = apply_projection[:, mixer_width + NS : mixer_width + 2 * NS]
    token_offset = mixer_width + 2 * NS
    query_raw = apply_projection[:, token_offset : token_offset + QUERY_HEADS * HEAD_SIZE]
    token_offset = token_offset + QUERY_HEADS * HEAD_SIZE
    unrotated_key = apply_projection[
        :, token_offset : token_offset + KEY_VALUE_HEADS * HEAD_SIZE
    ]
    token_offset = token_offset + KEY_VALUE_HEADS * HEAD_SIZE
    unprojected_value = apply_projection[
        :, token_offset : token_offset + KEY_VALUE_HEADS * HEAD_SIZE
    ]
    step_raw = apply_projection[:, token_offset + KEY_VALUE_HEADS * HEAD_SIZE :]
    piece_index = lax.axis_index("ctx")
    query_place = piece_index * count_of_rows + jnp.arange(count_of_rows)
    token_position = query_place.astype(jnp.float32)
    query_rows = (
        apply_rotation(query_raw.reshape(count_of_rows, QUERY_HEADS, HEAD_SIZE), token_position)
        * HEAD_SIZE ** (-0.5)
    ).astype(jnp.bfloat16)
    keys_own = (
        apply_rotation(
            unrotated_key.reshape(count_of_rows, KEY_VALUE_HEADS, HEAD_SIZE), token_position
        )
        .astype(jnp.bfloat16)
        .reshape(count_of_rows, KEY_VALUE_HEADS * HEAD_SIZE)
    )
    values_own = unprojected_value.astype(jnp.bfloat16)
    segment_float = segments.astype(jnp.float32)
    pieces = lax.axis_size("ctx")
    key_width = KEY_VALUE_HEADS * HEAD_SIZE
    gathered = jnp.concatenate(
        gather_ctx(jnp.concatenate([keys_own, values_own], axis=1)), axis=0
    )
    gathered_keys, gathered_values = gathered[:, :key_width], gathered[:, key_width:]
    document_length = gathered_keys.shape[0]
    segment_all = lax.all_gather(segment_float.astype(jnp.bfloat16), "ctx").astype(jnp.float32)
    before_index = jnp.maximum(piece_index - 1, 0)
    before_value = lax.dynamic_index_in_dim(segment_all, before_index, 0, keepdims=False)[-1]
    previous = jnp.where(piece_index > 0, before_value, -1.0)
    block_of = piece_index ^ jnp.arange(pieces)
    segment_all = jnp.take(segment_all, block_of, axis=0).reshape(-1)
    key_place = (block_of[:, None] * count_of_rows + jnp.arange(count_of_rows)[None]).reshape(-1)
    grouped_queries = query_rows.reshape(count_of_rows, KEY_VALUE_HEADS, repeat_heads, HEAD_SIZE)
    grouped_keys = gathered_keys.reshape(document_length, KEY_VALUE_HEADS, HEAD_SIZE)
    grouped_values = gathered_values.reshape(document_length, KEY_VALUE_HEADS, HEAD_SIZE)
    scores = jnp.einsum(
        "qgrd,kgd->grqk", grouped_queries, grouped_keys, preferred_element_type=jnp.float32
    )
    allowed = (query_place[:, None] >= key_place[None, :]) & (
        segment_float[:, None] == segment_all[None, :]
    )
    scores = jnp.where(allowed, scores, -1e30)
    highest = jnp.max(scores, axis=-1, keepdims=True)
    expanded = jnp.exp(scores - highest)
    chance = expanded / jnp.sum(expanded, axis=-1, keepdims=True)
    chance_low = chance.astype(jnp.bfloat16)
    attention_result = jnp.einsum(
        "grqk,kgd->qgrd", chance_low, grouped_values, preferred_element_type=jnp.float32
    ).reshape(count_of_rows, QUERY_HEADS * HEAD_SIZE)
    own_part, end_state, carried = block_terms(
        inputs_x,
        input_b,
        input_c,
        step_raw,
        segment_float,
        previous,
        step_bias,
        decay_log,
        skip_gain,
    )
    carry_state = entering(carried[-1], end_state, False)
    mixer_state = own_part + carried[:, :, None] * jnp.einsum(
        "tn,hpn->thp", input_c, carry_state
    )
    ssm_out = mixer_state.reshape(count_of_rows, mixer_width)
    silu_z = jax.nn.silu(gate_z)
    gated = ssm_out * silu_z
    middle = jnp.concatenate(
        [gated.astype(jnp.bfloat16), attention_result.astype(jnp.bfloat16)], axis=1
    )
    residual = hidden + jnp.einsum(
        "tc,dc->td", middle, out_turned, preferred_element_type=jnp.float32
    )
    inv_second = lax.rsqrt(jnp.mean(residual * residual, axis=-1, keepdims=True) + EPSILON)
    normed_two = (residual * inv_second * feed_gain).astype(jnp.bfloat16)
    gate_both = jnp.dot(normed_two, full_gate_up, preferred_element_type=jnp.float32)
    gate_part = gate_both[:, :FF]
    up_part = gate_both[:, FF:]
    silu_gate = jax.nn.silu(gate_part)
    active = (silu_gate * up_part).astype(jnp.bfloat16)
    layer_out = (
        residual + jnp.einsum("tf,df->td", active, down_turned, preferred_element_type=jnp.float32)
    ).astype(jnp.bfloat16)
    back_out, back_gate_up, back_down = (out_turned, full_gate_up, down_turned)
    grad_output = cotangent.astype(jnp.float32)
    owned_down = weight_grad(cotangent, active)
    grad_active = jnp.einsum("td,df->tf", cotangent, back_down, preferred_element_type=jnp.float32)
    grad_gate = grad_active * up_part * silu_slope(gate_part)
    grad_upper = grad_active * silu_gate
    grad_both = jnp.concatenate([grad_gate, grad_upper], axis=1).astype(jnp.bfloat16)
    owned_gate_up = weight_grad(normed_two, grad_both)
    grad_two = jnp.einsum("tf,df->td", grad_both, back_gate_up, preferred_element_type=jnp.float32)
    grad_feed_gain = jnp.sum(grad_two * residual * inv_second, axis=0)
    scaled_two = grad_two * feed_gain
    grad_residual = (
        grad_output
        + inv_second * scaled_two
        - residual
        * (inv_second * inv_second * inv_second)
        * jnp.mean(scaled_two * residual, axis=-1, keepdims=True)
    )
    grad_mix = grad_residual.astype(jnp.bfloat16)
    gradient_between = jnp.einsum(
        "td,dc->tc", grad_mix, back_out, preferred_element_type=jnp.float32
    )
    grad_gated = gradient_between[:, :mixer_width]
    grad_group = (
        gradient_between[:, mixer_width:]
        .astype(jnp.bfloat16)
        .reshape(count_of_rows, KEY_VALUE_HEADS, repeat_heads, HEAD_SIZE)
    )
    grad_chance = jnp.einsum(
        "qgrd,kgd->grqk", grad_group, grouped_values, preferred_element_type=jnp.float32
    )
    inner_total = jnp.sum(chance * grad_chance, axis=-1, keepdims=True)
    grad_scores = (chance * (grad_chance - inner_total)).astype(jnp.bfloat16)
    grad_queries = jnp.einsum(
        "grqk,kgd->qgrd", grad_scores, grouped_keys, preferred_element_type=jnp.float32
    )
    key_contributions = jnp.einsum(
        "grqk,qgrd->kgd", grad_scores, grouped_queries, preferred_element_type=jnp.float32
    )
    value_contributions = jnp.einsum(
        "grqk,qgrd->kgd", chance_low, grad_group, preferred_element_type=jnp.float32
    )
    both_gradients = jnp.concatenate(
        [
            key_contributions.reshape(document_length, key_width),
            value_contributions.reshape(document_length, key_width),
        ],
        axis=1,
    ).astype(jnp.bfloat16)
    both_gradients = scatter_ctx(
        [both_gradients[j * count_of_rows : (j + 1) * count_of_rows] for j in range(pieces)]
    )
    key_gradients, grad_values = both_gradients[:, :key_width], both_gradients[:, key_width:]
    grad_query_raw = apply_rotation(
        grad_queries.reshape(count_of_rows, QUERY_HEADS, HEAD_SIZE), -token_position
    ) * HEAD_SIZE ** (-0.5)
    gradient_key_unrotated = apply_rotation(
        key_gradients.reshape(count_of_rows, KEY_VALUE_HEADS, HEAD_SIZE), -token_position
    )
    grad_mixer = (grad_gated * silu_z).reshape(count_of_rows, SH, SP)
    grad_z = (grad_gated * ssm_out * silu_slope(gate_z)).astype(jnp.bfloat16)
    owned_mid = scatter_weight(
        *[
            jnp.concatenate([weight_half(normed, grad_z, h), weight_half(grad_mix, middle, h)], axis=1)
            for h in (0, 1)
        ]
    )
    local_pull = jnp.einsum("th,thp,tn->hpn", carried, grad_mixer, input_c)
    state_grad = entering(carried[-1], local_pull, True)

    def whole_block(
        block_x, block_b, block_c, block_step, bias_step, log_decay, gain_skip, state_in
    ):
        own_block, end_block, carried_block = block_terms(
            block_x,
            block_b,
            block_c,
            block_step,
            segment_float,
            previous,
            bias_step,
            log_decay,
            gain_skip,
        )
        result = own_block + carried_block[:, :, None] * jnp.einsum(
            "tn,hpn->thp", block_c, state_in
        )
        return (result, end_block + carried_block[-1][:, None, None] * state_in)

    unused_out, pullback = jax.vjp(
        whole_block,
        inputs_x,
        input_b,
        input_c,
        step_raw,
        step_bias,
        decay_log,
        skip_gain,
        carry_state,
    )
    block_grads = pullback((grad_mixer, state_grad))
    grad_project = jnp.concatenate(
        [
            block_grads[0],
            block_grads[1],
            block_grads[2],
            grad_query_raw.reshape(count_of_rows, QUERY_HEADS * HEAD_SIZE),
            gradient_key_unrotated.reshape(count_of_rows, KEY_VALUE_HEADS * HEAD_SIZE),
            grad_values,
            block_grads[3],
        ],
        axis=1,
    ).astype(jnp.bfloat16)
    owned_mix = weight_grad(normed, grad_project)
    grad_normed = jnp.einsum(
        "tc,dc->td", grad_project, full_mix, preferred_element_type=jnp.float32
    ) + jnp.einsum("tc,dc->td", grad_z, full_z, preferred_element_type=jnp.float32)
    grad_norm_gain = jnp.sum(grad_normed * hidden * inv_first, axis=0)
    scaled_one = grad_normed * norm_gain
    grad_hidden = (
        grad_residual
        + inv_first * scaled_one
        - hidden
        * (inv_first * inv_first * inv_first)
        * jnp.mean(scaled_one * hidden, axis=-1, keepdims=True)
    )
    gain_grads = jnp.dot(
        jnp.stack([grad_norm_gain, grad_feed_gain]),
        turn.T.astype(jnp.float32),
        precision=lax.Precision.HIGHEST,
    )
    small = jnp.concatenate([block_grads[4], block_grads[5], block_grads[6]])
    packed = jnp.concatenate(
        [gain_grads.reshape(-1, NS), jnp.pad(small, (0, NS - 3 * SH))[None]], axis=0
    )
    packed = total_over_all(packed)
    total_gain = packed[:-1].reshape(2, width)
    total_norm, total_feed = total_gain[0], total_gain[1]
    total_bias, total_decay, total_skip = (packed[-1, i * SH : (i + 1) * SH] for i in range(3))
    mix_edge = mixer_width + 2 * NS
    owned_in = jnp.concatenate(
        [
            owned_mid[:, :mixer_width],
            owned_mix[:, :mix_edge],
            owned_mix[:, owned_mix.shape[1] - SH :],
            owned_mix[:, mix_edge : owned_mix.shape[1] - SH],
        ],
        axis=1,
    )
    owned_out = owned_mid[:, mixer_width:]
    layer_out, grad_hidden = (
        jnp.dot(v.astype(jnp.bfloat16), turn.T, preferred_element_type=jnp.float32).astype(
            jnp.bfloat16
        )
        for v in (layer_out, grad_hidden)
    )
    return (
        layer_out,
        grad_hidden,
        owned_in,
        owned_out.T,
        owned_gate_up,
        owned_down.T,
        total_norm,
        total_feed,
        total_bias,
        total_decay,
        total_skip,
    )


def solution(mesh):
    return jax.shard_map(
        local,
        mesh=mesh,
        in_specs=(
            P(("fsdp", "ctx"), None),
            P(("fsdp", "ctx")),
            P(("fsdp", "ctx"), None),
            P(("fsdp", "ctx"), None),
            P(None, ("fsdp", "ctx")),
            P(("fsdp", "ctx"), None),
            P(None, ("fsdp", "ctx")),
            P(),
            P(),
            P(),
            P(),
            P(),
        ),
        out_specs=(
            P(("fsdp", "ctx"), None),
            P(("fsdp", "ctx"), None),
            P(("fsdp", "ctx"), None),
            P(None, ("fsdp", "ctx")),
            P(("fsdp", "ctx"), None),
            P(None, ("fsdp", "ctx")),
            P(),
            P(),
            P(),
            P(),
            P(),
        ),
        check_vma=False,
    )
```

```python
import jax
import jax.numpy as jnp
from jax import lax
from jax.experimental import pallas as pl
from jax.experimental.pallas import tpu as pltpu
from jax.sharding import PartitionSpec as P

FF = 2048
SH = 24
SP = 64
NS = 128
QUERY_HEADS = 8
KEY_VALUE_HEADS = 2
HEAD_SIZE = 64
KEY_WIDTH = KEY_VALUE_HEADS * HEAD_SIZE
REPEAT = QUERY_HEADS // KEY_VALUE_HEADS


EPSILON = 1e-06
ROTARY_BASE = 100000000000.0


def swap(value, mask):
    size = lax.axis_size("fsdp")
    return lax.ppermute(value, "fsdp", [(i, i ^ mask) for i in range(size)])


def swap_ctx(value, mask):
    size = lax.axis_size("ctx")
    return lax.ppermute(value, "ctx", [(i, i ^ mask) for i in range(size)])


def after(value, *others):
    return lax.optimization_barrier((value, others))[0]


def chip_masks():
    bits = lax.axis_size("fsdp").bit_length() - 2
    masks = [2 << i for i in range(bits)]
    x_masks, y_masks = masks[: bits // 2], masks[bits // 2 :]
    return (y_masks + x_masks, x_masks + y_masks)


def gather_first(blocks):
    half = len(blocks) // 2
    return [jnp.concatenate(blocks[:half], axis=0), jnp.concatenate(blocks[half:], axis=0)]


def gather_inner(parts, *hold):
    out = []
    for part, masks in zip(parts, chip_masks()):
        for mask in masks[:-1]:
            part = jnp.concatenate([part, after(swap(part, mask), *hold)], axis=0)
        out.append(part)
    return out


def gather_last(parts):
    return [swap(part, masks[-1]) for part, masks in zip(parts, chip_masks())]


def gather_core(parts, others):
    pieces = []
    for own in zip(parts, others):
        pieces += list(own) + [swap(piece, 1) for piece in own]
    return pieces


def piece_rows(width):
    devices = lax.axis_size("fsdp")
    block = width // (2 * devices)
    runs = []
    for half, masks in enumerate(chip_masks()):
        for core in (0, 1):
            for last in (0, 1):
                piece = half * 4 + core * 2 + last
                for inner in range(devices // 4):
                    chip = last * masks[-1]
                    for i, mask in enumerate(masks[:-1]):
                        chip += ((inner >> i) & 1) * mask
                    start = core * (width // 2) + half * (width // 4) + (chip >> 1) * block
                    runs.append((piece, inner * block, start, block))
    return runs


def plus(left, right):
    return (left.astype(jnp.float32) + right.astype(jnp.float32)).astype(jnp.bfloat16)


def scatter_first(kept, arrived):
    quarter, columns = kept.shape[0] // 2, kept.shape[1]
    parts = []
    for h, masks in enumerate(chip_masks()):
        rows = slice(h * quarter, (h + 1) * quarter)
        shape = [2] * len(masks) + [-1, columns]
        parts.append(plus(kept[rows].reshape(shape), arrived[rows].reshape(shape)))
    return parts


def scatter_chip(parts, first, count, *hold):
    out = []
    for part, masks in zip(parts, chip_masks()):
        order = masks[::-1]
        left = sorted(order[first:], reverse=True)
        for mask in order[first : first + count]:
            axis = left.index(mask)
            left.remove(mask)
            here = lax.index_in_dim(part, 0, axis, keepdims=False)
            there = lax.index_in_dim(part, 1, axis, keepdims=False)
            part = plus(here, after(swap(there, mask), *hold))
        out.append(part)
    return out


def scatter_last(parts):
    pieces = lax.axis_size("ctx") // 2
    blocks = []
    for part in parts:
        rows = part.shape[0] // pieces
        blocks += [part[j * rows : (j + 1) * rows] for j in range(pieces)]
    return scatter_ctx(blocks)


NT = (((1,), (1,)), ((), ()))
TN = (((0,), (0,)), ((), ()))
VMEM_BYTES = 58 * 1024 * 1024


def cost():
    return pl.CostEstimate(flops=1, bytes_accessed=1, transcendentals=0)


def params():
    return pltpu.CompilerParams(vmem_limit_bytes=VMEM_BYTES)


def weight_kernel(edge, rows_one, rows_two, columns, out, turned):
    step = pl.program_id(0)

    @pl.when(step == 0)
    def _():
        turned[...] = rows_one[...].T

    @pl.when(step == edge)
    def _():
        turned[...] = rows_two[...].T

    out[...] = dot(turned[...], columns[...]).astype(jnp.bfloat16)


def weight_half(rows_one, rows_two, columns, edge, half, tile=512):
    tokens, width = rows_one.shape
    half_rows = pl.BlockSpec((tokens, width // 2), lambda j: (0, half))
    count = columns.shape[1]
    return pl.pallas_call(
        lambda *refs: weight_kernel(edge // tile, *refs),
        grid=(count // tile,),
        in_specs=[half_rows, half_rows, pl.BlockSpec((tokens, tile), lambda j: (0, j))],
        out_specs=pl.BlockSpec((width // 2, tile), lambda j: (0, j)),
        out_shape=jax.ShapeDtypeStruct((width // 2, count), jnp.bfloat16),
        scratch_shapes=[pltpu.VMEM((width // 2, tokens), jnp.bfloat16)],
        compiler_params=params(),
        name="weight_grad",
        cost_estimate=cost(),
    )(rows_one, rows_two, columns)


def fetch(pieces, whole, semaphore, runs, start, stop):
    for piece, source, target, count in runs:
        pltpu.make_async_copy(
            pieces[piece].at[pl.ds(source, count), start:stop],
            whole.at[pl.ds(target, count), start:stop],
            semaphore,
        ).start()


def fetched(whole, semaphore, start, stop):
    view = whole.at[:, start:stop]
    pltpu.make_async_copy(view, view, semaphore).wait()


def dot(left, right):
    return jnp.dot(left, right, preferred_element_type=jnp.float32)


def dot_nt(left, right):
    return lax.dot_general(left, right, NT, preferred_element_type=jnp.float32)


def tiles(total, tile, body):
    @pl.loop(0, total // tile)
    def _(i):
        body(pl.ds(pl.multiple_of(i * tile, tile), tile))


def project_kernel(runs, hidden, gain, turn_cos, turn_sin, segment_row, *refs):
    pieces, refs = refs[:8], refs[8:]
    normed, project, queries, packed, whole, semaphore = refs
    columns, tokens = whole.shape[1], hidden.shape[0]
    fetch(pieces, whole, semaphore, runs, 0, columns)
    h = hidden[...].astype(jnp.float32)
    inverse = lax.rsqrt(jnp.mean(h * h, axis=-1, keepdims=True) + EPSILON)
    normed[...] = (h * inverse * gain[...]).astype(jnp.bfloat16)
    fetched(whole, semaphore, 0, columns)

    def body(at):
        project[:, at] = dot(normed[...], whole[:, at])

    tiles(columns, 384, body)
    start = SH * SP + 2 * NS
    turned = project[:, start : start + QUERY_HEADS * HEAD_SIZE].T
    queries[...] = (rotate(turned, turn_cos, turn_sin) * HEAD_SIZE ** (-0.5)).astype(jnp.bfloat16)
    start = start + QUERY_HEADS * HEAD_SIZE
    keys = rotate(project[:, start : start + KEY_WIDTH].T, turn_cos, turn_sin)
    packed[:tokens, :KEY_WIDTH] = keys.T.astype(jnp.bfloat16)
    start = start + KEY_WIDTH
    packed[:tokens, KEY_WIDTH:] = project[:, start : start + KEY_WIDTH].astype(jnp.bfloat16)
    packed[tokens:, :] = jnp.broadcast_to(segment_row[...], (16, 2 * KEY_WIDTH)).astype(jnp.bfloat16)


def rotate(turned, turn_cos, turn_sin, sign=1.0):
    half = HEAD_SIZE // 2
    c, s = turn_cos[...], turn_sin[...] * sign
    out = []
    for start in range(0, turned.shape[0], HEAD_SIZE):
        first, second = turned[start : start + half], turned[start + half : start + HEAD_SIZE]
        out += [first * c - second * s, second * c + first * s]
    return jnp.concatenate(out, axis=0)


def full_specs(count):
    return [pl.BlockSpec(memory_space=pltpu.VMEM)] * count


def any_specs(count):
    return [pl.BlockSpec(memory_space=pl.ANY)] * count


def project_in(hidden, gain, turn_cos, turn_sin, segment_row, pieces):
    tokens, width = hidden.shape
    columns = pieces[0].shape[1]
    runs = piece_rows(width)
    return pl.pallas_call(
        lambda *refs: project_kernel(runs, *refs),
        in_specs=full_specs(5) + any_specs(8),
        out_specs=full_specs(4),
        out_shape=[
            jax.ShapeDtypeStruct((tokens, width), jnp.bfloat16),
            jax.ShapeDtypeStruct((tokens, columns), jnp.float32),
            jax.ShapeDtypeStruct((QUERY_HEADS * HEAD_SIZE, tokens), jnp.bfloat16),
            jax.ShapeDtypeStruct((tokens + 16, 2 * KEY_WIDTH), jnp.bfloat16),
        ],
        scratch_shapes=[pltpu.VMEM((width, columns), jnp.bfloat16), pltpu.SemaphoreType.DMA],
        compiler_params=params(),
        name="project_in",
        cost_estimate=cost(),
    )(hidden, gain[None], turn_cos, turn_sin, segment_row, *pieces)


def spread_heads():
    head = lax.broadcasted_iota(jnp.int32, (NS, SH * SP), 1) // SP
    return (lax.broadcasted_iota(jnp.int32, (NS, SH * SP), 0) == head).astype(jnp.float32)


def dot_exact(left, right):
    return jnp.dot(
        left, right, precision=lax.Precision.HIGHEST, preferred_element_type=jnp.float32
    )


def step_terms(project, bias, decay):
    tokens = project.shape[0]
    raw = project[:, project.shape[1] - NS :] + bias[...]
    step = jnp.maximum(raw, 0.0) + jnp.log1p(jnp.exp(-jnp.abs(raw)))
    rate = -jnp.exp(decay[...]) * step
    rows = lax.broadcasted_iota(jnp.int32, (tokens, tokens), 0)
    columns = lax.broadcasted_iota(jnp.int32, (tokens, tokens), 1)
    running = dot_exact((rows >= columns).astype(jnp.float32), rate)
    return raw, step, rate, running


def tail_terms(running, segment_column):
    tokens = running.shape[0]
    same = segment_column[...] == segment_column[tokens - 1 :, :]
    return jnp.where(same, jnp.exp(running[tokens - 1 :, :] - running), 0.0)


def split_low(values):
    high = values.astype(jnp.bfloat16)
    return high, (values - high.astype(jnp.float32)).astype(jnp.bfloat16)


def twice(values):
    return jnp.concatenate([values, values], axis=0)


def column_of(values, head):
    lane = lax.broadcasted_iota(jnp.int32, values.shape, 1)
    return jnp.sum(jnp.where(lane == head, values, 0.0), axis=1, keepdims=True)


def state_kernel(project, bias, decay, skip, spread, column, row, own, packed, running_out, bias_sum, turned):
    tokens, inner = own.shape
    _, step, _, running = step_terms(project, bias, decay)
    running_out[...] = running
    tail = tail_terms(running, column) * step
    tail = dot_exact(tail, spread[...])
    values = project[:, :inner]
    states = dot(project[:, inner : inner + NS].T.astype(jnp.bfloat16), (tail * values).astype(jnp.bfloat16))
    packed[:NS, :] = states.astype(jnp.bfloat16)
    last = dot_exact(jnp.broadcast_to(jnp.exp(running[tokens - 1 :, :]), (8, NS)), spread[...])
    packed[NS:, :] = jnp.concatenate([last, last], axis=0).astype(jnp.bfloat16)
    at_row = lax.broadcasted_iota(jnp.int32, (tokens, tokens), 0)
    at_column = lax.broadcasted_iota(jnp.int32, (tokens, tokens), 1)
    allowed = (at_row >= at_column) & (column[...] == row[...])
    turned[0] = running.T
    turned[1] = step.T
    bias_sum[...] = jnp.where(allowed, 0.0, -1e30)
    match = lax.dot_general(
        project[:, inner + NS : inner + 2 * NS],
        project[:, inner : inner + NS],
        NT,
        precision=lax.Precision.HIGHEST,
        preferred_element_type=jnp.float32,
    )
    lane = lax.broadcasted_iota(jnp.int32, (tokens, NS), 1)

    @pl.loop(0, SH // 2)
    def _(pair):
        at = pl.ds(pl.multiple_of(pair * NS, NS), NS)
        values = project[:, at]
        parts = []
        for k in (0, 1):
            head = 2 * pair + k
            gap = column_of(running_out[...], head) - turned[0, pl.ds(head, 1), :]
            weight = jnp.exp(jnp.minimum(gap, 0.0) + bias_sum[...])
            weight = weight * match * turned[1, pl.ds(head, 1), :]
            parts.append(dot(weight.astype(jnp.bfloat16), values.astype(jnp.bfloat16)))
        own[:, at] = jnp.where(lane < SP, parts[0], parts[1]) + skip[:, at] * values


def state_forward(project, bias, decay, skip, spread, column, row):
    tokens, inner = project.shape[0], SH * SP
    return pl.pallas_call(
        state_kernel,
        in_specs=full_specs(7),
        out_specs=full_specs(3),
        out_shape=[
            jax.ShapeDtypeStruct((tokens, inner), jnp.float32),
            jax.ShapeDtypeStruct((NS + 16, inner), jnp.bfloat16),
            jax.ShapeDtypeStruct((tokens, NS), jnp.float32),
        ],
        scratch_shapes=[
            pltpu.VMEM((tokens, tokens), jnp.float32),
            pltpu.VMEM((2, NS, tokens), jnp.float32),
        ],
        compiler_params=params(),
        name="state_forward",
        cost_estimate=cost(),
    )(project, bias, decay, skip, spread, column, row)


def key_masks(place, row, blocks, masks):
    tokens = row.shape[1]
    key = lax.broadcasted_iota(jnp.int32, (tokens, tokens), 0)
    query = lax.broadcasted_iota(jnp.int32, (tokens, tokens), 1)
    for j, block in enumerate(blocks):
        label = block[tokens : tokens + 16, :tokens].astype(jnp.float32).T[:, :1]
        ahead = ((place[0] ^ j) - place[0]) * tokens
        allowed = (key + ahead <= query) & (label == row[...])
        masks[j] = jnp.where(allowed, 0.0, -1e30)


def attend_kernel(count, place, queries, row, *refs):
    blocks, (attended, total, masks, scores, turned, values) = refs[:count], refs[count:]
    tokens = row.shape[1]
    key_masks(place, row, blocks, masks)
    for j, block in enumerate(blocks):
        values[j] = block[:tokens, KEY_WIDTH:].T
    for group in range(KEY_VALUE_HEADS):
        lanes = slice(group * HEAD_SIZE, (group + 1) * HEAD_SIZE)

        @pl.loop(0, REPEAT)
        def _(r):
            head = group * REPEAT + r
            at = pl.ds(pl.multiple_of(head * HEAD_SIZE, HEAD_SIZE), HEAD_SIZE)
            highest = None
            for j, block in enumerate(blocks):
                score = dot(block[:tokens, lanes], queries[at, :]) + masks[j]
                scores[j] = score
                top = jnp.max(score, axis=0, keepdims=True)
                highest = top if highest is None else jnp.maximum(highest, top)
            sums = 0.0
            for j in range(count):
                score = jnp.exp(scores[j] - highest)
                scores[j] = score
                sums = sums + jnp.sum(score, axis=0, keepdims=True)
            inverse = 1.0 / sums
            result = 0.0
            for j in range(count):
                result = result + dot(values[j, lanes, :], (scores[j] * inverse).astype(jnp.bfloat16))
            turned[at, :] = result
            total[pl.ds(head, 1), :] = highest + jnp.log(sums)

    attended[...] = turned[...].T.astype(jnp.bfloat16)


def attend(place, queries, row, blocks):
    tokens, count = row.shape[1], len(blocks)
    return pl.pallas_call(
        lambda *refs: attend_kernel(count, *refs),
        in_specs=[pl.BlockSpec(memory_space=pltpu.SMEM)] + full_specs(2 + count),
        out_specs=full_specs(2),
        out_shape=[
            jax.ShapeDtypeStruct((tokens, QUERY_HEADS * HEAD_SIZE), jnp.bfloat16),
            jax.ShapeDtypeStruct((QUERY_HEADS, tokens), jnp.float32),
        ],
        scratch_shapes=[
            pltpu.VMEM((count, tokens, tokens), jnp.float32),
            pltpu.VMEM((count, tokens, tokens), jnp.float32),
            pltpu.VMEM((QUERY_HEADS * HEAD_SIZE, tokens), jnp.float32),
            pltpu.VMEM((count, KEY_WIDTH, tokens), jnp.bfloat16),
        ],
        compiler_params=params(),
        name="attend",
        cost_estimate=cost(),
    )(place, queries, row, *blocks)


def attend_back_kernel(count, place, queries, row, grad_att, total, turn_cos, turn_sin, *refs):
    blocks, refs = refs[:count], refs[count:]
    grad_query, grad_blocks, refs = refs[0], refs[1 : 1 + count], refs[1 + count :]
    masks, chances, slopes, turned_keys, turned_grad, grad_turned, key_sums, value_sums = refs
    tokens = row.shape[1]
    key_masks(place, row, blocks, masks)
    turned_grad[...] = grad_att[...].T
    for j, block in enumerate(blocks):
        turned_keys[j] = block[:tokens, :KEY_WIDTH].T
    for group in range(KEY_VALUE_HEADS):
        lanes = slice(group * HEAD_SIZE, (group + 1) * HEAD_SIZE)
        ahead = slice(KEY_WIDTH + group * HEAD_SIZE, KEY_WIDTH + (group + 1) * HEAD_SIZE)
        key_sums[...] = jnp.zeros_like(key_sums)
        value_sums[...] = jnp.zeros_like(value_sums)

        @pl.loop(0, REPEAT)
        def _(r):
            head = group * REPEAT + r
            at = pl.ds(pl.multiple_of(head * HEAD_SIZE, HEAD_SIZE), HEAD_SIZE)
            query, grad = queries[at, :], turned_grad[at, :]
            query_rows, grad_rows = query.T, grad.T
            inside = 0.0
            for j, block in enumerate(blocks):
                score = dot(block[:tokens, lanes], query) + masks[j]
                chance = jnp.exp(score - total[pl.ds(head, 1), :])
                slope = dot(block[:tokens, ahead], grad)
                chances[j], slopes[j] = chance, slope
                inside = inside + jnp.sum(chance * slope, axis=0, keepdims=True)
                value_sums[j] = value_sums[j] + dot(chance.astype(jnp.bfloat16), grad_rows)
            result = 0.0
            for j in range(count):
                slope = (chances[j] * (slopes[j] - inside)).astype(jnp.bfloat16)
                key_sums[j] = key_sums[j] + dot(slope, query_rows)
                result = result + dot(turned_keys[j, lanes, :], slope)
            grad_turned[at, :] = result

        for j in range(count):
            grad_blocks[j][:, lanes] = key_sums[j].astype(jnp.bfloat16)
            grad_blocks[j][:, ahead] = value_sums[j].astype(jnp.bfloat16)
    turned = rotate(grad_turned[...], turn_cos, turn_sin, -1.0) * HEAD_SIZE ** (-0.5)
    grad_query[...] = turned.T.astype(jnp.bfloat16)


def attend_back(place, queries, row, grad_att, total, turn_cos, turn_sin, blocks):
    tokens, count = row.shape[1], len(blocks)
    square = pltpu.VMEM((count, tokens, tokens), jnp.float32)
    heads = QUERY_HEADS * HEAD_SIZE
    return pl.pallas_call(
        lambda *refs: attend_back_kernel(count, *refs),
        in_specs=[pl.BlockSpec(memory_space=pltpu.SMEM)] + full_specs(6 + count),
        out_specs=full_specs(1 + count),
        out_shape=[jax.ShapeDtypeStruct((tokens, heads), jnp.bfloat16)]
        + [jax.ShapeDtypeStruct((tokens, 2 * KEY_WIDTH), jnp.bfloat16)] * count,
        scratch_shapes=[
            square,
            square,
            square,
            pltpu.VMEM((count, KEY_WIDTH, tokens), jnp.bfloat16),
            pltpu.VMEM((heads, tokens), jnp.bfloat16),
            pltpu.VMEM((heads, tokens), jnp.float32),
            pltpu.VMEM((count, tokens, HEAD_SIZE), jnp.float32),
            pltpu.VMEM((count, tokens, HEAD_SIZE), jnp.float32),
        ],
        compiler_params=params(),
        name="attend_back",
        cost_estimate=cost(),
    )(place, queries, row, grad_att, total, turn_cos, turn_sin, *blocks)


def state_back_kernel(
    project, bias, decay, skip, spread, column, row, grad_y, carried, entered, grad_state,
    grad_query, grad_keys, turn_cos, turn_sin,
    grad_project, small, bias_sum, turned, match_grad, column_sums, row_sums, running_keep, step_keep,
):
    tokens, inner = grad_y.shape
    raw, step, rate, running = step_terms(project, bias, decay)
    running_keep[...], step_keep[...] = running, step
    decayed = tail_terms(running, column)
    tail = decayed * step
    turned[...] = running.T
    values_b = project[:, inner : inner + NS]
    values_c = project[:, inner + NS : inner + 2 * NS]
    low_b, low_c = values_b.astype(jnp.bfloat16), values_c.astype(jnp.bfloat16)
    both_b = jnp.concatenate(split_low(values_b), axis=1)
    both_c = jnp.concatenate(split_low(values_c), axis=1)
    key = lax.broadcasted_iota(jnp.int32, (tokens, tokens), 0)
    query = lax.broadcasted_iota(jnp.int32, (tokens, tokens), 1)
    bias_sum[...] = jnp.where((query >= key) & (column[...] == row[...]), 0.0, -1e30)
    match = lax.dot_general(
        values_b, values_c, NT, precision=lax.Precision.HIGHEST, preferred_element_type=jnp.float32
    )
    match_grad[...] = jnp.zeros_like(match_grad)
    column_sums[...] = jnp.zeros_like(column_sums)
    row_sums[...] = jnp.zeros_like(row_sums)
    lane = lax.broadcasted_iota(jnp.int32, (tokens, NS), 1)

    @pl.loop(0, SH // 2)
    def _(pair):
        at = pl.ds(pl.multiple_of(pair * NS, NS), NS)
        low, rest = split_low(project[:, at])
        low_grad, rest_grad = split_low(grad_y[:, at])
        turned_grad, turned_rest = low_grad.T, rest_grad.T
        parts = []
        for k in (0, 1):
            head = 2 * pair + k
            rows = slice(k * SP, (k + 1) * SP)
            gap = turned[pl.ds(head, 1), :] - column_of(running_keep[...], head)
            weight = jnp.exp(jnp.minimum(gap, 0.0) + bias_sum[...])
            step_column = column_of(step_keep[...], head)
            slope = dot(
                jnp.concatenate([low[:, rows], rest[:, rows], low[:, rows]], axis=1),
                jnp.concatenate([turned_grad[rows], turned_grad[rows], turned_rest[rows]], axis=0),
            )
            slope = slope * weight
            scaled = slope * step_column
            match_grad[...] = match_grad[...] + scaled
            row_sums[pl.ds(head, 1), :] = jnp.sum(scaled * match, axis=0, keepdims=True)
            sums = jnp.sum(slope * match, axis=1, keepdims=True)
            column_sums[...] = column_sums[...] + jnp.where(lane == head, sums, 0.0)
            weight = weight * match * step_column
            parts.append(dot(weight.astype(jnp.bfloat16), low_grad))
        grad_x = jnp.where(lane < SP, parts[0], parts[1]) + skip[:, at] * grad_y[:, at]
        tail_wide = dot_exact(tail, spread[:, at])
        grad_x = grad_x + tail_wide * dot(low_b, grad_state[:, at])
        grad_project[:, at] = grad_x.astype(jnp.bfloat16)

    x, grad = project[:, :inner], grad_y[...]
    carried_wide = dot_exact(carried[...], spread[...])
    tail_wide = dot_exact(tail, spread[...])
    out_b = dot_nt((tail_wide * x).astype(jnp.bfloat16), grad_state[...])
    out_c = dot_nt((carried_wide * grad).astype(jnp.bfloat16), entered[...])
    low_match = match_grad[...].astype(jnp.bfloat16)
    out_b = out_b + dot(low_match, low_c)
    out_c = out_c + dot(match_grad[...].T.astype(jnp.bfloat16), low_b)
    grad_project[:, inner : inner + NS] = out_b.astype(jnp.bfloat16)
    grad_project[:, inner + NS : inner + 2 * NS] = out_c.astype(jnp.bfloat16)

    def per_head(wide):
        return lax.dot_general(
            wide, spread[...], NT, precision=lax.Precision.HIGHEST, preferred_element_type=jnp.float32
        )

    grad_tail = per_head(x * dot(both_b, twice(grad_state[...])))
    grad_carried = per_head(grad * dot(both_c, twice(entered[...])))
    kept = jnp.sum(grad_state[...].astype(jnp.float32) * entered[...].astype(jnp.float32), axis=0, keepdims=True)
    kept = per_head(jnp.broadcast_to(kept, (8, inner)))[:1]
    at_token = lax.broadcasted_iota(jnp.int32, (tokens, NS), 0)
    grad_carried = grad_carried + jnp.where(at_token == tokens - 1, kept, 0.0)
    grad_step = column_sums[...] + grad_tail * decayed
    through = grad_tail * tail
    grad_running = row_sums[...].T - step * column_sums[...] + grad_carried * carried[...] - through
    through = jnp.sum(through, axis=0, keepdims=True)
    grad_running = grad_running + jnp.where(at_token == tokens - 1, through, 0.0)
    grad_rate = dot_exact((query >= key).astype(jnp.float32), grad_running)
    grad_step = grad_step - grad_rate * jnp.exp(decay[...])
    grad_raw = grad_step * jax.nn.sigmoid(raw)
    grad_raw = jnp.where(lane < SH, grad_raw, 0.0)
    grad_skip = per_head(jnp.broadcast_to(jnp.sum(grad * x, axis=0, keepdims=True), (8, inner)))[:1]
    small[0:1, :] = jnp.sum(grad_raw, axis=0, keepdims=True)
    small[1:2, :] = jnp.sum(grad_rate * rate, axis=0, keepdims=True)
    small[2:3, :] = grad_skip
    small[3:, :] = jnp.zeros((5, NS), jnp.float32)
    start = inner + 2 * NS
    heads = QUERY_HEADS * HEAD_SIZE
    grad_project[:, start : start + heads] = grad_query[...]
    start = start + heads
    turned_key = rotate(grad_keys[:, :KEY_WIDTH].T, turn_cos, turn_sin, -1.0)
    grad_project[:, start : start + KEY_WIDTH] = turned_key.T.astype(jnp.bfloat16)
    start = start + KEY_WIDTH
    grad_project[:, start : start + KEY_WIDTH] = grad_keys[:, KEY_WIDTH:].astype(jnp.bfloat16)
    grad_project[:, start + KEY_WIDTH :] = grad_raw.astype(jnp.bfloat16)


def state_back(project, *others):
    tokens, inner = project.shape[0], SH * SP
    square = pltpu.VMEM((tokens, tokens), jnp.float32)
    narrow = pltpu.VMEM((tokens, NS), jnp.float32)
    return pl.pallas_call(
        state_back_kernel,
        in_specs=full_specs(1 + len(others)),
        out_specs=full_specs(2),
        out_shape=[
            jax.ShapeDtypeStruct(project.shape, jnp.bfloat16),
            jax.ShapeDtypeStruct((8, NS), jnp.float32),
        ],
        scratch_shapes=[
            square,
            pltpu.VMEM((NS, tokens), jnp.float32),
            square,
            narrow,
            pltpu.VMEM((NS, tokens), jnp.float32),
            narrow,
            narrow,
        ],
        compiler_params=params(),
        name="state_back",
        cost_estimate=cost(),
    )(project, *others)


def entering(packed, same, reverse):
    size = lax.axis_size("ctx")
    total, decay = 0.0, 1.0
    for shift in range(1, size):
        pairs = [(i, i + shift) for i in range(size - shift)]
        if reverse:
            pairs = [(j, i) for i, j in pairs]
        part = lax.ppermute(packed, "ctx", pairs).astype(jnp.float32)
        total = total + decay * part[:NS]
        decay = decay * jnp.where(same[shift], part[NS : NS + 1], 0.0)
    return total.astype(jnp.bfloat16)


def project_back_kernel(runs, hidden, gain, grad_project, partial, grad_residual, *refs):
    pieces, (grad_hidden, gain_grad, whole, grad_normed, semaphore) = refs[:8], refs[8:]
    columns = whole.shape[1]
    fetch(pieces, whole, semaphore, runs, 0, columns)
    h = hidden[...].astype(jnp.float32)
    inverse = lax.rsqrt(jnp.mean(h * h, axis=-1, keepdims=True) + EPSILON)
    fetched(whole, semaphore, 0, columns)

    def body(at):
        grad_normed[:, at] = partial[:, at] + dot_nt(grad_project[...], whole[at, :])

    tiles(whole.shape[0], 256, body)
    grad = grad_normed[...]
    gain_grad[...] = jnp.sum(grad * h * inverse, axis=0, keepdims=True)
    scaled = grad * gain[...]
    mean = jnp.mean(scaled * h, axis=-1, keepdims=True)
    grad_hidden[...] = (
        grad_residual[...] + inverse * scaled - h * (inverse * inverse * inverse) * mean
    ).astype(jnp.bfloat16)


def project_back(hidden, gain, grad_project, partial, grad_residual, pieces):
    tokens, width = hidden.shape
    columns = pieces[0].shape[1]
    runs = piece_rows(width)
    return pl.pallas_call(
        lambda *refs: project_back_kernel(runs, *refs),
        in_specs=full_specs(5) + any_specs(8),
        out_specs=full_specs(2),
        out_shape=[
            jax.ShapeDtypeStruct((tokens, width), jnp.bfloat16),
            jax.ShapeDtypeStruct((1, width), jnp.float32),
        ],
        scratch_shapes=[
            pltpu.VMEM((width, columns), jnp.bfloat16),
            pltpu.VMEM((tokens, width), jnp.float32),
            pltpu.SemaphoreType.DMA,
        ],
        compiler_params=params(),
        name="project_back",
        cost_estimate=cost(),
    )(hidden, gain[None], grad_project, partial, grad_residual, *pieces)


def middle_kernel(
    runs, hidden, normed, cotangent, own, reads, entered, carried, spread, attended, gain, *refs
):
    mid_pieces, feed_pieces, refs = refs[:8], refs[8:16], refs[16:]
    layer_out, normed_two, feed_columns, grad_mix, mid_columns = refs[:5]
    grad_residual, grad_y, grad_att, grad_normed, gain_grad, pulled = refs[5:11]
    mid, feed, gate_z, ssm_out, gate, up, residual, grad_two, semaphores = refs[11:]
    width, inner = hidden.shape[1], own.shape[1]
    low_reads = jnp.concatenate(split_low(reads[...]), axis=1)
    turned_reads = reads[...].T.astype(jnp.bfloat16)
    mixed = mid.shape[1] - inner
    hidden_units = feed.shape[1] // 3
    tile, rows = 512, 256
    fetch(mid_pieces, mid, semaphores.at[0], runs, 0, inner)
    fetch(mid_pieces, mid, semaphores.at[1], runs, inner, inner + mixed)
    fetch(feed_pieces, feed, semaphores.at[2], runs, 0, 2 * hidden_units)
    fetch(feed_pieces, feed, semaphores.at[3], runs, 2 * hidden_units, 3 * hidden_units)

    def shift(at, by):
        return pl.ds(pl.multiple_of(at.start + by, 128), at.size)

    fetched(mid, semaphores.at[0], 0, inner)

    def gating(at):
        z = dot(normed[...], mid[:, at])
        gate_z[:, at] = z
        wide = dot_exact(carried[...], spread[:, at])
        y = own[:, at] + wide * dot(low_reads, twice(entered[:, at]))
        ssm_out[:, at] = y
        gated = y * (z * jax.nn.sigmoid(z))
        mid_columns[:, shift(at, inner)] = gated.astype(jnp.bfloat16)

    tiles(inner, tile, gating)
    mid_columns[:, 2 * inner :] = attended[...]
    fetched(mid, semaphores.at[1], inner, inner + mixed)

    def mixing(at):
        residual[:, at] = hidden[:, at].astype(jnp.float32) + dot_nt(
            mid_columns[:, inner:], mid[at, inner:]
        )

    tiles(width, rows, mixing)
    value = residual[...]
    inverse = lax.rsqrt(jnp.mean(value * value, axis=-1, keepdims=True) + EPSILON)
    normed_two[...] = (value * inverse * gain[...]).astype(jnp.bfloat16)
    fetched(feed, semaphores.at[2], 0, 2 * hidden_units)

    def opening(at):
        g = dot(normed_two[...], feed[:, at])
        u = dot(normed_two[...], feed[:, shift(at, hidden_units)])
        gate[:, at] = g
        up[:, at] = u
        active = (g * jax.nn.sigmoid(g)) * u
        feed_columns[:, shift(at, 2 * hidden_units)] = active.astype(jnp.bfloat16)

    tiles(hidden_units, tile, opening)
    fetched(feed, semaphores.at[3], 2 * hidden_units, 3 * hidden_units)

    def closing(at):
        layer_out[:, at] = (
            residual[:, at] + dot_nt(feed_columns[:, 2 * hidden_units :], feed[at, 2 * hidden_units :])
        ).astype(jnp.bfloat16)

    tiles(width, rows, closing)

    def activation(at):
        grad_active = dot(cotangent[...], feed[:, shift(at, 2 * hidden_units)])
        g, u = gate[:, at], up[:, at]
        s = jax.nn.sigmoid(g)
        feed_columns[:, at] = (grad_active * u * (s * (1.0 + g * (1.0 - s)))).astype(jnp.bfloat16)
        feed_columns[:, shift(at, hidden_units)] = (grad_active * (g * s)).astype(jnp.bfloat16)

    tiles(hidden_units, tile, activation)

    def opening_back(at):
        grad_two[:, at] = dot_nt(
            feed_columns[:, : 2 * hidden_units], feed[at, : 2 * hidden_units]
        )

    tiles(width, rows, opening_back)
    value = residual[...]
    grad = grad_two[...]
    gain_grad[...] = jnp.sum(grad * value * inverse, axis=0, keepdims=True)
    scaled = grad * gain[...]
    mean = jnp.mean(scaled * value, axis=-1, keepdims=True)
    grad = (
        cotangent[...].astype(jnp.float32)
        + inverse * scaled
        - value * (inverse * inverse * inverse) * mean
    )
    grad_residual[...] = grad
    grad_mix[...] = grad.astype(jnp.bfloat16)

    def gating_back(at):
        grad_gated = dot(grad_mix[...], mid[:, shift(at, inner)])
        z = gate_z[:, at]
        s = jax.nn.sigmoid(z)
        grad = grad_gated * (z * s)
        grad_y[:, at] = grad
        wide = dot_exact(carried[...], spread[:, at])
        pulled[:NS, at] = dot(turned_reads, (wide * grad).astype(jnp.bfloat16)).astype(jnp.bfloat16)
        grad_z = grad_gated * ssm_out[:, at] * (s * (1.0 + z * (1.0 - s)))
        mid_columns[:, at] = grad_z.astype(jnp.bfloat16)

    tiles(inner, tile, gating_back)
    grad_att[...] = dot(grad_mix[...], mid[:, 2 * inner :]).astype(jnp.bfloat16)

    def normed_back(at):
        grad_normed[:, at] = dot_nt(mid_columns[:, :inner], mid[at, :inner])

    tiles(width, rows, normed_back)
    tokens = hidden.shape[0]
    last = jnp.broadcast_to(carried[tokens - 1 :, :], (8, NS))
    last = dot_exact(last, spread[...])
    pulled[NS:, :] = jnp.concatenate([last, last], axis=0).astype(jnp.bfloat16)


def middle(
    hidden, normed, cotangent, own, reads, entered, carried, spread, attended, gain, mid_pieces, feed_pieces
):
    tokens, width = hidden.shape
    inner, heads = own.shape[1], attended.shape[1]
    mid, feed = mid_pieces[0].shape[1], feed_pieces[0].shape[1]
    runs = piece_rows(width)
    low = lambda n: jax.ShapeDtypeStruct((tokens, n), jnp.bfloat16)
    high = lambda n: jax.ShapeDtypeStruct((tokens, n), jnp.float32)
    return pl.pallas_call(
        lambda *refs: middle_kernel(runs, *refs),
        in_specs=full_specs(10) + any_specs(16),
        out_specs=full_specs(11),
        out_shape=[
            low(width),
            low(width),
            low(feed),
            low(width),
            low(mid),
            high(width),
            high(inner),
            low(heads),
            high(width),
            jax.ShapeDtypeStruct((1, width), jnp.float32),
            jax.ShapeDtypeStruct((NS + 16, inner), jnp.bfloat16),
        ],
        scratch_shapes=[
            pltpu.VMEM((width, mid), jnp.bfloat16),
            pltpu.VMEM((width, feed), jnp.bfloat16),
            pltpu.VMEM((tokens, inner), jnp.float32),
            pltpu.VMEM((tokens, inner), jnp.float32),
            pltpu.VMEM((tokens, feed // 3), jnp.float32),
            pltpu.VMEM((tokens, feed // 3), jnp.float32),
            pltpu.VMEM((tokens, width), jnp.float32),
            pltpu.VMEM((tokens, width), jnp.float32),
            pltpu.SemaphoreType.DMA((4,)),
        ],
        compiler_params=params(),
        name="middle",
        cost_estimate=cost(),
    )(
        hidden, normed, cotangent, own, reads, entered, carried, spread, attended, gain[None],
        *mid_pieces, *feed_pieces
    )


def width_order(width):
    devices, pieces = lax.axis_size("fsdp"), lax.axis_size("ctx")
    rows = width // (devices * pieces)
    block = rows * pieces // 2
    place = jnp.arange(width)
    core, half = place // (width // 2), (place // (width // 4)) % 2
    inner = place % (width // 4)
    device = lax.axis_index("fsdp") ^ (2 * (inner // block) + core)
    along = lax.axis_index("ctx") ^ ((inner % block) // rows + half * (pieces // 2))
    return (device * pieces + along) * rows + inner % rows


def gather_ctx(value, *hold):
    size = lax.axis_size("ctx")
    blocks = [value]
    if size == 4:
        one, two = swap_ctx(value, 1), swap_ctx(value, 2)
        return [value, one, two, swap_ctx(after(two, *hold), 1)]
    mask = 1
    while mask < size:
        blocks = blocks + [swap_ctx(block, mask) for block in blocks]
        mask *= 2
    return blocks


def scatter_ctx(blocks):
    size = lax.axis_size("ctx")
    if size == 4:
        two = plus(blocks[2], swap_ctx(blocks[3], 1))
        one = swap_ctx(blocks[1], 1)
        total = blocks[0].astype(jnp.float32) + one.astype(jnp.float32)
        return total + swap_ctx(two, 2).astype(jnp.float32)
    while size > 1:
        size //= 2
        blocks = [plus(blocks[j], swap_ctx(blocks[j + size], size)) for j in range(size)]
    return blocks[0].astype(jnp.float32)


def total_steps():
    return [
        (axis, 1 << i)
        for axis in ("fsdp", "ctx")
        for i in range(lax.axis_size(axis).bit_length() - 1)
    ]


def total_step(value, axis, mask):
    pairs = [(i, i ^ mask) for i in range(lax.axis_size(axis))]
    return value + lax.ppermute(value, axis, pairs)


def local(
    hidden_in,
    segments,
    cotangent,
    mixer_in,
    mixer_out,
    gate_up,
    down_weight,
    norm_gain,
    feed_gain,
    step_bias,
    decay_log,
    skip_gain,
):
    mixer_width = SH * SP
    width = hidden_in.shape[1]
    edges = [mixer_width, 2 * mixer_width, 2 * mixer_width + 2 * NS]
    edges += [edges[-1] + SH, mixer_in.shape[1]]
    in_z = mixer_in[:, : edges[0]]
    in_mix = jnp.concatenate(
        [
            mixer_in[:, edges[0] : edges[2]],
            mixer_in[:, edges[3] : edges[4]],
            mixer_in[:, edges[2] : edges[3]],
        ],
        axis=1,
    )
    in_mix = jnp.pad(in_mix, ((0, 0), (0, -in_mix.shape[1] % NS)))
    in_mid = jnp.concatenate([in_z, mixer_out.T], axis=1)
    in_feed = jnp.concatenate([gate_up, down_weight.T], axis=1)
    mix_blocks = gather_ctx(in_mix)
    mix_parts = gather_inner(gather_first(mix_blocks))
    mix_others = gather_last(mix_parts)
    mid_blocks = gather_ctx(after(in_mid, mix_blocks[-1]), mix_parts)
    mid_first = gather_first(after(mid_blocks, mix_others))
    mix_pieces = gather_core(mix_parts, mix_others)
    order = width_order(width)
    turn = (jnp.arange(width)[:, None] == order[None, :]).astype(jnp.bfloat16)
    hidden_in, cotangent = (
        jnp.dot(v, turn, preferred_element_type=jnp.float32).astype(jnp.bfloat16)
        for v in (hidden_in, cotangent)
    )
    gains = jnp.dot(
        jnp.stack([norm_gain, feed_gain]),
        turn.astype(jnp.float32),
        precision=lax.Precision.HIGHEST,
    )
    norm_gain, feed_gain = gains[0], gains[1]
    tokens = hidden_in.shape[0]
    piece = lax.axis_index("ctx")
    frequency = ROTARY_BASE ** (jnp.arange(HEAD_SIZE // 2, dtype=jnp.float32) * (-2.0 / HEAD_SIZE))
    token_position = (piece * tokens + jnp.arange(tokens)).astype(jnp.float32)
    angles = frequency[:, None] * token_position[None, :]
    turn_cos, turn_sin = jnp.cos(angles), jnp.sin(angles)
    segment_float = segments.astype(jnp.float32)
    row, column = segment_float[None, :], segment_float[:, None]
    place = piece.astype(jnp.int32)[None]
    spread = spread_heads()
    bias, decay = (jnp.pad(v, (0, NS - SH))[None] for v in (step_bias, decay_log))
    skip = jnp.repeat(skip_gain, SP)[None]
    normed, project, queries, packed = project_in(
        after(hidden_in, mid_first),
        norm_gain,
        turn_cos,
        turn_sin,
        jnp.pad(row, ((0, 0), (0, 2 * KEY_WIDTH - tokens))),
        mix_pieces,
    )
    mid_parts = gather_inner(mid_first, project)
    mid_others = gather_last(mid_parts)
    feed_blocks = gather_ctx(after(in_feed, mid_first), project)
    blocks = gather_ctx(packed)
    own, states, running = state_forward(
        after(project, mid_parts), bias, decay, skip, spread, column, row
    )
    feed_first = gather_first(after(feed_blocks, own))
    pieces = lax.axis_size("ctx")
    ends = jnp.stack([block[tokens, tokens - 1] for block in blocks]).astype(jnp.float32)
    block_of = piece ^ jnp.arange(pieces)

    def end_of(number):
        return jnp.sum(jnp.where(block_of == number, ends, 0.0))

    same = [None] + [
        (piece - k > 0) & (end_of(piece - k) == end_of(piece - k - 1)) for k in range(1, pieces)
    ]
    previous = jnp.where(piece > 0, end_of(piece - 1), -1.0)
    entered = entering(states, same, False)
    attended, total = attend(place, after(queries, feed_first, own, mid_others), row, blocks)
    mid_pieces = gather_core(mid_parts, mid_others)
    feed_parts = gather_inner(feed_first, attended)
    feed_others = gather_last(feed_parts)
    feed_pieces = gather_core(feed_parts, feed_others)
    carried = jnp.where(column == previous, jnp.exp(running), 0.0)
    reads = project[:, mixer_width + NS : mixer_width + 2 * NS]
    (
        layer_out,
        normed_two,
        feed_columns,
        grad_mix,
        mid_columns,
        grad_residual,
        grad_y,
        grad_att,
        grad_normed_part,
        grad_feed_gain,
        pulled,
    ) = middle(
        hidden_in,
        normed,
        cotangent,
        own,
        reads,
        entered,
        carried,
        spread,
        attended,
        feed_gain,
        mid_pieces,
        feed_pieces,
    )
    feed_args = (normed_two, cotangent, feed_columns, 2 * FF)
    mid_args = (normed, grad_mix, mid_columns, mixer_width)
    inner_stages = len(chip_masks()[0]) - 1
    feed_sent = weight_half(*feed_args, 1, 2048)
    feed_arrived = swap(feed_sent, 1)
    grad_query, *grad_blocks = attend_back(
        place, queries, row, after(grad_att, feed_sent), total, turn_cos, turn_sin, blocks
    )
    feed_kept = weight_half(*after(feed_args[:3], grad_blocks), feed_args[3], 0, 2048)
    grad_keys = scatter_ctx(grad_blocks)
    feed_sums = scatter_first(feed_kept, feed_arrived)
    mid_sent = weight_half(*after(mid_args[:3], feed_sums), mid_args[3], 1, 512)
    mid_arrived = swap(mid_sent, 1)
    grad_state = entering(pulled, [None] + [True] * (pieces - 1), True)
    mid_kept = weight_half(*after(mid_args[:3], mid_sent, grad_keys, grad_state), mid_args[3], 0, 512)
    mid_sums = scatter_first(mid_kept, mid_arrived)
    grad_project, small = state_back(
        project,
        bias,
        decay,
        skip,
        spread,
        column,
        row,
        after(grad_y, mid_sums),
        carried,
        entered,
        grad_state,
        grad_query,
        grad_keys,
        turn_cos,
        turn_sin,
    )
    feed_sums = scatter_chip(feed_sums, 0, inner_stages, grad_project)
    mix_args = (normed, normed, after(grad_project, feed_sums))
    mix_sent = weight_half(*mix_args, grad_project.shape[1], 1, 896)
    mix_arrived = swap(mix_sent, 1)
    mid_sums = scatter_chip(mid_sums, 0, inner_stages, mix_sent)
    mix_kept = weight_half(*after(mix_args, mid_sums), grad_project.shape[1], 0, 896)
    mix_sums = scatter_first(mix_kept, mix_arrived)
    grad_project = after(grad_project, mix_sums)
    grad_hidden, grad_norm_gain = project_back(
        hidden_in, norm_gain, grad_project, grad_normed_part, grad_residual, mix_pieces
    )
    gain_grads = jnp.dot(
        jnp.concatenate([grad_norm_gain, grad_feed_gain]),
        turn.T.astype(jnp.float32),
        precision=lax.Precision.HIGHEST,
    )
    packed = jnp.concatenate([gain_grads.reshape(-1, NS), small], axis=0)
    feed_sums = scatter_chip(feed_sums, inner_stages, 1, grad_hidden)
    steps = total_steps()
    packed = total_step(after(packed, feed_sums), *steps[0])
    mid_sums = scatter_chip(mid_sums, inner_stages, 1, packed)
    packed = total_step(after(packed, mid_sums), *steps[1])
    mix_sums = scatter_chip(mix_sums, 0, inner_stages, packed)
    packed = total_step(after(packed, mix_sums), *steps[2])
    mix_sums = scatter_chip(mix_sums, inner_stages, 1, packed)
    owned_feed, owned_mid, owned_mix = (scatter_last(v) for v in (feed_sums, mid_sums, mix_sums))
    for step in steps[3:]:
        packed = total_step(packed, *step)
    small, total_gain = packed[-small.shape[0] :], packed[: -small.shape[0]].reshape(2, width)
    total_norm, total_feed = total_gain[0], total_gain[1]
    total_bias, total_decay, total_skip = (small[i, :SH] for i in range(3))
    mix_edge = mixer_width + 2 * NS
    token_offset = grad_project.shape[1] - NS
    owned_in = jnp.concatenate(
        [
            owned_mid[:, :mixer_width],
            owned_mix[:, :mix_edge],
            owned_mix[:, token_offset : token_offset + SH],
            owned_mix[:, mix_edge:token_offset],
        ],
        axis=1,
    )
    owned_out = owned_mid[:, mixer_width:]
    layer_out, grad_hidden = (
        jnp.dot(v.astype(jnp.bfloat16), turn.T, preferred_element_type=jnp.float32).astype(
            jnp.bfloat16
        )
        for v in (layer_out, grad_hidden)
    )
    return (
        layer_out,
        grad_hidden,
        owned_in,
        owned_out.T,
        owned_feed[:, : 2 * FF],
        owned_feed[:, 2 * FF :].T,
        total_norm,
        total_feed,
        total_bias,
        total_decay,
        total_skip,
    )


def solution(mesh):
    return jax.shard_map(
        local,
        mesh=mesh,
        in_specs=(
            P(("fsdp", "ctx"), None),
            P(("fsdp", "ctx")),
            P(("fsdp", "ctx"), None),
            P(("fsdp", "ctx"), None),
            P(None, ("fsdp", "ctx")),
            P(("fsdp", "ctx"), None),
            P(None, ("fsdp", "ctx")),
            P(),
            P(),
            P(),
            P(),
            P(),
        ),
        out_specs=(
            P(("fsdp", "ctx"), None),
            P(("fsdp", "ctx"), None),
            P(("fsdp", "ctx"), None),
            P(None, ("fsdp", "ctx")),
            P(("fsdp", "ctx"), None),
            P(None, ("fsdp", "ctx")),
            P(),
            P(),
            P(),
            P(),
            P(),
        ),
        check_vma=False,
    )
```

```python
import jax
import jax.numpy as jnp
from jax import lax
from jax.experimental import pallas as pl
from jax.experimental.pallas import tpu as pltpu
from jax.sharding import PartitionSpec as P

FF = 2048
SH = 24
SP = 64
NS = 128
QUERY_HEADS = 8
KEY_VALUE_HEADS = 2
HEAD_SIZE = 64
KEY_WIDTH = KEY_VALUE_HEADS * HEAD_SIZE
REPEAT = QUERY_HEADS // KEY_VALUE_HEADS


EPSILON = 1e-06
ROTARY_BASE = 100000000000.0


def swap(value, mask):
    size = lax.axis_size("fsdp")
    return lax.ppermute(value, "fsdp", [(i, i ^ mask) for i in range(size)])


def swap_ctx(value, mask):
    size = lax.axis_size("ctx")
    return lax.ppermute(value, "ctx", [(i, i ^ mask) for i in range(size)])


def after(value, *others):
    return lax.optimization_barrier((value, others))[0]


def chip_masks():
    bits = lax.axis_size("fsdp").bit_length() - 2
    masks = [2 << i for i in range(bits)]
    x_masks, y_masks = masks[: bits // 2], masks[bits // 2 :]
    return (y_masks + x_masks, x_masks + y_masks)


def gather_first(blocks):
    half = len(blocks) // 2
    return [jnp.concatenate(blocks[:half], axis=0), jnp.concatenate(blocks[half:], axis=0)]


def gather_inner(parts, *hold):
    out = []
    for part, masks in zip(parts, chip_masks()):
        for mask in masks[:-1]:
            part = jnp.concatenate([part, after(swap(part, mask), *hold)], axis=0)
        out.append(part)
    return out


def gather_last(parts):
    return [swap(part, masks[-1]) for part, masks in zip(parts, chip_masks())]


def gather_core(parts, others):
    pieces = []
    for own in zip(parts, others):
        pieces += list(own) + [swap(piece, 1) for piece in own]
    return pieces


def piece_rows(width):
    devices = lax.axis_size("fsdp")
    block = width // (2 * devices)
    runs = []
    for half, masks in enumerate(chip_masks()):
        for core in (0, 1):
            for last in (0, 1):
                piece = half * 4 + core * 2 + last
                for inner in range(devices // 4):
                    chip = last * masks[-1]
                    for i, mask in enumerate(masks[:-1]):
                        chip += ((inner >> i) & 1) * mask
                    start = core * (width // 2) + half * (width // 4) + (chip >> 1) * block
                    runs.append((piece, inner * block, start, block))
    return runs


def plus(left, right):
    return (left.astype(jnp.float32) + right.astype(jnp.float32)).astype(jnp.bfloat16)


def total(values):
    result = values[0].astype(jnp.float32)
    for value in values[1:]:
        result = result + value.astype(jnp.float32)
    return result


def split_next(parts, stage):
    stay, go = [], []
    for terms, masks in zip(parts, chip_masks()):
        order = masks[::-1]
        axis = sorted(order[stage:], reverse=True).index(order[stage])
        stay.append([lax.index_in_dim(v, 0, axis, keepdims=False) for v in terms])
        go.append(
            total([lax.index_in_dim(v, 1, axis, keepdims=False) for v in terms]).astype(jnp.bfloat16)
        )
    return stay, go


def arrive(stay, go, stage, *hold):
    return [
        terms + [after(swap(value, masks[::-1][stage]), *hold)]
        for terms, value, masks in zip(stay, go, chip_masks())
    ]


def next_go(stay, go, *hold):
    parts = arrive(stay, go, 0, *hold)
    last = len(chip_masks()[0]) - 1
    for stage in range(1, last):
        stay, go = split_next(parts, stage)
        parts = arrive(stay, go, stage)
    return split_next(parts, last)


def low_total(terms):
    return total(terms).astype(jnp.bfloat16)


def scatter_near(stay, go, hold):
    pieces = lax.axis_size("ctx")
    blocks = []
    for terms in arrive(stay, go, len(chip_masks()[0]) - 1, hold):
        rows = terms[0].shape[0] // (pieces // 2)
        blocks += [[v[j * rows : (j + 1) * rows] for v in terms] for j in range(pieces // 2)]
    size = pieces
    while size > 4:
        size //= 2
        blocks = [blocks[j] + [swap_ctx(low_total(blocks[j + size]), size)] for j in range(size)]
    return blocks[0], blocks[2], [low_total(blocks[1]), low_total(blocks[3])]


def scatter_far(stay, through, go, *hold):
    one, far = after([swap_ctx(v, 1) for v in go], *hold)
    return stay + [one], low_total(through + [far])


def scatter_end(stay, two):
    return total(stay + [swap_ctx(two, 2)])


NT = (((1,), (1,)), ((), ()))
TN = (((0,), (0,)), ((), ()))
VMEM_BYTES = 58 * 1024 * 1024


def cost(microseconds):
    return pl.CostEstimate(
        flops=int(microseconds * 1e9), bytes_accessed=int(microseconds * 3e6), transcendentals=0
    )


def params():
    return pltpu.CompilerParams(vmem_limit_bytes=VMEM_BYTES)


def weight_kernel(edge, rows_one, rows_two, columns, out, turned):
    step = pl.program_id(0)

    @pl.when(step == 0)
    def _():
        turned[...] = rows_one[...].T

    @pl.when(step == edge)
    def _():
        turned[...] = rows_two[...].T

    out[...] = dot(turned[...], columns[...]).astype(jnp.bfloat16)


def weight_half(rows_one, rows_two, columns, edge, half, tile=512):
    tokens, width = rows_one.shape
    half_rows = pl.BlockSpec((tokens, width // 2), lambda j: (0, half))
    count = columns.shape[1]
    return pl.pallas_call(
        lambda *refs: weight_kernel(edge // tile, *refs),
        grid=(count // tile,),
        in_specs=[half_rows, half_rows, pl.BlockSpec((tokens, tile), lambda j: (0, j))],
        out_specs=pl.BlockSpec((width // 2, tile), lambda j: (0, j)),
        out_shape=jax.ShapeDtypeStruct((width // 2, count), jnp.bfloat16),
        scratch_shapes=[pltpu.VMEM((width // 2, tokens), jnp.bfloat16)],
        compiler_params=params(),
        name="weight_grad",
        cost_estimate=cost(0),
    )(rows_one, rows_two, columns)


def sum_rows(width):
    devices = lax.axis_size("fsdp")
    block = width // (2 * devices)
    runs = []
    for half, masks in enumerate(chip_masks()):
        bit = masks[-1] >> 1
        for value in (0, bit):
            chips = [c for c in range(devices // 2) if c & bit == value]
            runs.append([half * (width // 4) + c * block for c in chips])
    return runs, block


def weight_sum_kernel(edge, runs, block, rows_one, rows_two, columns, arrived, *refs):
    out, turned = refs[:4], refs[4]
    step = pl.program_id(0)

    @pl.when(step == 0)
    def _():
        turned[...] = rows_one[...].T

    @pl.when(step == edge)
    def _():
        turned[...] = rows_two[...].T

    value = dot(turned[...], columns[...]) + arrived[...].astype(jnp.float32)
    value = value.astype(jnp.bfloat16)
    for ref, starts in zip(out, runs):
        for i, start in enumerate(starts):
            ref[i * block : (i + 1) * block, :] = value[start : start + block]


def weight_sum(rows_one, rows_two, columns, edge, arrived, tile):
    tokens, width = rows_one.shape
    half_rows = pl.BlockSpec((tokens, width // 2), lambda j: (0, 0))
    count = columns.shape[1]
    runs, block = sum_rows(width)
    results = pl.pallas_call(
        lambda *refs: weight_sum_kernel(edge // tile, runs, block, *refs),
        grid=(count // tile,),
        in_specs=[
            half_rows,
            half_rows,
            pl.BlockSpec((tokens, tile), lambda j: (0, j)),
            pl.BlockSpec((width // 2, tile), lambda j: (0, j)),
        ],
        out_specs=[pl.BlockSpec((width // 8, tile), lambda j: (0, j))] * 4,
        out_shape=[jax.ShapeDtypeStruct((width // 8, count), jnp.bfloat16)] * 4,
        scratch_shapes=[pltpu.VMEM((width // 2, tokens), jnp.bfloat16)],
        compiler_params=params(),
        name="weight_sum",
        cost_estimate=cost(0),
    )(rows_one, rows_two, columns, arrived)
    shape = [2] * (len(chip_masks()[0]) - 1) + [block, count]
    stay_a, go_a, stay_b, go_b = (v.reshape(shape) for v in results)
    return [[stay_a], [stay_b]], [go_a, go_b]


def fetch(pieces, whole, semaphore, runs, start, stop):
    for piece, source, target, count in runs:
        pltpu.make_async_copy(
            pieces[piece].at[pl.ds(source, count), start:stop],
            whole.at[pl.ds(target, count), start:stop],
            semaphore,
        ).start()


def fetched(whole, semaphore, start, stop):
    view = whole.at[:, start:stop]
    pltpu.make_async_copy(view, view, semaphore).wait()


def dot(left, right):
    return jnp.dot(left, right, preferred_element_type=jnp.float32)


def dot_nt(left, right):
    return lax.dot_general(left, right, NT, preferred_element_type=jnp.float32)


def tiles(total, tile, body):
    for start in range(0, total, tile):
        body(slice(start, start + tile))


def looped(total, tile, body):
    @pl.loop(0, total // tile)
    def _(i):
        body(pl.ds(pl.multiple_of(i * tile, tile), tile))


def project_kernel(runs, hidden, gain, turn_cos, turn_sin, segment_row, *refs):
    pieces, refs = refs[:8], refs[8:]
    normed, project, queries, packed, whole, semaphore = refs
    columns, tokens = whole.shape[1], hidden.shape[0]
    fetch(pieces, whole, semaphore, runs, 0, columns)
    h = hidden[...].astype(jnp.float32)
    inverse = lax.rsqrt(jnp.mean(h * h, axis=-1, keepdims=True) + EPSILON)
    normed[...] = (h * inverse * gain[...]).astype(jnp.bfloat16)
    fetched(whole, semaphore, 0, columns)

    def body(at):
        project[:, at] = dot(normed[...], whole[:, at])

    tiles(columns, 384, body)
    start = SH * SP + 2 * NS
    turned = project[:, start : start + QUERY_HEADS * HEAD_SIZE].T
    queries[...] = (rotate(turned, turn_cos, turn_sin) * HEAD_SIZE ** (-0.5)).astype(jnp.bfloat16)
    start = start + QUERY_HEADS * HEAD_SIZE
    keys = rotate(project[:, start : start + KEY_WIDTH].T, turn_cos, turn_sin)
    packed[:tokens, :KEY_WIDTH] = keys.T.astype(jnp.bfloat16)
    start = start + KEY_WIDTH
    packed[:tokens, KEY_WIDTH:] = project[:, start : start + KEY_WIDTH].astype(jnp.bfloat16)
    packed[tokens:, :] = jnp.broadcast_to(segment_row[...], (16, 2 * KEY_WIDTH)).astype(jnp.bfloat16)


def rotate(turned, turn_cos, turn_sin, sign=1.0):
    half = HEAD_SIZE // 2
    c, s = turn_cos[...], turn_sin[...] * sign
    out = []
    for start in range(0, turned.shape[0], HEAD_SIZE):
        first, second = turned[start : start + half], turned[start + half : start + HEAD_SIZE]
        out += [first * c - second * s, second * c + first * s]
    return jnp.concatenate(out, axis=0)


def full_specs(count):
    return [pl.BlockSpec(memory_space=pltpu.VMEM)] * count


def any_specs(count):
    return [pl.BlockSpec(memory_space=pl.ANY)] * count


def project_in(hidden, gain, turn_cos, turn_sin, segment_row, pieces):
    tokens, width = hidden.shape
    columns = pieces[0].shape[1]
    runs = piece_rows(width)
    return pl.pallas_call(
        lambda *refs: project_kernel(runs, *refs),
        in_specs=full_specs(5) + any_specs(8),
        out_specs=full_specs(4),
        out_shape=[
            jax.ShapeDtypeStruct((tokens, width), jnp.bfloat16),
            jax.ShapeDtypeStruct((tokens, columns), jnp.float32),
            jax.ShapeDtypeStruct((QUERY_HEADS * HEAD_SIZE, tokens), jnp.bfloat16),
            jax.ShapeDtypeStruct((tokens + 16, 2 * KEY_WIDTH), jnp.bfloat16),
        ],
        scratch_shapes=[pltpu.VMEM((width, columns), jnp.bfloat16), pltpu.SemaphoreType.DMA],
        compiler_params=params(),
        name="project_in",
        cost_estimate=cost(0),
    )(hidden, gain[None], turn_cos, turn_sin, segment_row, *pieces)


def spread_heads():
    head = lax.broadcasted_iota(jnp.int32, (NS, SH * SP), 1) // SP
    return (lax.broadcasted_iota(jnp.int32, (NS, SH * SP), 0) == head).astype(jnp.float32)


def dot_exact(left, right):
    return jnp.dot(
        left, right, precision=lax.Precision.HIGHEST, preferred_element_type=jnp.float32
    )


def step_terms(project, bias, decay):
    tokens = project.shape[0]
    raw = project[:, project.shape[1] - NS :] + bias[...]
    step = jnp.maximum(raw, 0.0) + jnp.log1p(jnp.exp(-jnp.abs(raw)))
    rate = -jnp.exp(decay[...]) * step
    rows = lax.broadcasted_iota(jnp.int32, (tokens, tokens), 0)
    columns = lax.broadcasted_iota(jnp.int32, (tokens, tokens), 1)
    running = dot_exact((rows >= columns).astype(jnp.float32), rate)
    return raw, step, rate, running


def tail_terms(running, segment_column):
    tokens = running.shape[0]
    same = segment_column[...] == segment_column[tokens - 1 :, :]
    return jnp.where(same, jnp.exp(running[tokens - 1 :, :] - running), 0.0)


def split_low(values):
    high = values.astype(jnp.bfloat16)
    return high, (values - high.astype(jnp.float32)).astype(jnp.bfloat16)


def twice(values):
    return jnp.concatenate([values, values], axis=0)


def state_kernel(project, bias, decay, skip, spread, column, row, own, packed, running_out, bias_sum, turned):
    tokens, inner = own.shape
    _, step, _, running = step_terms(project, bias, decay)
    running_out[...] = running
    tail = tail_terms(running, column) * step
    tail = dot_exact(tail, spread[...])
    values = project[:, :inner]
    states = dot(project[:, inner : inner + NS].T.astype(jnp.bfloat16), (tail * values).astype(jnp.bfloat16))
    packed[:NS, :] = states.astype(jnp.bfloat16)
    last = dot_exact(jnp.broadcast_to(jnp.exp(running[tokens - 1 :, :]), (8, NS)), spread[...])
    packed[NS:, :] = jnp.concatenate([last, last], axis=0).astype(jnp.bfloat16)
    at_row = lax.broadcasted_iota(jnp.int32, (tokens, tokens), 0)
    at_column = lax.broadcasted_iota(jnp.int32, (tokens, tokens), 1)
    allowed = (at_row >= at_column) & (column[...] == row[...])
    turned[0] = running.T
    turned[1] = step.T
    bias_sum[...] = jnp.where(allowed, 0.0, -1e30)
    match = lax.dot_general(
        project[:, inner + NS : inner + 2 * NS],
        project[:, inner : inner + NS],
        NT,
        precision=lax.Precision.HIGHEST,
        preferred_element_type=jnp.float32,
    )
    lane = lax.broadcasted_iota(jnp.int32, (tokens, NS), 1)

    for pair in range(SH // 2):
        at = slice(pair * NS, (pair + 1) * NS)
        values = project[:, at]
        parts = []
        for k in (0, 1):
            head = 2 * pair + k
            gap = running_out[:, head : head + 1] - turned[0, slice(head, head + 1), :]
            weight = jnp.exp(jnp.minimum(gap, 0.0) + bias_sum[...])
            weight = weight * match * turned[1, slice(head, head + 1), :]
            parts.append(dot(weight.astype(jnp.bfloat16), values.astype(jnp.bfloat16)))
        own[:, at] = jnp.where(lane < SP, parts[0], parts[1]) + skip[:, at] * values


def state_forward(project, bias, decay, skip, spread, column, row):
    tokens, inner = project.shape[0], SH * SP
    return pl.pallas_call(
        state_kernel,
        in_specs=full_specs(7),
        out_specs=full_specs(3),
        out_shape=[
            jax.ShapeDtypeStruct((tokens, inner), jnp.float32),
            jax.ShapeDtypeStruct((NS + 16, inner), jnp.bfloat16),
            jax.ShapeDtypeStruct((tokens, NS), jnp.float32),
        ],
        scratch_shapes=[
            pltpu.VMEM((tokens, tokens), jnp.float32),
            pltpu.VMEM((2, NS, tokens), jnp.float32),
        ],
        compiler_params=params(),
        name="state_forward",
        cost_estimate=cost(0),
    )(project, bias, decay, skip, spread, column, row)


def key_masks(place, row, blocks, masks):
    tokens = row.shape[1]
    key = lax.broadcasted_iota(jnp.int32, (tokens, tokens), 0)
    query = lax.broadcasted_iota(jnp.int32, (tokens, tokens), 1)
    for j, block in enumerate(blocks):
        label = block[tokens : tokens + 16, :tokens].astype(jnp.float32).T[:, :1]
        ahead = ((place[0] ^ j) - place[0]) * tokens
        allowed = (key + ahead <= query) & (label == row[...])
        masks[j] = jnp.where(allowed, 0.0, -1e30)


def attend_kernel(count, place, queries, row, *refs):
    blocks, refs = refs[:count], refs[count:]
    attended, total, flags, masks, scores, turned, values = refs
    tokens = row.shape[1]
    ends = [block[tokens : tokens + 16, tokens - 1 : tokens].astype(jnp.float32)[:8] for block in blocks]

    def end_of(number):
        found = jnp.zeros((8, 1), jnp.float32)
        for j, end in enumerate(ends):
            found = found + jnp.where((place[0] ^ j) == number, end, 0.0)
        return found

    lane = lax.broadcasted_iota(jnp.int32, (8, NS), 1)
    known = jnp.where(lane == NS - 1, jnp.where(place[0] > 0, end_of(place[0] - 1), -1.0), 0.0)
    for k in range(count):
        same = (end_of(place[0] - k) == end_of(place[0] - k - 1)) & (place[0] > k)
        known = known + jnp.where((lane == k) & same, 1.0, 0.0)
    flags[...] = known
    key_masks(place, row, blocks, masks)
    for j, block in enumerate(blocks):
        values[j] = block[:tokens, KEY_WIDTH:].T
    for group in range(KEY_VALUE_HEADS):
        lanes = slice(group * HEAD_SIZE, (group + 1) * HEAD_SIZE)

        for r in range(REPEAT):
            head = group * REPEAT + r
            at = slice(head * HEAD_SIZE, (head + 1) * HEAD_SIZE)
            highest = None
            for j, block in enumerate(blocks):
                score = dot(block[:tokens, lanes], queries[at, :]) + masks[j]
                scores[j] = score
                top = jnp.max(score, axis=0, keepdims=True)
                highest = top if highest is None else jnp.maximum(highest, top)
            sums = 0.0
            for j in range(count):
                score = jnp.exp(scores[j] - highest)
                scores[j] = score
                sums = sums + jnp.sum(score, axis=0, keepdims=True)
            inverse = 1.0 / sums
            result = 0.0
            for j in range(count):
                result = result + dot(values[j, lanes, :], (scores[j] * inverse).astype(jnp.bfloat16))
            turned[at, :] = result
            total[slice(head, head + 1), :] = highest + jnp.log(sums)

    attended[...] = turned[...].T.astype(jnp.bfloat16)


def attend(place, queries, row, blocks):
    tokens, count = row.shape[1], len(blocks)
    return pl.pallas_call(
        lambda *refs: attend_kernel(count, *refs),
        in_specs=[pl.BlockSpec(memory_space=pltpu.SMEM)] + full_specs(2 + count),
        out_specs=full_specs(3),
        out_shape=[
            jax.ShapeDtypeStruct((tokens, QUERY_HEADS * HEAD_SIZE), jnp.bfloat16),
            jax.ShapeDtypeStruct((QUERY_HEADS, tokens), jnp.float32),
            jax.ShapeDtypeStruct((8, NS), jnp.float32),
        ],
        scratch_shapes=[
            pltpu.VMEM((count, tokens, tokens), jnp.float32),
            pltpu.VMEM((count, tokens, tokens), jnp.float32),
            pltpu.VMEM((QUERY_HEADS * HEAD_SIZE, tokens), jnp.float32),
            pltpu.VMEM((count, KEY_WIDTH, tokens), jnp.bfloat16),
        ],
        compiler_params=params(),
        name="attend",
        cost_estimate=cost(0),
    )(place, queries, row, *blocks)


def attend_back_kernel(count, place, queries, row, grad_att, total, turn_cos, turn_sin, *refs):
    blocks, refs = refs[:count], refs[count:]
    grad_query, grad_blocks, refs = refs[0], refs[1 : 1 + count], refs[1 + count :]
    masks, chances, slopes, turned_keys, turned_grad, grad_turned, key_sums, value_sums = refs
    tokens = row.shape[1]
    key_masks(place, row, blocks, masks)
    turned_grad[...] = grad_att[...].T
    for j, block in enumerate(blocks):
        turned_keys[j] = block[:tokens, :KEY_WIDTH].T
    for group in range(KEY_VALUE_HEADS):
        lanes = slice(group * HEAD_SIZE, (group + 1) * HEAD_SIZE)
        ahead = slice(KEY_WIDTH + group * HEAD_SIZE, KEY_WIDTH + (group + 1) * HEAD_SIZE)
        key_sums[...] = jnp.zeros_like(key_sums)
        value_sums[...] = jnp.zeros_like(value_sums)

        for r in range(REPEAT):
            head = group * REPEAT + r
            at = slice(head * HEAD_SIZE, (head + 1) * HEAD_SIZE)
            query, grad = queries[at, :], turned_grad[at, :]
            query_rows, grad_rows = query.T, grad.T
            inside = 0.0
            for j, block in enumerate(blocks):
                score = dot(block[:tokens, lanes], query) + masks[j]
                chance = jnp.exp(score - total[slice(head, head + 1), :])
                slope = dot(block[:tokens, ahead], grad)
                chances[j], slopes[j] = chance, slope
                inside = inside + jnp.sum(chance * slope, axis=0, keepdims=True)
                value_sums[j] = value_sums[j] + dot(chance.astype(jnp.bfloat16), grad_rows)
            result = 0.0
            for j in range(count):
                slope = (chances[j] * (slopes[j] - inside)).astype(jnp.bfloat16)
                key_sums[j] = key_sums[j] + dot(slope, query_rows)
                result = result + dot(turned_keys[j, lanes, :], slope)
            grad_turned[at, :] = result

        for j in range(count):
            grad_blocks[j][:, lanes] = key_sums[j].astype(jnp.bfloat16)
            grad_blocks[j][:, ahead] = value_sums[j].astype(jnp.bfloat16)
    turned = rotate(grad_turned[...], turn_cos, turn_sin, -1.0) * HEAD_SIZE ** (-0.5)
    grad_query[...] = turned.T.astype(jnp.bfloat16)


def attend_back(place, queries, row, grad_att, total, turn_cos, turn_sin, blocks):
    tokens, count = row.shape[1], len(blocks)
    square = pltpu.VMEM((count, tokens, tokens), jnp.float32)
    heads = QUERY_HEADS * HEAD_SIZE
    return pl.pallas_call(
        lambda *refs: attend_back_kernel(count, *refs),
        in_specs=[pl.BlockSpec(memory_space=pltpu.SMEM)] + full_specs(6 + count),
        out_specs=full_specs(1 + count),
        out_shape=[jax.ShapeDtypeStruct((tokens, heads), jnp.bfloat16)]
        + [jax.ShapeDtypeStruct((tokens, 2 * KEY_WIDTH), jnp.bfloat16)] * count,
        scratch_shapes=[
            square,
            square,
            square,
            pltpu.VMEM((count, KEY_WIDTH, tokens), jnp.bfloat16),
            pltpu.VMEM((heads, tokens), jnp.bfloat16),
            pltpu.VMEM((heads, tokens), jnp.float32),
            pltpu.VMEM((count, tokens, HEAD_SIZE), jnp.float32),
            pltpu.VMEM((count, tokens, HEAD_SIZE), jnp.float32),
        ],
        compiler_params=params(),
        name="attend_back",
        cost_estimate=cost(60),
    )(place, queries, row, grad_att, total, turn_cos, turn_sin, *blocks)


def state_back_kernel(
    project, bias, decay, skip, spread, column, row, grad_y, carried, entered, near, far,
    grad_query, grad_keys, turn_cos, turn_sin,
    grad_project, small, grad_state, bias_sum, turned, match_grad, column_sums, row_sums, running_keep, step_keep,
):
    tokens, inner = grad_y.shape
    raw, step, rate, running = step_terms(project, bias, decay)
    running_keep[...], step_keep[...] = running, step
    grad_state[...] = entered_state(jnp.ones((8, NS), jnp.float32), near, far)
    decayed = tail_terms(running, column)
    tail = decayed * step
    turned[...] = running.T
    values_b = project[:, inner : inner + NS]
    values_c = project[:, inner + NS : inner + 2 * NS]
    low_b, low_c = values_b.astype(jnp.bfloat16), values_c.astype(jnp.bfloat16)
    both_b = jnp.concatenate(split_low(values_b), axis=1)
    both_c = jnp.concatenate(split_low(values_c), axis=1)
    key = lax.broadcasted_iota(jnp.int32, (tokens, tokens), 0)
    query = lax.broadcasted_iota(jnp.int32, (tokens, tokens), 1)
    bias_sum[...] = jnp.where((query >= key) & (column[...] == row[...]), 0.0, -1e30)
    match = lax.dot_general(
        values_b, values_c, NT, precision=lax.Precision.HIGHEST, preferred_element_type=jnp.float32
    )
    match_grad[...] = jnp.zeros_like(match_grad)
    column_sums[...] = jnp.zeros_like(column_sums)
    row_sums[...] = jnp.zeros_like(row_sums)
    lane = lax.broadcasted_iota(jnp.int32, (tokens, NS), 1)

    for pair in range(SH // 2):
        at = slice(pair * NS, (pair + 1) * NS)
        low, rest = split_low(project[:, at])
        low_grad, rest_grad = split_low(grad_y[:, at])
        turned_grad, turned_rest = low_grad.T, rest_grad.T
        parts = []
        for k in (0, 1):
            head = 2 * pair + k
            rows = slice(k * SP, (k + 1) * SP)
            gap = turned[slice(head, head + 1), :] - running_keep[:, head : head + 1]
            weight = jnp.exp(jnp.minimum(gap, 0.0) + bias_sum[...])
            step_column = step_keep[:, head : head + 1]
            slope = dot(
                jnp.concatenate([low[:, rows], rest[:, rows], low[:, rows]], axis=1),
                jnp.concatenate([turned_grad[rows], turned_grad[rows], turned_rest[rows]], axis=0),
            )
            slope = slope * weight
            scaled = slope * step_column
            match_grad[...] = match_grad[...] + scaled
            row_sums[slice(head, head + 1), :] = jnp.sum(scaled * match, axis=0, keepdims=True)
            sums = jnp.sum(slope * match, axis=1, keepdims=True)
            column_sums[...] = column_sums[...] + jnp.where(lane == head, sums, 0.0)
            weight = weight * match * step_column
            parts.append(dot(weight.astype(jnp.bfloat16), low_grad))
        grad_x = jnp.where(lane < SP, parts[0], parts[1]) + skip[:, at] * grad_y[:, at]
        tail_wide = dot_exact(tail, spread[:, at])
        grad_x = grad_x + tail_wide * dot(low_b, grad_state[:, at])
        grad_project[:, at] = grad_x.astype(jnp.bfloat16)

    x, grad = project[:, :inner], grad_y[...]
    carried_wide = dot_exact(carried[...], spread[...])
    tail_wide = dot_exact(tail, spread[...])
    out_b = dot_nt((tail_wide * x).astype(jnp.bfloat16), grad_state[...])
    out_c = dot_nt((carried_wide * grad).astype(jnp.bfloat16), entered[...])
    low_match = match_grad[...].astype(jnp.bfloat16)
    out_b = out_b + dot(low_match, low_c)
    out_c = out_c + dot(match_grad[...].T.astype(jnp.bfloat16), low_b)
    grad_project[:, inner : inner + NS] = out_b.astype(jnp.bfloat16)
    grad_project[:, inner + NS : inner + 2 * NS] = out_c.astype(jnp.bfloat16)

    def per_head(wide):
        return lax.dot_general(
            wide, spread[...], NT, precision=lax.Precision.HIGHEST, preferred_element_type=jnp.float32
        )

    grad_tail = per_head(x * dot(both_b, twice(grad_state[...])))
    grad_carried = per_head(grad * dot(both_c, twice(entered[...])))
    kept = jnp.sum(grad_state[...].astype(jnp.float32) * entered[...].astype(jnp.float32), axis=0, keepdims=True)
    kept = per_head(jnp.broadcast_to(kept, (8, inner)))[:1]
    at_token = lax.broadcasted_iota(jnp.int32, (tokens, NS), 0)
    grad_carried = grad_carried + jnp.where(at_token == tokens - 1, kept, 0.0)
    grad_step = column_sums[...] + grad_tail * decayed
    through = grad_tail * tail
    grad_running = row_sums[...].T - step * column_sums[...] + grad_carried * carried[...] - through
    through = jnp.sum(through, axis=0, keepdims=True)
    grad_running = grad_running + jnp.where(at_token == tokens - 1, through, 0.0)
    grad_rate = dot_exact((query >= key).astype(jnp.float32), grad_running)
    grad_step = grad_step - grad_rate * jnp.exp(decay[...])
    grad_raw = grad_step * jax.nn.sigmoid(raw)
    grad_raw = jnp.where(lane < SH, grad_raw, 0.0)
    grad_skip = per_head(jnp.broadcast_to(jnp.sum(grad * x, axis=0, keepdims=True), (8, inner)))[:1]
    small[0:1, :] = jnp.sum(grad_raw, axis=0, keepdims=True)
    small[1:2, :] = jnp.sum(grad_rate * rate, axis=0, keepdims=True)
    small[2:3, :] = grad_skip
    small[3:, :] = jnp.zeros((5, NS), jnp.float32)
    start = inner + 2 * NS
    heads = QUERY_HEADS * HEAD_SIZE
    grad_project[:, start : start + heads] = grad_query[...]
    start = start + heads
    turned_key = rotate(grad_keys[:, :KEY_WIDTH].T, turn_cos, turn_sin, -1.0)
    grad_project[:, start : start + KEY_WIDTH] = turned_key.T.astype(jnp.bfloat16)
    start = start + KEY_WIDTH
    grad_project[:, start : start + KEY_WIDTH] = grad_keys[:, KEY_WIDTH:].astype(jnp.bfloat16)
    grad_project[:, start + KEY_WIDTH :] = grad_raw.astype(jnp.bfloat16)


def state_back(project, *others):
    tokens, inner = project.shape[0], SH * SP
    square = pltpu.VMEM((tokens, tokens), jnp.float32)
    narrow = pltpu.VMEM((tokens, NS), jnp.float32)
    return pl.pallas_call(
        state_back_kernel,
        in_specs=full_specs(1 + len(others)),
        out_specs=full_specs(2),
        out_shape=[
            jax.ShapeDtypeStruct(project.shape, jnp.bfloat16),
            jax.ShapeDtypeStruct((8, NS), jnp.float32),
        ],
        scratch_shapes=[
            pltpu.VMEM((NS, inner), jnp.bfloat16),
            square,
            pltpu.VMEM((NS, tokens), jnp.float32),
            square,
            narrow,
            pltpu.VMEM((NS, tokens), jnp.float32),
            narrow,
            narrow,
        ],
        compiler_params=params(),
        name="state_back",
        cost_estimate=cost(60),
    )(project, *others)


def shift_ctx(value, by, reverse):
    size = lax.axis_size("ctx")
    pairs = [(i, i + by) for i in range(size - by)]
    return lax.ppermute(value, "ctx", [(j, i) for i, j in pairs] if reverse else pairs)


def join_kernel(flags, own, near, both):
    keep = own[NS : NS + 1, :].astype(jnp.float32) * flags[0:1, 0:1]
    both[...] = (own[:NS, :].astype(jnp.float32) + keep * near[:NS, :].astype(jnp.float32)).astype(
        jnp.bfloat16
    )


def entering_near(packed, same, reverse):
    near = shift_ctx(packed, 1, reverse)
    if lax.axis_size("ctx") != 4:
        return near, packed
    both = pl.pallas_call(
        join_kernel,
        in_specs=full_specs(3),
        out_specs=full_specs(1)[0],
        out_shape=jax.ShapeDtypeStruct((NS, packed.shape[1]), jnp.bfloat16),
        compiler_params=params(),
        name="join",
        cost_estimate=cost(0),
    )(same, packed, near)
    return near, both


def entering_far(both, same, reverse):
    if lax.axis_size("ctx") == 4:
        return shift_ctx(both, 2, reverse)
    total, decay = 0.0, 1.0
    for shift in range(2, lax.axis_size("ctx")):
        part = shift_ctx(both, shift, reverse).astype(jnp.float32)
        total = total + decay * part[:NS]
        decay = decay * same[0, shift] * part[NS : NS + 1]
    return total.astype(jnp.bfloat16)


def entered_state(flags, near, far):
    keep = near[NS : NS + 1, :].astype(jnp.float32) * flags[0:1, 1:2]
    state = near[:NS, :].astype(jnp.float32) + keep * far[...].astype(jnp.float32)
    return state.astype(jnp.bfloat16)


def project_back_kernel(runs, hidden, gain, grad_project, partial, grad_residual, *refs):
    pieces, (grad_hidden, gain_grad, whole, grad_normed, semaphore) = refs[:8], refs[8:]
    columns = whole.shape[1]
    fetch(pieces, whole, semaphore, runs, 0, columns)
    h = hidden[...].astype(jnp.float32)
    inverse = lax.rsqrt(jnp.mean(h * h, axis=-1, keepdims=True) + EPSILON)
    fetched(whole, semaphore, 0, columns)

    def body(at):
        grad_normed[:, at] = partial[:, at] + dot_nt(grad_project[...], whole[at, :])

    tiles(whole.shape[0], 256, body)
    grad = grad_normed[...]
    gain_grad[...] = jnp.sum(grad * h * inverse, axis=0, keepdims=True)
    scaled = grad * gain[...]
    mean = jnp.mean(scaled * h, axis=-1, keepdims=True)
    grad_hidden[...] = (
        grad_residual[...] + inverse * scaled - h * (inverse * inverse * inverse) * mean
    ).astype(jnp.bfloat16)


def project_back(hidden, gain, grad_project, partial, grad_residual, pieces):
    tokens, width = hidden.shape
    columns = pieces[0].shape[1]
    runs = piece_rows(width)
    return pl.pallas_call(
        lambda *refs: project_back_kernel(runs, *refs),
        in_specs=full_specs(5) + any_specs(8),
        out_specs=full_specs(2),
        out_shape=[
            jax.ShapeDtypeStruct((tokens, width), jnp.bfloat16),
            jax.ShapeDtypeStruct((1, width), jnp.float32),
        ],
        scratch_shapes=[
            pltpu.VMEM((width, columns), jnp.bfloat16),
            pltpu.VMEM((tokens, width), jnp.float32),
            pltpu.SemaphoreType.DMA,
        ],
        compiler_params=params(),
        name="project_back",
        cost_estimate=cost(8),
    )(hidden, gain[None], grad_project, partial, grad_residual, *pieces)


def middle_kernel(
    runs, flags, hidden, normed, cotangent, own, project, near, far, running, column, spread, attended, gain, *refs
):
    mid_pieces, feed_pieces, refs = refs[:8], refs[8:16], refs[16:]
    layer_out, normed_two, feed_columns, grad_mix, mid_columns = refs[:5]
    grad_residual, grad_y, grad_att, grad_normed, gain_grad, pulled, entered, carried = refs[5:13]
    mid, feed, gate_z, ssm_out, gate, up, residual, grad_two, semaphores = refs[13:]
    width, inner = hidden.shape[1], own.shape[1]
    reads = project[:, inner + NS : inner + 2 * NS]
    low_reads = jnp.concatenate(split_low(reads), axis=1)
    turned_reads = reads.T.astype(jnp.bfloat16)
    middle_width = inner + attended.shape[1]
    edges = [0, inner, inner + middle_width]
    hidden_units = feed.shape[1] // 3
    tile, rows = 512, 256
    mid_runs = [(0, edges[1]), (edges[1], edges[2])]
    for i, (start, stop) in enumerate(mid_runs):
        fetch(mid_pieces, mid, semaphores.at[i], runs, start, stop)
    feed_runs = [(0, 2 * hidden_units), (2 * hidden_units, 3 * hidden_units)]
    for i, (start, stop) in enumerate(feed_runs):
        fetch(feed_pieces, feed, semaphores.at[2 + i], runs, start, stop)
    entered[...] = entered_state(flags, near, far)
    carried[...] = jnp.where(column[...] == flags[0:1, NS - 1 : NS], jnp.exp(running[...]), 0.0)

    def shift(at, by):
        return pl.ds(pl.multiple_of(at.start + by, 128), at.size)

    fetched(mid, semaphores.at[0], 0, inner)

    def gating(at):
        z = dot(normed[...], mid[:, at])
        gate_z[:, at] = z
        wide = dot_exact(carried[...], spread[:, at])
        y = own[:, at] + wide * dot(low_reads, twice(entered[:, at]))
        ssm_out[:, at] = y
        gated = y * (z * jax.nn.sigmoid(z))
        mid_columns[:, shift(at, inner)] = gated.astype(jnp.bfloat16)

    looped(inner, tile, gating)
    mid_columns[:, 2 * inner :] = attended[...]
    fetched(mid, semaphores.at[1], inner, edges[2])

    def mixing(at):
        residual[:, at] = hidden[:, at].astype(jnp.float32) + dot_nt(
            mid_columns[:, inner:], mid[at, inner:]
        )

    looped(width, rows, mixing)
    value = residual[...]
    inverse = lax.rsqrt(jnp.mean(value * value, axis=-1, keepdims=True) + EPSILON)
    normed_two[...] = (value * inverse * gain[...]).astype(jnp.bfloat16)
    fetched(feed, semaphores.at[2], 0, 2 * hidden_units)

    def opening(at):
        g = dot(normed_two[...], feed[:, at])
        u = dot(normed_two[...], feed[:, shift(at, hidden_units)])
        gate[:, at] = g
        up[:, at] = u
        active = (g * jax.nn.sigmoid(g)) * u
        feed_columns[:, shift(at, 2 * hidden_units)] = active.astype(jnp.bfloat16)

    looped(hidden_units, tile, opening)
    fetched(feed, semaphores.at[3], 2 * hidden_units, 3 * hidden_units)

    def closing(at):
        layer_out[:, at] = (
            residual[:, at] + dot_nt(feed_columns[:, 2 * hidden_units :], feed[at, 2 * hidden_units :])
        ).astype(jnp.bfloat16)

    looped(width, rows, closing)

    def activation(at):
        grad_active = dot(cotangent[...], feed[:, shift(at, 2 * hidden_units)])
        g, u = gate[:, at], up[:, at]
        s = jax.nn.sigmoid(g)
        feed_columns[:, at] = (grad_active * u * (s * (1.0 + g * (1.0 - s)))).astype(jnp.bfloat16)
        feed_columns[:, shift(at, hidden_units)] = (grad_active * (g * s)).astype(jnp.bfloat16)

    looped(hidden_units, tile, activation)

    def opening_back(at):
        grad_two[:, at] = dot_nt(
            feed_columns[:, : 2 * hidden_units], feed[at, : 2 * hidden_units]
        )

    looped(width, rows, opening_back)
    value = residual[...]
    grad = grad_two[...]
    gain_grad[...] = jnp.sum(grad * value * inverse, axis=0, keepdims=True)
    scaled = grad * gain[...]
    mean = jnp.mean(scaled * value, axis=-1, keepdims=True)
    grad = (
        cotangent[...].astype(jnp.float32)
        + inverse * scaled
        - value * (inverse * inverse * inverse) * mean
    )
    grad_residual[...] = grad
    grad_mix[...] = grad.astype(jnp.bfloat16)

    def gating_back(at):
        grad_gated = dot(grad_mix[...], mid[:, shift(at, inner)])
        z = gate_z[:, at]
        s = jax.nn.sigmoid(z)
        grad = grad_gated * (z * s)
        grad_y[:, at] = grad
        wide = dot_exact(carried[...], spread[:, at])
        pulled[:NS, at] = dot(turned_reads, (wide * grad).astype(jnp.bfloat16)).astype(jnp.bfloat16)
        grad_z = grad_gated * ssm_out[:, at] * (s * (1.0 + z * (1.0 - s)))
        mid_columns[:, at] = grad_z.astype(jnp.bfloat16)

    looped(inner, tile, gating_back)
    grad_att[...] = dot(grad_mix[...], mid[:, 2 * inner :]).astype(jnp.bfloat16)

    def normed_back(at):
        grad_normed[:, at] = dot_nt(mid_columns[:, :inner], mid[at, :inner])

    looped(width, rows, normed_back)
    tokens = hidden.shape[0]
    last = jnp.broadcast_to(carried[tokens - 1 :, :], (8, NS))
    last = dot_exact(last, spread[...])
    pulled[NS:, :] = jnp.concatenate([last, last], axis=0).astype(jnp.bfloat16)


def middle(
    flags, hidden, normed, cotangent, own, project, near, far, running, column, spread, attended, gain,
    mid_pieces, feed_pieces
):
    tokens, width = hidden.shape
    inner, heads = own.shape[1], attended.shape[1]
    mid = 2 * inner + heads
    feed = feed_pieces[0].shape[1]
    runs = piece_rows(width)
    low = lambda n: jax.ShapeDtypeStruct((tokens, n), jnp.bfloat16)
    high = lambda n: jax.ShapeDtypeStruct((tokens, n), jnp.float32)
    return pl.pallas_call(
        lambda *refs: middle_kernel(runs, *refs),
        in_specs=full_specs(13) + any_specs(16),
        out_specs=full_specs(13),
        out_shape=[
            low(width),
            low(width),
            low(feed),
            low(width),
            low(mid),
            high(width),
            high(inner),
            low(heads),
            high(width),
            jax.ShapeDtypeStruct((1, width), jnp.float32),
            jax.ShapeDtypeStruct((NS + 16, inner), jnp.bfloat16),
            jax.ShapeDtypeStruct((NS, inner), jnp.bfloat16),
            high(NS),
        ],
        scratch_shapes=[
            pltpu.VMEM((width, mid), jnp.bfloat16),
            pltpu.VMEM((width, feed), jnp.bfloat16),
            pltpu.VMEM((tokens, inner), jnp.float32),
            pltpu.VMEM((tokens, inner), jnp.float32),
            pltpu.VMEM((tokens, feed // 3), jnp.float32),
            pltpu.VMEM((tokens, feed // 3), jnp.float32),
            pltpu.VMEM((tokens, width), jnp.float32),
            pltpu.VMEM((tokens, width), jnp.float32),
            pltpu.SemaphoreType.DMA((4,)),
        ],
        compiler_params=params(),
        name="middle",
        cost_estimate=cost(29),
    )(
        flags, hidden, normed, cotangent, own, project, near, far, running, column, spread, attended, gain[None],
        *mid_pieces, *feed_pieces
    )


def width_order(width):
    devices, pieces = lax.axis_size("fsdp"), lax.axis_size("ctx")
    rows = width // (devices * pieces)
    block = rows * pieces // 2
    place = jnp.arange(width)
    core, half = place // (width // 2), (place // (width // 4)) % 2
    inner = place % (width // 4)
    device = lax.axis_index("fsdp") ^ (2 * (inner // block) + core)
    along = lax.axis_index("ctx") ^ ((inner % block) // rows + half * (pieces // 2))
    return (device * pieces + along) * rows + inner % rows


def gather_ctx(value, *hold):
    size = lax.axis_size("ctx")
    blocks = [value]
    if size == 4:
        one, two = swap_ctx(value, 1), swap_ctx(value, 2)
        return [value, one, two, swap_ctx(after(two, one, *hold), 1)]
    mask = 1
    while mask < size:
        blocks = blocks + [swap_ctx(block, mask) for block in blocks]
        mask *= 2
    return blocks


def scatter_ctx(blocks, early, late):
    size = lax.axis_size("ctx")
    if size == 4:
        far = after(swap_ctx(blocks[3], 1), early)
        one, two = after([swap_ctx(blocks[1], 1), swap_ctx(plus(blocks[2], far), 2)], late)
        return total([blocks[0], one, two])
    while size > 1:
        size //= 2
        blocks = [plus(blocks[j], swap_ctx(blocks[j + size], size)) for j in range(size)]
    return blocks[0].astype(jnp.float32)


def total_steps():
    return [
        (axis, 1 << i)
        for axis in ("fsdp", "ctx")
        for i in range(lax.axis_size(axis).bit_length() - 1)
    ]


def total_step(value, axis, mask):
    pairs = [(i, i ^ mask) for i in range(lax.axis_size(axis))]
    return value + lax.ppermute(value, axis, pairs)


def local(
    hidden_in,
    segments,
    cotangent,
    mixer_in,
    mixer_out,
    gate_up,
    down_weight,
    norm_gain,
    feed_gain,
    step_bias,
    decay_log,
    skip_gain,
):
    mixer_width = SH * SP
    width = hidden_in.shape[1]
    edges = [mixer_width, 2 * mixer_width, 2 * mixer_width + 2 * NS]
    edges += [edges[-1] + SH, mixer_in.shape[1]]
    in_z = mixer_in[:, : edges[0]]
    in_mix = jnp.concatenate(
        [
            mixer_in[:, edges[0] : edges[2]],
            mixer_in[:, edges[3] : edges[4]],
            mixer_in[:, edges[2] : edges[3]],
        ],
        axis=1,
    )
    in_mix = jnp.pad(in_mix, ((0, 0), (0, -in_mix.shape[1] % NS)))
    in_mid = jnp.concatenate([in_z, mixer_out.T], axis=1)
    in_feed = jnp.concatenate([gate_up, down_weight.T], axis=1)
    mix_blocks = gather_ctx(in_mix)
    mix_parts = gather_inner(gather_first(mix_blocks))
    mix_others = gather_last(mix_parts)
    mid_blocks = gather_ctx(after(in_mid, mix_blocks[-1]), mix_parts)
    mid_first = gather_first(after(mid_blocks, mix_others))
    feed_blocks = gather_ctx(after(in_feed, mid_blocks[1:3]), mid_first)
    mix_pieces = gather_core(mix_parts, mix_others)
    order = width_order(width)
    turn = (jnp.arange(width)[:, None] == order[None, :]).astype(jnp.bfloat16)
    hidden_in, cotangent = (
        jnp.dot(v, turn, preferred_element_type=jnp.float32).astype(jnp.bfloat16)
        for v in (hidden_in, cotangent)
    )
    gains = jnp.dot(
        jnp.stack([norm_gain, feed_gain]),
        turn.astype(jnp.float32),
        precision=lax.Precision.HIGHEST,
    )
    norm_gain, feed_gain = gains[0], gains[1]
    tokens = hidden_in.shape[0]
    piece = lax.axis_index("ctx")
    frequency = ROTARY_BASE ** (jnp.arange(HEAD_SIZE // 2, dtype=jnp.float32) * (-2.0 / HEAD_SIZE))
    token_position = (piece * tokens + jnp.arange(tokens)).astype(jnp.float32)
    angles = frequency[:, None] * token_position[None, :]
    turn_cos, turn_sin = jnp.cos(angles), jnp.sin(angles)
    segment_float = segments.astype(jnp.float32)
    row, column = segment_float[None, :], segment_float[:, None]
    place = piece.astype(jnp.int32)[None]
    spread = spread_heads()
    bias, decay = (jnp.pad(v, (0, NS - SH))[None] for v in (step_bias, decay_log))
    skip = jnp.repeat(skip_gain, SP)[None]
    normed, project, queries, packed = project_in(
        after(hidden_in, mid_first, feed_blocks[1:3]),
        norm_gain,
        turn_cos,
        turn_sin,
        jnp.pad(row, ((0, 0), (0, 2 * KEY_WIDTH - tokens))),
        mix_pieces,
    )
    mid_parts = gather_inner(mid_first, project)
    mid_others = gather_last(mid_parts)
    blocks = gather_ctx(packed)
    feed_first = gather_first(after(feed_blocks, project))
    own, states, running = state_forward(
        after(project, mid_parts, feed_first), bias, decay, skip, spread, column, row
    )
    feed_parts = gather_inner(feed_first, own)
    attended, total, flags = attend(place, after(queries, feed_parts, mid_others), row, blocks)
    near, both = entering_near(states, flags, False)
    feed_others = gather_last(feed_parts)
    mid_pieces = gather_core(mid_parts, mid_others)
    feed_pieces = gather_core(feed_parts, feed_others)
    far = entering_far(both, flags, False)
    (
        layer_out,
        normed_two,
        feed_columns,
        grad_mix,
        mid_columns,
        grad_residual,
        grad_y,
        grad_att,
        grad_normed_part,
        grad_feed_gain,
        pulled,
        entered,
        carried,
    ) = middle(
        flags,
        hidden_in,
        normed,
        cotangent,
        own,
        project,
        near,
        far,
        running,
        column,
        spread,
        attended,
        feed_gain,
        mid_pieces,
        feed_pieces,
    )
    feed_args = (normed_two, cotangent, feed_columns, 2 * FF)
    mid_args = (normed, grad_mix, mid_columns, mixer_width)
    whole = jnp.ones((8, NS), jnp.float32)
    mid_sent = weight_half(*mid_args, 1, 512)
    mid_arrived = swap(mid_sent, 1)
    feed_sent = weight_half(*after(feed_args[:3], mid_sent), feed_args[3], 1, 2048)
    feed_arrived = swap(feed_sent, 1)
    near, both = entering_near(pulled, after(whole, feed_sent), True)
    grad_query, *grad_blocks = attend_back(
        place, queries, row, after(grad_att, feed_sent, both), total, turn_cos, turn_sin, blocks
    )
    far = entering_far(both, whole, True)
    mid_go = weight_sum(*after(mid_args[:3], grad_blocks), mid_args[3], mid_arrived, 512)
    feed_go = weight_sum(*after(feed_args[:3], mid_go), feed_args[3], feed_arrived, 2048)
    grad_keys = scatter_ctx(grad_blocks, mid_go, feed_go)
    grad_project, small = state_back(
        project,
        bias,
        decay,
        skip,
        spread,
        column,
        row,
        after(grad_y, feed_go),
        carried,
        entered,
        near,
        far,
        grad_query,
        grad_keys,
        turn_cos,
        turn_sin,
    )
    mid_go = next_go(*mid_go, grad_project)
    mix_args = (normed, normed, after(grad_project, mid_go[1]))
    mix_sent = weight_half(*mix_args, grad_project.shape[1], 1, 896)
    mix_arrived = swap(mix_sent, 1)
    feed_go = next_go(*feed_go, mix_sent)
    mid_near = scatter_near(*mid_go, feed_go[1])
    mix_go = weight_sum(
        *after(mix_args, feed_go[1], mid_near[2]), grad_project.shape[1], mix_arrived, 896
    )
    grad_hidden, grad_norm_gain = project_back(
        hidden_in, norm_gain, after(grad_project, mix_go), grad_normed_part, grad_residual, mix_pieces
    )
    mid_far = scatter_far(*mid_near, grad_hidden)
    gain_grads = jnp.dot(
        jnp.concatenate([grad_norm_gain, grad_feed_gain]),
        turn.T.astype(jnp.float32),
        precision=lax.Precision.HIGHEST,
    )
    packed = jnp.concatenate([gain_grads.reshape(-1, NS), small], axis=0)
    steps = total_steps()
    along = len(chip_masks()[0]) + 1
    packed = total_step(after(packed, mid_far[1]), *steps[0])
    feed_near = scatter_near(*feed_go, packed)
    mix_go = next_go(*mix_go, feed_near[2])
    feed_far = scatter_far(*feed_near, mix_go[1])
    mix_near = scatter_near(*mix_go, feed_far[1])
    packed = after(packed, mix_near[2])
    for step in steps[1:along]:
        packed = total_step(packed, *step)
    mix_far = scatter_far(*mix_near, packed)
    packed = after(packed, mix_far[1])
    for step in steps[along:]:
        packed = total_step(packed, *step)
    owned_mid, owned_feed, owned_mix = (scatter_end(*v) for v in (mid_far, feed_far, mix_far))
    small, total_gain = packed[-small.shape[0] :], packed[: -small.shape[0]].reshape(2, width)
    total_norm, total_feed = total_gain[0], total_gain[1]
    total_bias, total_decay, total_skip = (small[i, :SH] for i in range(3))
    mix_edge = mixer_width + 2 * NS
    token_offset = grad_project.shape[1] - NS
    owned_in = jnp.concatenate(
        [
            owned_mid[:, :mixer_width],
            owned_mix[:, :mix_edge],
            owned_mix[:, token_offset : token_offset + SH],
            owned_mix[:, mix_edge:token_offset],
        ],
        axis=1,
    )
    owned_out = owned_mid[:, mixer_width:]
    layer_out, grad_hidden = (
        jnp.dot(v.astype(jnp.bfloat16), turn.T, preferred_element_type=jnp.float32).astype(
            jnp.bfloat16
        )
        for v in (layer_out, grad_hidden)
    )
    return (
        layer_out,
        grad_hidden,
        owned_in,
        owned_out.T,
        owned_feed[:, : 2 * FF],
        owned_feed[:, 2 * FF :].T,
        total_norm,
        total_feed,
        total_bias,
        total_decay,
        total_skip,
    )


def solution(mesh):
    return jax.shard_map(
        local,
        mesh=mesh,
        in_specs=(
            P(("fsdp", "ctx"), None),
            P(("fsdp", "ctx")),
            P(("fsdp", "ctx"), None),
            P(("fsdp", "ctx"), None),
            P(None, ("fsdp", "ctx")),
            P(("fsdp", "ctx"), None),
            P(None, ("fsdp", "ctx")),
            P(),
            P(),
            P(),
            P(),
            P(),
        ),
        out_specs=(
            P(("fsdp", "ctx"), None),
            P(("fsdp", "ctx"), None),
            P(("fsdp", "ctx"), None),
            P(None, ("fsdp", "ctx")),
            P(("fsdp", "ctx"), None),
            P(None, ("fsdp", "ctx")),
            P(),
            P(),
            P(),
            P(),
            P(),
        ),
        check_vma=False,
    )
```

```python
import jax
import jax.numpy as jnp
from jax import lax
from jax.experimental import pallas as pl
from jax.experimental.pallas import tpu as pltpu
from jax.sharding import PartitionSpec as P

FF = 2048
SH = 24
SP = 64
NS = 128
QUERY_HEADS = 8
KEY_VALUE_HEADS = 2
HEAD_SIZE = 64
KEY_WIDTH = KEY_VALUE_HEADS * HEAD_SIZE
REPEAT = QUERY_HEADS // KEY_VALUE_HEADS


EPSILON = 1e-06
ROTARY_BASE = 100000000000.0


def swap(value, mask):
    size = lax.axis_size("fsdp")
    return lax.ppermute(value, "fsdp", [(i, i ^ mask) for i in range(size)])


def swap_ctx(value, mask):
    size = lax.axis_size("ctx")
    return lax.ppermute(value, "ctx", [(i, i ^ mask) for i in range(size)])


def after(value, *others):
    return lax.optimization_barrier((value, others))[0]


def chip_masks():
    bits = lax.axis_size("fsdp").bit_length() - 2
    masks = [2 << i for i in range(bits)]
    x_masks, y_masks = masks[: bits // 2], masks[bits // 2 :]
    return (y_masks + x_masks, x_masks + y_masks)


def gather_first(blocks):
    half = len(blocks) // 2
    return [jnp.concatenate(blocks[:half], axis=0), jnp.concatenate(blocks[half:], axis=0)]


def gather_inner(parts, *hold):
    out = []
    for part, masks in zip(parts, chip_masks()):
        for mask in masks[:-1]:
            part = jnp.concatenate([part, after(swap(part, mask), *hold)], axis=0)
        out.append(part)
    return out


def gather_last(parts):
    return [swap(part, masks[-1]) for part, masks in zip(parts, chip_masks())]


def gather_core(parts, others):
    pieces = []
    for own in zip(parts, others):
        pieces += list(own) + [swap(piece, 1) for piece in own]
    return pieces


def piece_rows(width):
    devices = lax.axis_size("fsdp")
    block = width // (2 * devices)
    runs = []
    for half, masks in enumerate(chip_masks()):
        for core in (0, 1):
            for last in (0, 1):
                piece = half * 4 + core * 2 + last
                for inner in range(devices // 4):
                    chip = last * masks[-1]
                    for i, mask in enumerate(masks[:-1]):
                        chip += ((inner >> i) & 1) * mask
                    start = core * (width // 2) + half * (width // 4) + (chip >> 1) * block
                    runs.append((piece, inner * block, start, block))
    return runs


def plus(left, right):
    return (left.astype(jnp.float32) + right.astype(jnp.float32)).astype(jnp.bfloat16)


def total(values):
    result = values[0].astype(jnp.float32)
    for value in values[1:]:
        result = result + value.astype(jnp.float32)
    return result


def split_next(parts, stage):
    stay, go = [], []
    for terms, masks in zip(parts, chip_masks()):
        order = masks[::-1]
        axis = sorted(order[stage:], reverse=True).index(order[stage])
        stay.append([lax.index_in_dim(v, 0, axis, keepdims=False) for v in terms])
        go.append(
            total([lax.index_in_dim(v, 1, axis, keepdims=False) for v in terms]).astype(jnp.bfloat16)
        )
    return stay, go


def arrive(stay, go, stage, *hold):
    return [
        terms + [after(swap(value, masks[::-1][stage]), *hold)]
        for terms, value, masks in zip(stay, go, chip_masks())
    ]


def next_go(stay, go, *hold):
    parts = arrive(stay, go, 0, *hold)
    last = len(chip_masks()[0]) - 1
    for stage in range(1, last):
        stay, go = split_next(parts, stage)
        parts = arrive(stay, go, stage)
    return split_next(parts, last)


def low_total(terms):
    return total(terms).astype(jnp.bfloat16)


def scatter_near(stay, go, hold):
    pieces = lax.axis_size("ctx")
    blocks = []
    for terms in arrive(stay, go, len(chip_masks()[0]) - 1, hold):
        rows = terms[0].shape[0] // (pieces // 2)
        blocks += [[v[j * rows : (j + 1) * rows] for v in terms] for j in range(pieces // 2)]
    size = pieces
    while size > 4:
        size //= 2
        blocks = [blocks[j] + [swap_ctx(low_total(blocks[j + size]), size)] for j in range(size)]
    return blocks[0], blocks[2], [low_total(blocks[1]), low_total(blocks[3])]


def scatter_far(stay, through, go, *hold):
    one, far = after([swap_ctx(v, 1) for v in go], *hold)
    return stay + [one], low_total(through + [far])


def scatter_end(stay, two):
    return total(stay + [swap_ctx(two, 2)])


NT = (((1,), (1,)), ((), ()))
TN = (((0,), (0,)), ((), ()))
VMEM_BYTES = 58 * 1024 * 1024


def cost(microseconds):
    return pl.CostEstimate(
        flops=int(microseconds * 1e9), bytes_accessed=int(microseconds * 3e6), transcendentals=0
    )


def params():
    return pltpu.CompilerParams(vmem_limit_bytes=VMEM_BYTES)


def weight_kernel(edge, rows_one, rows_two, columns, out, turned):
    step = pl.program_id(0)

    @pl.when(step == 0)
    def _():
        turned[...] = rows_one[...].T

    @pl.when(step == edge)
    def _():
        turned[...] = rows_two[...].T

    out[...] = dot(turned[...], columns[...]).astype(jnp.bfloat16)


def weight_half(rows_one, rows_two, columns, edge, half, tile=512):
    tokens, width = rows_one.shape
    half_rows = pl.BlockSpec((tokens, width // 2), lambda j: (0, half))
    count = columns.shape[1]
    return pl.pallas_call(
        lambda *refs: weight_kernel(edge // tile, *refs),
        grid=(count // tile,),
        in_specs=[half_rows, half_rows, pl.BlockSpec((tokens, tile), lambda j: (0, j))],
        out_specs=pl.BlockSpec((width // 2, tile), lambda j: (0, j)),
        out_shape=jax.ShapeDtypeStruct((width // 2, count), jnp.bfloat16),
        scratch_shapes=[pltpu.VMEM((width // 2, tokens), jnp.bfloat16)],
        compiler_params=params(),
        name="weight_grad",
        cost_estimate=cost(0),
    )(rows_one, rows_two, columns)


def sum_rows(width):
    devices = lax.axis_size("fsdp")
    block = width // (2 * devices)
    runs = []
    for half, masks in enumerate(chip_masks()):
        bit = masks[-1] >> 1
        for value in (0, bit):
            chips = [c for c in range(devices // 2) if c & bit == value]
            runs.append([half * (width // 4) + c * block for c in chips])
    return runs, block


def weight_sum_kernel(edge, runs, block, rows_one, rows_two, columns, arrived, *refs):
    out, turned = refs[:4], refs[4]
    step = pl.program_id(0)

    @pl.when(step == 0)
    def _():
        turned[...] = rows_one[...].T

    @pl.when(step == edge)
    def _():
        turned[...] = rows_two[...].T

    value = dot(turned[...], columns[...]) + arrived[...].astype(jnp.float32)
    value = value.astype(jnp.bfloat16)
    for ref, starts in zip(out, runs):
        for i, start in enumerate(starts):
            ref[i * block : (i + 1) * block, :] = value[start : start + block]


def weight_sum(rows_one, rows_two, columns, edge, arrived, tile):
    tokens, width = rows_one.shape
    half_rows = pl.BlockSpec((tokens, width // 2), lambda j: (0, 0))
    count = columns.shape[1]
    runs, block = sum_rows(width)
    results = pl.pallas_call(
        lambda *refs: weight_sum_kernel(edge // tile, runs, block, *refs),
        grid=(count // tile,),
        in_specs=[
            half_rows,
            half_rows,
            pl.BlockSpec((tokens, tile), lambda j: (0, j)),
            pl.BlockSpec((width // 2, tile), lambda j: (0, j)),
        ],
        out_specs=[pl.BlockSpec((width // 8, tile), lambda j: (0, j))] * 4,
        out_shape=[jax.ShapeDtypeStruct((width // 8, count), jnp.bfloat16)] * 4,
        scratch_shapes=[pltpu.VMEM((width // 2, tokens), jnp.bfloat16)],
        compiler_params=params(),
        name="weight_sum",
        cost_estimate=cost(0),
    )(rows_one, rows_two, columns, arrived)
    shape = [2] * (len(chip_masks()[0]) - 1) + [block, count]
    stay_a, go_a, stay_b, go_b = (v.reshape(shape) for v in results)
    return [[stay_a], [stay_b]], [go_a, go_b]


def fetch(pieces, whole, semaphore, runs, start, stop):
    for piece, source, target, count in runs:
        pltpu.make_async_copy(
            pieces[piece].at[pl.ds(source, count), start:stop],
            whole.at[pl.ds(target, count), start:stop],
            semaphore,
        ).start()


def fetched(whole, semaphore, start, stop):
    view = whole.at[:, start:stop]
    pltpu.make_async_copy(view, view, semaphore).wait()


def dot(left, right):
    return jnp.dot(left, right, preferred_element_type=jnp.float32)


def dot_nt(left, right):
    return lax.dot_general(left, right, NT, preferred_element_type=jnp.float32)


def tiles(total, tile, body):
    for start in range(0, total, tile):
        body(slice(start, start + tile))


def looped(total, tile, body):
    @pl.loop(0, total // tile)
    def _(i):
        body(pl.ds(pl.multiple_of(i * tile, tile), tile))


def project_kernel(runs, hidden, gain, turn_cos, turn_sin, segment_row, *refs):
    pieces, refs = refs[:8], refs[8:]
    normed, project, queries, packed, whole, semaphore = refs
    columns, tokens = whole.shape[1], hidden.shape[0]
    fetch(pieces, whole, semaphore, runs, 0, columns)
    h = hidden[...].astype(jnp.float32)
    inverse = lax.rsqrt(jnp.mean(h * h, axis=-1, keepdims=True) + EPSILON)
    normed[...] = (h * inverse * gain[...]).astype(jnp.bfloat16)
    fetched(whole, semaphore, 0, columns)

    def body(at):
        project[:, at] = dot(normed[...], whole[:, at])

    tiles(columns, 384, body)
    start = SH * SP + 2 * NS
    turned = project[:, start : start + QUERY_HEADS * HEAD_SIZE].T
    queries[...] = (rotate(turned, turn_cos, turn_sin) * HEAD_SIZE ** (-0.5)).astype(jnp.bfloat16)
    start = start + QUERY_HEADS * HEAD_SIZE
    keys = rotate(project[:, start : start + KEY_WIDTH].T, turn_cos, turn_sin)
    packed[:tokens, :KEY_WIDTH] = keys.T.astype(jnp.bfloat16)
    start = start + KEY_WIDTH
    packed[:tokens, KEY_WIDTH:] = project[:, start : start + KEY_WIDTH].astype(jnp.bfloat16)
    packed[tokens:, :] = jnp.broadcast_to(segment_row[...], (16, 2 * KEY_WIDTH)).astype(jnp.bfloat16)


def rotate(turned, turn_cos, turn_sin, sign=1.0):
    half = HEAD_SIZE // 2
    c, s = turn_cos[...], turn_sin[...] * sign
    out = []
    for start in range(0, turned.shape[0], HEAD_SIZE):
        first, second = turned[start : start + half], turned[start + half : start + HEAD_SIZE]
        out += [first * c - second * s, second * c + first * s]
    return jnp.concatenate(out, axis=0)


def full_specs(count):
    return [pl.BlockSpec(memory_space=pltpu.VMEM)] * count


def any_specs(count):
    return [pl.BlockSpec(memory_space=pl.ANY)] * count


def project_in(hidden, gain, turn_cos, turn_sin, segment_row, pieces):
    tokens, width = hidden.shape
    columns = pieces[0].shape[1]
    runs = piece_rows(width)
    return pl.pallas_call(
        lambda *refs: project_kernel(runs, *refs),
        in_specs=full_specs(5) + any_specs(8),
        out_specs=full_specs(4),
        out_shape=[
            jax.ShapeDtypeStruct((tokens, width), jnp.bfloat16),
            jax.ShapeDtypeStruct((tokens, columns), jnp.float32),
            jax.ShapeDtypeStruct((QUERY_HEADS * HEAD_SIZE, tokens), jnp.bfloat16),
            jax.ShapeDtypeStruct((tokens + 16, 2 * KEY_WIDTH), jnp.bfloat16),
        ],
        scratch_shapes=[pltpu.VMEM((width, columns), jnp.bfloat16), pltpu.SemaphoreType.DMA],
        compiler_params=params(),
        name="project_in",
        cost_estimate=cost(0),
    )(hidden, gain[None], turn_cos, turn_sin, segment_row, *pieces)


def spread_heads():
    head = lax.broadcasted_iota(jnp.int32, (NS, SH * SP), 1) // SP
    return (lax.broadcasted_iota(jnp.int32, (NS, SH * SP), 0) == head).astype(jnp.float32)


def dot_exact(left, right):
    return jnp.dot(
        left, right, precision=lax.Precision.HIGHEST, preferred_element_type=jnp.float32
    )


def step_terms(project, bias, decay):
    tokens = project.shape[0]
    raw = project[:, project.shape[1] - NS :] + bias[...]
    step = jnp.maximum(raw, 0.0) + jnp.log1p(jnp.exp(-jnp.abs(raw)))
    rate = -jnp.exp(decay[...]) * step
    rows = lax.broadcasted_iota(jnp.int32, (tokens, tokens), 0)
    columns = lax.broadcasted_iota(jnp.int32, (tokens, tokens), 1)
    running = dot_exact((rows >= columns).astype(jnp.float32), rate)
    return raw, step, rate, running


def tail_terms(running, segment_column):
    tokens = running.shape[0]
    same = segment_column[...] == segment_column[tokens - 1 :, :]
    return jnp.where(same, jnp.exp(running[tokens - 1 :, :] - running), 0.0)


def split_low(values):
    high = values.astype(jnp.bfloat16)
    return high, (values - high.astype(jnp.float32)).astype(jnp.bfloat16)


def twice(values):
    return jnp.concatenate([values, values], axis=0)


def state_kernel(project, bias, decay, skip, spread, column, row, own, packed, running_out, bias_sum, turned):
    tokens, inner = own.shape
    _, step, _, running = step_terms(project, bias, decay)
    running_out[...] = running
    tail = tail_terms(running, column) * step
    tail = dot_exact(tail, spread[...])
    values = project[:, :inner]
    states = dot(project[:, inner : inner + NS].T.astype(jnp.bfloat16), (tail * values).astype(jnp.bfloat16))
    packed[:NS, :] = states.astype(jnp.bfloat16)
    last = dot_exact(jnp.broadcast_to(jnp.exp(running[tokens - 1 :, :]), (8, NS)), spread[...])
    packed[NS:, :] = jnp.concatenate([last, last], axis=0).astype(jnp.bfloat16)
    at_row = lax.broadcasted_iota(jnp.int32, (tokens, tokens), 0)
    at_column = lax.broadcasted_iota(jnp.int32, (tokens, tokens), 1)
    allowed = (at_row >= at_column) & (column[...] == row[...])
    turned[0] = running.T
    turned[1] = step.T
    bias_sum[...] = jnp.where(allowed, 0.0, -1e30)
    match = lax.dot_general(
        project[:, inner + NS : inner + 2 * NS],
        project[:, inner : inner + NS],
        NT,
        precision=lax.Precision.HIGHEST,
        preferred_element_type=jnp.float32,
    )
    lane = lax.broadcasted_iota(jnp.int32, (tokens, NS), 1)

    for pair in range(SH // 2):
        at = slice(pair * NS, (pair + 1) * NS)
        values = project[:, at]
        parts = []
        for k in (0, 1):
            head = 2 * pair + k
            gap = running_out[:, head : head + 1] - turned[0, slice(head, head + 1), :]
            weight = jnp.exp(jnp.minimum(gap, 0.0) + bias_sum[...])
            weight = weight * match * turned[1, slice(head, head + 1), :]
            parts.append(dot(weight.astype(jnp.bfloat16), values.astype(jnp.bfloat16)))
        own[:, at] = jnp.where(lane < SP, parts[0], parts[1]) + skip[:, at] * values


def state_forward(project, bias, decay, skip, spread, column, row):
    tokens, inner = project.shape[0], SH * SP
    return pl.pallas_call(
        state_kernel,
        in_specs=full_specs(7),
        out_specs=full_specs(3),
        out_shape=[
            jax.ShapeDtypeStruct((tokens, inner), jnp.float32),
            jax.ShapeDtypeStruct((NS + 16, inner), jnp.bfloat16),
            jax.ShapeDtypeStruct((tokens, NS), jnp.float32),
        ],
        scratch_shapes=[
            pltpu.VMEM((tokens, tokens), jnp.float32),
            pltpu.VMEM((2, NS, tokens), jnp.float32),
        ],
        compiler_params=params(),
        name="state_forward",
        cost_estimate=cost(0),
    )(project, bias, decay, skip, spread, column, row)


def key_masks(place, row, blocks, masks):
    tokens = row.shape[1]
    key = lax.broadcasted_iota(jnp.int32, (tokens, tokens), 0)
    query = lax.broadcasted_iota(jnp.int32, (tokens, tokens), 1)
    for j, block in enumerate(blocks):
        label = block[tokens : tokens + 16, :tokens].astype(jnp.float32).T[:, :1]
        ahead = ((place[0] ^ j) - place[0]) * tokens
        allowed = (key + ahead <= query) & (label == row[...])
        masks[j] = jnp.where(allowed, 0.0, -1e30)


def attend_kernel(count, place, queries, row, *refs):
    blocks, refs = refs[:count], refs[count:]
    attended, total, flags, masks, scores, turned, values = refs
    tokens = row.shape[1]
    ends = [block[tokens : tokens + 16, tokens - 1 : tokens].astype(jnp.float32)[:8] for block in blocks]

    def end_of(number):
        found = jnp.zeros((8, 1), jnp.float32)
        for j, end in enumerate(ends):
            found = found + jnp.where((place[0] ^ j) == number, end, 0.0)
        return found

    lane = lax.broadcasted_iota(jnp.int32, (8, NS), 1)
    known = jnp.where(lane == NS - 1, jnp.where(place[0] > 0, end_of(place[0] - 1), -1.0), 0.0)
    for k in range(count):
        same = (end_of(place[0] - k) == end_of(place[0] - k - 1)) & (place[0] > k)
        known = known + jnp.where((lane == k) & same, 1.0, 0.0)
    flags[...] = known
    key_masks(place, row, blocks, masks)
    for j, block in enumerate(blocks):
        values[j] = block[:tokens, KEY_WIDTH:].T
    for group in range(KEY_VALUE_HEADS):
        lanes = slice(group * HEAD_SIZE, (group + 1) * HEAD_SIZE)

        for r in range(REPEAT):
            head = group * REPEAT + r
            at = slice(head * HEAD_SIZE, (head + 1) * HEAD_SIZE)
            highest = None
            for j, block in enumerate(blocks):
                score = dot(block[:tokens, lanes], queries[at, :]) + masks[j]
                scores[j] = score
                top = jnp.max(score, axis=0, keepdims=True)
                highest = top if highest is None else jnp.maximum(highest, top)
            sums = 0.0
            for j in range(count):
                score = jnp.exp(scores[j] - highest)
                scores[j] = score
                sums = sums + jnp.sum(score, axis=0, keepdims=True)
            inverse = 1.0 / sums
            result = 0.0
            for j in range(count):
                result = result + dot(values[j, lanes, :], (scores[j] * inverse).astype(jnp.bfloat16))
            turned[at, :] = result
            total[slice(head, head + 1), :] = highest + jnp.log(sums)

    attended[...] = turned[...].T.astype(jnp.bfloat16)


def attend(place, queries, row, blocks):
    tokens, count = row.shape[1], len(blocks)
    return pl.pallas_call(
        lambda *refs: attend_kernel(count, *refs),
        in_specs=[pl.BlockSpec(memory_space=pltpu.SMEM)] + full_specs(2 + count),
        out_specs=full_specs(3),
        out_shape=[
            jax.ShapeDtypeStruct((tokens, QUERY_HEADS * HEAD_SIZE), jnp.bfloat16),
            jax.ShapeDtypeStruct((QUERY_HEADS, tokens), jnp.float32),
            jax.ShapeDtypeStruct((8, NS), jnp.float32),
        ],
        scratch_shapes=[
            pltpu.VMEM((count, tokens, tokens), jnp.float32),
            pltpu.VMEM((count, tokens, tokens), jnp.float32),
            pltpu.VMEM((QUERY_HEADS * HEAD_SIZE, tokens), jnp.float32),
            pltpu.VMEM((count, KEY_WIDTH, tokens), jnp.bfloat16),
        ],
        compiler_params=params(),
        name="attend",
        cost_estimate=cost(0),
    )(place, queries, row, *blocks)


def attend_back_kernel(count, place, queries, row, grad_att, total, turn_cos, turn_sin, *refs):
    blocks, refs = refs[:count], refs[count:]
    grad_query, grad_blocks, refs = refs[0], refs[1 : 1 + count], refs[1 + count :]
    masks, chances, slopes, turned_keys, turned_grad, grad_turned, key_sums, value_sums = refs
    tokens = row.shape[1]
    key_masks(place, row, blocks, masks)
    turned_grad[...] = grad_att[...].T
    for j, block in enumerate(blocks):
        turned_keys[j] = block[:tokens, :KEY_WIDTH].T
    for group in range(KEY_VALUE_HEADS):
        lanes = slice(group * HEAD_SIZE, (group + 1) * HEAD_SIZE)
        ahead = slice(KEY_WIDTH + group * HEAD_SIZE, KEY_WIDTH + (group + 1) * HEAD_SIZE)
        key_sums[...] = jnp.zeros_like(key_sums)
        value_sums[...] = jnp.zeros_like(value_sums)

        for r in range(REPEAT):
            head = group * REPEAT + r
            at = slice(head * HEAD_SIZE, (head + 1) * HEAD_SIZE)
            query, grad = queries[at, :], turned_grad[at, :]
            query_rows, grad_rows = query.T, grad.T
            inside = 0.0
            for j, block in enumerate(blocks):
                score = dot(block[:tokens, lanes], query) + masks[j]
                chance = jnp.exp(score - total[slice(head, head + 1), :])
                slope = dot(block[:tokens, ahead], grad)
                chances[j], slopes[j] = chance, slope
                inside = inside + jnp.sum(chance * slope, axis=0, keepdims=True)
                value_sums[j] = value_sums[j] + dot(chance.astype(jnp.bfloat16), grad_rows)
            result = 0.0
            for j in range(count):
                slope = (chances[j] * (slopes[j] - inside)).astype(jnp.bfloat16)
                key_sums[j] = key_sums[j] + dot(slope, query_rows)
                result = result + dot(turned_keys[j, lanes, :], slope)
            grad_turned[at, :] = result

        for j in range(count):
            grad_blocks[j][:, lanes] = key_sums[j].astype(jnp.bfloat16)
            grad_blocks[j][:, ahead] = value_sums[j].astype(jnp.bfloat16)
    turned = rotate(grad_turned[...], turn_cos, turn_sin, -1.0) * HEAD_SIZE ** (-0.5)
    grad_query[...] = turned.T.astype(jnp.bfloat16)


def attend_back(place, queries, row, grad_att, total, turn_cos, turn_sin, blocks):
    tokens, count = row.shape[1], len(blocks)
    square = pltpu.VMEM((count, tokens, tokens), jnp.float32)
    heads = QUERY_HEADS * HEAD_SIZE
    return pl.pallas_call(
        lambda *refs: attend_back_kernel(count, *refs),
        in_specs=[pl.BlockSpec(memory_space=pltpu.SMEM)] + full_specs(6 + count),
        out_specs=full_specs(1 + count),
        out_shape=[jax.ShapeDtypeStruct((tokens, heads), jnp.bfloat16)]
        + [jax.ShapeDtypeStruct((tokens, 2 * KEY_WIDTH), jnp.bfloat16)] * count,
        scratch_shapes=[
            square,
            square,
            square,
            pltpu.VMEM((count, KEY_WIDTH, tokens), jnp.bfloat16),
            pltpu.VMEM((heads, tokens), jnp.bfloat16),
            pltpu.VMEM((heads, tokens), jnp.float32),
            pltpu.VMEM((count, tokens, HEAD_SIZE), jnp.float32),
            pltpu.VMEM((count, tokens, HEAD_SIZE), jnp.float32),
        ],
        compiler_params=params(),
        name="attend_back",
        cost_estimate=cost(60),
    )(place, queries, row, grad_att, total, turn_cos, turn_sin, *blocks)


def state_back_kernel(
    project, bias, decay, skip, spread, column, row, grad_y, carried, entered, near, far,
    grad_query, grad_keys, turn_cos, turn_sin,
    grad_project, small, grad_state, bias_sum, turned, match_grad, column_sums, row_sums, running_keep, step_keep,
):
    tokens, inner = grad_y.shape
    raw, step, rate, running = step_terms(project, bias, decay)
    running_keep[...], step_keep[...] = running, step
    grad_state[...] = entered_state(jnp.ones((8, NS), jnp.float32), near, far)
    decayed = tail_terms(running, column)
    tail = decayed * step
    turned[...] = running.T
    values_b = project[:, inner : inner + NS]
    values_c = project[:, inner + NS : inner + 2 * NS]
    low_b, low_c = values_b.astype(jnp.bfloat16), values_c.astype(jnp.bfloat16)
    both_b = jnp.concatenate(split_low(values_b), axis=1)
    both_c = jnp.concatenate(split_low(values_c), axis=1)
    key = lax.broadcasted_iota(jnp.int32, (tokens, tokens), 0)
    query = lax.broadcasted_iota(jnp.int32, (tokens, tokens), 1)
    bias_sum[...] = jnp.where((query >= key) & (column[...] == row[...]), 0.0, -1e30)
    match = lax.dot_general(
        values_b, values_c, NT, precision=lax.Precision.HIGHEST, preferred_element_type=jnp.float32
    )
    match_grad[...] = jnp.zeros_like(match_grad)
    column_sums[...] = jnp.zeros_like(column_sums)
    row_sums[...] = jnp.zeros_like(row_sums)
    lane = lax.broadcasted_iota(jnp.int32, (tokens, NS), 1)

    for pair in range(SH // 2):
        at = slice(pair * NS, (pair + 1) * NS)
        low, rest = split_low(project[:, at])
        low_grad, rest_grad = split_low(grad_y[:, at])
        turned_grad, turned_rest = low_grad.T, rest_grad.T
        parts = []
        for k in (0, 1):
            head = 2 * pair + k
            rows = slice(k * SP, (k + 1) * SP)
            gap = turned[slice(head, head + 1), :] - running_keep[:, head : head + 1]
            weight = jnp.exp(jnp.minimum(gap, 0.0) + bias_sum[...])
            step_column = step_keep[:, head : head + 1]
            slope = dot(
                jnp.concatenate([low[:, rows], rest[:, rows], low[:, rows]], axis=1),
                jnp.concatenate([turned_grad[rows], turned_grad[rows], turned_rest[rows]], axis=0),
            )
            slope = slope * weight
            scaled = slope * step_column
            match_grad[...] = match_grad[...] + scaled
            row_sums[slice(head, head + 1), :] = jnp.sum(scaled * match, axis=0, keepdims=True)
            sums = jnp.sum(slope * match, axis=1, keepdims=True)
            column_sums[...] = column_sums[...] + jnp.where(lane == head, sums, 0.0)
            weight = weight * match * step_column
            parts.append(dot(weight.astype(jnp.bfloat16), low_grad))
        grad_x = jnp.where(lane < SP, parts[0], parts[1]) + skip[:, at] * grad_y[:, at]
        tail_wide = dot_exact(tail, spread[:, at])
        grad_x = grad_x + tail_wide * dot(low_b, grad_state[:, at])
        grad_project[:, at] = grad_x.astype(jnp.bfloat16)

    x, grad = project[:, :inner], grad_y[...]
    carried_wide = dot_exact(carried[...], spread[...])
    tail_wide = dot_exact(tail, spread[...])
    out_b = dot_nt((tail_wide * x).astype(jnp.bfloat16), grad_state[...])
    out_c = dot_nt((carried_wide * grad).astype(jnp.bfloat16), entered[...])
    low_match = match_grad[...].astype(jnp.bfloat16)
    out_b = out_b + dot(low_match, low_c)
    out_c = out_c + dot(match_grad[...].T.astype(jnp.bfloat16), low_b)
    grad_project[:, inner : inner + NS] = out_b.astype(jnp.bfloat16)
    grad_project[:, inner + NS : inner + 2 * NS] = out_c.astype(jnp.bfloat16)

    def per_head(wide):
        return lax.dot_general(
            wide, spread[...], NT, precision=lax.Precision.HIGHEST, preferred_element_type=jnp.float32
        )

    grad_tail = per_head(x * dot(both_b, twice(grad_state[...])))
    grad_carried = per_head(grad * dot(both_c, twice(entered[...])))
    kept = jnp.sum(grad_state[...].astype(jnp.float32) * entered[...].astype(jnp.float32), axis=0, keepdims=True)
    kept = per_head(jnp.broadcast_to(kept, (8, inner)))[:1]
    at_token = lax.broadcasted_iota(jnp.int32, (tokens, NS), 0)
    grad_carried = grad_carried + jnp.where(at_token == tokens - 1, kept, 0.0)
    grad_step = column_sums[...] + grad_tail * decayed
    through = grad_tail * tail
    grad_running = row_sums[...].T - step * column_sums[...] + grad_carried * carried[...] - through
    through = jnp.sum(through, axis=0, keepdims=True)
    grad_running = grad_running + jnp.where(at_token == tokens - 1, through, 0.0)
    grad_rate = dot_exact((query >= key).astype(jnp.float32), grad_running)
    grad_step = grad_step - grad_rate * jnp.exp(decay[...])
    grad_raw = grad_step * jax.nn.sigmoid(raw)
    grad_raw = jnp.where(lane < SH, grad_raw, 0.0)
    grad_skip = per_head(jnp.broadcast_to(jnp.sum(grad * x, axis=0, keepdims=True), (8, inner)))[:1]
    small[0:1, :] = jnp.sum(grad_raw, axis=0, keepdims=True)
    small[1:2, :] = jnp.sum(grad_rate * rate, axis=0, keepdims=True)
    small[2:3, :] = grad_skip
    small[3:, :] = jnp.zeros((5, NS), jnp.float32)
    start = inner + 2 * NS
    heads = QUERY_HEADS * HEAD_SIZE
    grad_project[:, start : start + heads] = grad_query[...]
    start = start + heads
    turned_key = rotate(grad_keys[:, :KEY_WIDTH].T, turn_cos, turn_sin, -1.0)
    grad_project[:, start : start + KEY_WIDTH] = turned_key.T.astype(jnp.bfloat16)
    start = start + KEY_WIDTH
    grad_project[:, start : start + KEY_WIDTH] = grad_keys[:, KEY_WIDTH:].astype(jnp.bfloat16)
    grad_project[:, start + KEY_WIDTH :] = grad_raw.astype(jnp.bfloat16)


def state_back(project, *others):
    tokens, inner = project.shape[0], SH * SP
    square = pltpu.VMEM((tokens, tokens), jnp.float32)
    narrow = pltpu.VMEM((tokens, NS), jnp.float32)
    return pl.pallas_call(
        state_back_kernel,
        in_specs=full_specs(1 + len(others)),
        out_specs=full_specs(2),
        out_shape=[
            jax.ShapeDtypeStruct(project.shape, jnp.bfloat16),
            jax.ShapeDtypeStruct((8, NS), jnp.float32),
        ],
        scratch_shapes=[
            pltpu.VMEM((NS, inner), jnp.bfloat16),
            square,
            pltpu.VMEM((NS, tokens), jnp.float32),
            square,
            narrow,
            pltpu.VMEM((NS, tokens), jnp.float32),
            narrow,
            narrow,
        ],
        compiler_params=params(),
        name="state_back",
        cost_estimate=cost(60),
    )(project, *others)


def shift_ctx(value, by, reverse):
    size = lax.axis_size("ctx")
    pairs = [(i, i + by) for i in range(size - by)]
    return lax.ppermute(value, "ctx", [(j, i) for i, j in pairs] if reverse else pairs)


def join_kernel(flags, own, near, both):
    keep = own[NS : NS + 1, :].astype(jnp.float32) * flags[0:1, 0:1]
    both[...] = (own[:NS, :].astype(jnp.float32) + keep * near[:NS, :].astype(jnp.float32)).astype(
        jnp.bfloat16
    )


def entering_near(packed, same, reverse):
    near = shift_ctx(packed, 1, reverse)
    if lax.axis_size("ctx") != 4:
        return near, packed
    both = pl.pallas_call(
        join_kernel,
        in_specs=full_specs(3),
        out_specs=full_specs(1)[0],
        out_shape=jax.ShapeDtypeStruct((NS, packed.shape[1]), jnp.bfloat16),
        compiler_params=params(),
        name="join",
        cost_estimate=cost(0),
    )(same, packed, near)
    return near, both


def entering_far(both, same, reverse):
    if lax.axis_size("ctx") == 4:
        return shift_ctx(both, 2, reverse)
    total, decay = 0.0, 1.0
    for shift in range(2, lax.axis_size("ctx")):
        part = shift_ctx(both, shift, reverse).astype(jnp.float32)
        total = total + decay * part[:NS]
        decay = decay * same[0, shift] * part[NS : NS + 1]
    return total.astype(jnp.bfloat16)


def entered_state(flags, near, far):
    keep = near[NS : NS + 1, :].astype(jnp.float32) * flags[0:1, 1:2]
    state = near[:NS, :].astype(jnp.float32) + keep * far[...].astype(jnp.float32)
    return state.astype(jnp.bfloat16)


def project_back_kernel(runs, hidden, gain, grad_project, partial, grad_residual, *refs):
    pieces, (grad_hidden, gain_grad, whole, grad_normed, semaphore) = refs[:8], refs[8:]
    columns = whole.shape[1]
    fetch(pieces, whole, semaphore, runs, 0, columns)
    h = hidden[...].astype(jnp.float32)
    inverse = lax.rsqrt(jnp.mean(h * h, axis=-1, keepdims=True) + EPSILON)
    fetched(whole, semaphore, 0, columns)

    def body(at):
        grad_normed[:, at] = partial[:, at] + dot_nt(grad_project[...], whole[at, :])

    tiles(whole.shape[0], 256, body)
    grad = grad_normed[...]
    gain_grad[...] = jnp.sum(grad * h * inverse, axis=0, keepdims=True)
    scaled = grad * gain[...]
    mean = jnp.mean(scaled * h, axis=-1, keepdims=True)
    grad_hidden[...] = (
        grad_residual[...] + inverse * scaled - h * (inverse * inverse * inverse) * mean
    ).astype(jnp.bfloat16)


def project_back(hidden, gain, grad_project, partial, grad_residual, pieces):
    tokens, width = hidden.shape
    columns = pieces[0].shape[1]
    runs = piece_rows(width)
    return pl.pallas_call(
        lambda *refs: project_back_kernel(runs, *refs),
        in_specs=full_specs(5) + any_specs(8),
        out_specs=full_specs(2),
        out_shape=[
            jax.ShapeDtypeStruct((tokens, width), jnp.bfloat16),
            jax.ShapeDtypeStruct((1, width), jnp.float32),
        ],
        scratch_shapes=[
            pltpu.VMEM((width, columns), jnp.bfloat16),
            pltpu.VMEM((tokens, width), jnp.float32),
            pltpu.SemaphoreType.DMA,
        ],
        compiler_params=params(),
        name="project_back",
        cost_estimate=cost(60),
    )(hidden, gain[None], grad_project, partial, grad_residual, *pieces)


def middle_kernel(
    runs, flags, hidden, normed, cotangent, own, project, near, far, running, column, spread, attended, gain, *refs
):
    mid_pieces, feed_pieces, refs = refs[:8], refs[8:16], refs[16:]
    layer_out, normed_two, feed_columns, grad_mix, mid_columns = refs[:5]
    grad_residual, grad_y, grad_att, grad_normed, gain_grad, pulled, entered, carried = refs[5:13]
    mid, feed, gate_z, ssm_out, gate, up, residual, grad_two, semaphores = refs[13:]
    width, inner = hidden.shape[1], own.shape[1]
    reads = project[:, inner + NS : inner + 2 * NS]
    low_reads = jnp.concatenate(split_low(reads), axis=1)
    turned_reads = reads.T.astype(jnp.bfloat16)
    middle_width = inner + attended.shape[1]
    edges = [0, inner, inner + middle_width]
    hidden_units = feed.shape[1] // 3
    tile, rows = 512, 256
    mid_runs = [(0, edges[1]), (edges[1], edges[2])]
    for i, (start, stop) in enumerate(mid_runs):
        fetch(mid_pieces, mid, semaphores.at[i], runs, start, stop)
    feed_runs = [(0, 2 * hidden_units), (2 * hidden_units, 3 * hidden_units)]
    for i, (start, stop) in enumerate(feed_runs):
        fetch(feed_pieces, feed, semaphores.at[2 + i], runs, start, stop)
    entered[...] = entered_state(flags, near, far)
    carried[...] = jnp.where(column[...] == flags[0:1, NS - 1 : NS], jnp.exp(running[...]), 0.0)

    def shift(at, by):
        return pl.ds(pl.multiple_of(at.start + by, 128), at.size)

    fetched(mid, semaphores.at[0], 0, inner)

    def gating(at):
        z = dot(normed[...], mid[:, at])
        gate_z[:, at] = z
        wide = dot_exact(carried[...], spread[:, at])
        y = own[:, at] + wide * dot(low_reads, twice(entered[:, at]))
        ssm_out[:, at] = y
        gated = y * (z * jax.nn.sigmoid(z))
        mid_columns[:, shift(at, inner)] = gated.astype(jnp.bfloat16)

    looped(inner, tile, gating)
    mid_columns[:, 2 * inner :] = attended[...]
    fetched(mid, semaphores.at[1], inner, edges[2])

    def mixing(at):
        residual[:, at] = hidden[:, at].astype(jnp.float32) + dot_nt(
            mid_columns[:, inner:], mid[at, inner:]
        )

    looped(width, rows, mixing)
    value = residual[...]
    inverse = lax.rsqrt(jnp.mean(value * value, axis=-1, keepdims=True) + EPSILON)
    normed_two[...] = (value * inverse * gain[...]).astype(jnp.bfloat16)
    fetched(feed, semaphores.at[2], 0, 2 * hidden_units)

    def opening(at):
        g = dot(normed_two[...], feed[:, at])
        u = dot(normed_two[...], feed[:, shift(at, hidden_units)])
        gate[:, at] = g
        up[:, at] = u
        active = (g * jax.nn.sigmoid(g)) * u
        feed_columns[:, shift(at, 2 * hidden_units)] = active.astype(jnp.bfloat16)

    looped(hidden_units, tile, opening)
    fetched(feed, semaphores.at[3], 2 * hidden_units, 3 * hidden_units)

    def closing(at):
        layer_out[:, at] = (
            residual[:, at] + dot_nt(feed_columns[:, 2 * hidden_units :], feed[at, 2 * hidden_units :])
        ).astype(jnp.bfloat16)

    looped(width, rows, closing)

    def activation(at):
        grad_active = dot(cotangent[...], feed[:, shift(at, 2 * hidden_units)])
        g, u = gate[:, at], up[:, at]
        s = jax.nn.sigmoid(g)
        feed_columns[:, at] = (grad_active * u * (s * (1.0 + g * (1.0 - s)))).astype(jnp.bfloat16)
        feed_columns[:, shift(at, hidden_units)] = (grad_active * (g * s)).astype(jnp.bfloat16)

    looped(hidden_units, tile, activation)

    def opening_back(at):
        grad_two[:, at] = dot_nt(
            feed_columns[:, : 2 * hidden_units], feed[at, : 2 * hidden_units]
        )

    looped(width, rows, opening_back)
    value = residual[...]
    grad = grad_two[...]
    gain_grad[...] = jnp.sum(grad * value * inverse, axis=0, keepdims=True)
    scaled = grad * gain[...]
    mean = jnp.mean(scaled * value, axis=-1, keepdims=True)
    grad = (
        cotangent[...].astype(jnp.float32)
        + inverse * scaled
        - value * (inverse * inverse * inverse) * mean
    )
    grad_residual[...] = grad
    grad_mix[...] = grad.astype(jnp.bfloat16)

    def gating_back(at):
        grad_gated = dot(grad_mix[...], mid[:, shift(at, inner)])
        z = gate_z[:, at]
        s = jax.nn.sigmoid(z)
        grad = grad_gated * (z * s)
        grad_y[:, at] = grad
        wide = dot_exact(carried[...], spread[:, at])
        pulled[:NS, at] = dot(turned_reads, (wide * grad).astype(jnp.bfloat16)).astype(jnp.bfloat16)
        grad_z = grad_gated * ssm_out[:, at] * (s * (1.0 + z * (1.0 - s)))
        mid_columns[:, at] = grad_z.astype(jnp.bfloat16)

    looped(inner, tile, gating_back)
    grad_att[...] = dot(grad_mix[...], mid[:, 2 * inner :]).astype(jnp.bfloat16)

    def normed_back(at):
        grad_normed[:, at] = dot_nt(mid_columns[:, :inner], mid[at, :inner])

    looped(width, rows, normed_back)
    tokens = hidden.shape[0]
    last = jnp.broadcast_to(carried[tokens - 1 :, :], (8, NS))
    last = dot_exact(last, spread[...])
    pulled[NS:, :] = jnp.concatenate([last, last], axis=0).astype(jnp.bfloat16)


def middle(
    flags, hidden, normed, cotangent, own, project, near, far, running, column, spread, attended, gain,
    mid_pieces, feed_pieces
):
    tokens, width = hidden.shape
    inner, heads = own.shape[1], attended.shape[1]
    mid = 2 * inner + heads
    feed = feed_pieces[0].shape[1]
    runs = piece_rows(width)
    low = lambda n: jax.ShapeDtypeStruct((tokens, n), jnp.bfloat16)
    high = lambda n: jax.ShapeDtypeStruct((tokens, n), jnp.float32)
    return pl.pallas_call(
        lambda *refs: middle_kernel(runs, *refs),
        in_specs=full_specs(13) + any_specs(16),
        out_specs=full_specs(13),
        out_shape=[
            low(width),
            low(width),
            low(feed),
            low(width),
            low(mid),
            high(width),
            high(inner),
            low(heads),
            high(width),
            jax.ShapeDtypeStruct((1, width), jnp.float32),
            jax.ShapeDtypeStruct((NS + 16, inner), jnp.bfloat16),
            jax.ShapeDtypeStruct((NS, inner), jnp.bfloat16),
            high(NS),
        ],
        scratch_shapes=[
            pltpu.VMEM((width, mid), jnp.bfloat16),
            pltpu.VMEM((width, feed), jnp.bfloat16),
            pltpu.VMEM((tokens, inner), jnp.float32),
            pltpu.VMEM((tokens, inner), jnp.float32),
            pltpu.VMEM((tokens, feed // 3), jnp.float32),
            pltpu.VMEM((tokens, feed // 3), jnp.float32),
            pltpu.VMEM((tokens, width), jnp.float32),
            pltpu.VMEM((tokens, width), jnp.float32),
            pltpu.SemaphoreType.DMA((4,)),
        ],
        compiler_params=params(),
        name="middle",
        cost_estimate=cost(29),
    )(
        flags, hidden, normed, cotangent, own, project, near, far, running, column, spread, attended, gain[None],
        *mid_pieces, *feed_pieces
    )


def width_order(width):
    devices, pieces = lax.axis_size("fsdp"), lax.axis_size("ctx")
    rows = width // (devices * pieces)
    block = rows * pieces // 2
    place = jnp.arange(width)
    core, half = place // (width // 2), (place // (width // 4)) % 2
    inner = place % (width // 4)
    device = lax.axis_index("fsdp") ^ (2 * (inner // block) + core)
    along = lax.axis_index("ctx") ^ ((inner % block) // rows + half * (pieces // 2))
    return (device * pieces + along) * rows + inner % rows


def gather_ctx(value, *hold):
    size = lax.axis_size("ctx")
    blocks = [value]
    if size == 4:
        one, two = swap_ctx(value, 1), swap_ctx(value, 2)
        return [value, one, two, swap_ctx(after(two, one, *hold), 1)]
    mask = 1
    while mask < size:
        blocks = blocks + [swap_ctx(block, mask) for block in blocks]
        mask *= 2
    return blocks


def scatter_ctx(blocks, early, late):
    size = lax.axis_size("ctx")
    if size == 4:
        far = after(swap_ctx(blocks[3], 1), early)
        one, two = after([swap_ctx(blocks[1], 1), swap_ctx(plus(blocks[2], far), 2)], late)
        return total([blocks[0], one, two])
    while size > 1:
        size //= 2
        blocks = [plus(blocks[j], swap_ctx(blocks[j + size], size)) for j in range(size)]
    return blocks[0].astype(jnp.float32)


def total_steps():
    return [
        (axis, 1 << i)
        for axis in ("fsdp", "ctx")
        for i in range(lax.axis_size(axis).bit_length() - 1)
    ]


def total_step(value, axis, mask):
    pairs = [(i, i ^ mask) for i in range(lax.axis_size(axis))]
    return value + lax.ppermute(value, axis, pairs)


def local(
    hidden_in,
    segments,
    cotangent,
    mixer_in,
    mixer_out,
    gate_up,
    down_weight,
    norm_gain,
    feed_gain,
    step_bias,
    decay_log,
    skip_gain,
):
    mixer_width = SH * SP
    width = hidden_in.shape[1]
    edges = [mixer_width, 2 * mixer_width, 2 * mixer_width + 2 * NS]
    edges += [edges[-1] + SH, mixer_in.shape[1]]
    in_z = mixer_in[:, : edges[0]]
    in_mix = jnp.concatenate(
        [
            mixer_in[:, edges[0] : edges[2]],
            mixer_in[:, edges[3] : edges[4]],
            mixer_in[:, edges[2] : edges[3]],
        ],
        axis=1,
    )
    in_mix = jnp.pad(in_mix, ((0, 0), (0, -in_mix.shape[1] % NS)))
    in_mid = jnp.concatenate([in_z, mixer_out.T], axis=1)
    in_feed = jnp.concatenate([gate_up, down_weight.T], axis=1)
    mix_blocks = gather_ctx(in_mix)
    mix_parts = gather_inner(gather_first(mix_blocks))
    mix_others = gather_last(mix_parts)
    mid_blocks = gather_ctx(after(in_mid, mix_blocks[-1]), mix_parts)
    mid_first = gather_first(after(mid_blocks, mix_others))
    feed_blocks = gather_ctx(after(in_feed, mid_blocks[1:3]), mid_first)
    mix_pieces = gather_core(mix_parts, mix_others)
    order = width_order(width)
    turn = (jnp.arange(width)[:, None] == order[None, :]).astype(jnp.bfloat16)

    def unturn(value):
        value = jnp.dot(value, turn.T, preferred_element_type=jnp.float32)
        return value.astype(jnp.bfloat16)

    hidden_in, cotangent = (
        jnp.dot(v, turn, preferred_element_type=jnp.float32).astype(jnp.bfloat16)
        for v in (hidden_in, cotangent)
    )
    gains = jnp.dot(
        jnp.stack([norm_gain, feed_gain]),
        turn.astype(jnp.float32),
        precision=lax.Precision.HIGHEST,
    )
    norm_gain, feed_gain = gains[0], gains[1]
    tokens = hidden_in.shape[0]
    piece = lax.axis_index("ctx")
    frequency = ROTARY_BASE ** (jnp.arange(HEAD_SIZE // 2, dtype=jnp.float32) * (-2.0 / HEAD_SIZE))
    token_position = (piece * tokens + jnp.arange(tokens)).astype(jnp.float32)
    angles = frequency[:, None] * token_position[None, :]
    turn_cos, turn_sin = jnp.cos(angles), jnp.sin(angles)
    segment_float = segments.astype(jnp.float32)
    row, column = segment_float[None, :], segment_float[:, None]
    place = piece.astype(jnp.int32)[None]
    spread = spread_heads()
    bias, decay = (jnp.pad(v, (0, NS - SH))[None] for v in (step_bias, decay_log))
    skip = jnp.repeat(skip_gain, SP)[None]
    normed, project, queries, packed = project_in(
        after(hidden_in, mid_first, feed_blocks[1:3]),
        norm_gain,
        turn_cos,
        turn_sin,
        jnp.pad(row, ((0, 0), (0, 2 * KEY_WIDTH - tokens))),
        mix_pieces,
    )
    mid_parts = gather_inner(mid_first, project)
    mid_others = gather_last(mid_parts)
    blocks = gather_ctx(packed)
    feed_first = gather_first(after(feed_blocks, project))
    own, states, running = state_forward(
        after(project, mid_parts, feed_first), bias, decay, skip, spread, column, row
    )
    feed_parts = gather_inner(feed_first, own)
    attended, total, flags = attend(
        place, after(queries, feed_parts, mid_others, cotangent), row, blocks
    )
    near, both = entering_near(states, flags, False)
    feed_others = gather_last(feed_parts)
    mid_pieces = gather_core(mid_parts, mid_others)
    feed_pieces = gather_core(feed_parts, feed_others)
    far = entering_far(both, flags, False)
    (
        layer_out,
        normed_two,
        feed_columns,
        grad_mix,
        mid_columns,
        grad_residual,
        grad_y,
        grad_att,
        grad_normed_part,
        grad_feed_gain,
        pulled,
        entered,
        carried,
    ) = middle(
        flags,
        hidden_in,
        normed,
        cotangent,
        own,
        project,
        near,
        far,
        running,
        column,
        spread,
        attended,
        feed_gain,
        mid_pieces,
        feed_pieces,
    )
    feed_args = (normed_two, cotangent, feed_columns, 2 * FF)
    mid_args = (normed, grad_mix, mid_columns, mixer_width)
    whole = jnp.ones((8, NS), jnp.float32)
    mid_sent = weight_half(*mid_args, 1, 512)
    mid_arrived = swap(mid_sent, 1)
    feed_sent = weight_half(*after(feed_args[:3], mid_sent), feed_args[3], 1, 2048)
    feed_arrived = swap(feed_sent, 1)
    mid_go = weight_sum(*after(mid_args[:3], feed_sent), mid_args[3], mid_arrived, 512)
    near, both = entering_near(pulled, after(whole, mid_go), True)
    grad_query, *grad_blocks = attend_back(
        place, queries, row, after(grad_att, both), total, turn_cos, turn_sin, blocks
    )
    far = entering_far(both, whole, True)
    feed_go = weight_sum(*after(feed_args[:3], grad_blocks), feed_args[3], feed_arrived, 2048)
    grad_keys = scatter_ctx(grad_blocks, feed_go, feed_go)
    mid_go = next_go(*mid_go, feed_go)
    grad_project, small = state_back(
        project,
        bias,
        decay,
        skip,
        spread,
        column,
        row,
        after(grad_y, feed_go, mid_go[1]),
        carried,
        entered,
        near,
        far,
        grad_query,
        grad_keys,
        turn_cos,
        turn_sin,
    )
    mix_args = (normed, normed, grad_project)
    mix_sent = weight_half(*mix_args, grad_project.shape[1], 1, 896)
    mix_arrived = swap(mix_sent, 1)
    layer_out = unturn(layer_out)
    feed_go = next_go(*feed_go, mix_sent, layer_out)
    mid_near = scatter_near(*mid_go, feed_go[1])
    mix_go = weight_sum(
        *after(mix_args, feed_go[1], mid_near[2]), grad_project.shape[1], mix_arrived, 896
    )
    mid_far = scatter_far(*mid_near, mix_go)
    feed_near = scatter_near(*feed_go, mix_go)
    grad_hidden, grad_norm_gain = project_back(
        hidden_in,
        norm_gain,
        after(grad_project, mid_far[1], feed_near[2]),
        grad_normed_part,
        grad_residual,
        mix_pieces,
    )
    mix_go = next_go(*mix_go, grad_hidden)
    feed_far = scatter_far(*feed_near, mix_go[1])
    mix_near = scatter_near(*mix_go, feed_far[1])
    mix_far = scatter_far(*mix_near)
    grad_hidden, grad_norm_gain = after((grad_hidden, grad_norm_gain), mix_near[2])
    gain_grads = jnp.dot(
        jnp.concatenate([grad_norm_gain, grad_feed_gain]),
        turn.T.astype(jnp.float32),
        precision=lax.Precision.HIGHEST,
    )
    packed = jnp.concatenate([gain_grads.reshape(-1, NS), small], axis=0)
    steps = total_steps()
    for step in steps:
        packed = total_step(packed, *step)
    owned_mid, owned_feed, owned_mix = (scatter_end(*v) for v in (mid_far, feed_far, mix_far))
    small, total_gain = packed[-small.shape[0] :], packed[: -small.shape[0]].reshape(2, width)
    total_norm, total_feed = total_gain[0], total_gain[1]
    total_bias, total_decay, total_skip = (small[i, :SH] for i in range(3))
    mix_edge = mixer_width + 2 * NS
    token_offset = grad_project.shape[1] - NS
    owned_in = jnp.concatenate(
        [
            owned_mid[:, :mixer_width],
            owned_mix[:, :mix_edge],
            owned_mix[:, token_offset : token_offset + SH],
            owned_mix[:, mix_edge:token_offset],
        ],
        axis=1,
    )
    owned_out = owned_mid[:, mixer_width:]
    grad_hidden = unturn(grad_hidden)
    return (
        layer_out,
        grad_hidden,
        owned_in,
        owned_out.T,
        owned_feed[:, : 2 * FF],
        owned_feed[:, 2 * FF :].T,
        total_norm,
        total_feed,
        total_bias,
        total_decay,
        total_skip,
    )


def solution(mesh):
    return jax.shard_map(
        local,
        mesh=mesh,
        in_specs=(
            P(("fsdp", "ctx"), None),
            P(("fsdp", "ctx")),
            P(("fsdp", "ctx"), None),
            P(("fsdp", "ctx"), None),
            P(None, ("fsdp", "ctx")),
            P(("fsdp", "ctx"), None),
            P(None, ("fsdp", "ctx")),
            P(),
            P(),
            P(),
            P(),
            P(),
        ),
        out_specs=(
            P(("fsdp", "ctx"), None),
            P(("fsdp", "ctx"), None),
            P(("fsdp", "ctx"), None),
            P(None, ("fsdp", "ctx")),
            P(("fsdp", "ctx"), None),
            P(None, ("fsdp", "ctx")),
            P(),
            P(),
            P(),
            P(),
            P(),
        ),
        check_vma=False,
    )
```

```python
import jax
import jax.numpy as jnp
from jax import lax
from jax.experimental import pallas as pl
from jax.experimental.pallas import tpu as pltpu
from jax.sharding import PartitionSpec as P

FF = 2048
SH = 24
SP = 64
NS = 128
QUERY_HEADS = 8
KEY_VALUE_HEADS = 2
HEAD_SIZE = 64
KEY_WIDTH = KEY_VALUE_HEADS * HEAD_SIZE
REPEAT = QUERY_HEADS // KEY_VALUE_HEADS


EPSILON = 1e-06
ROTARY_BASE = 100000000000.0


def swap(value, mask):
    size = lax.axis_size("fsdp")
    return lax.ppermute(value, "fsdp", [(i, i ^ mask) for i in range(size)])


def swap_ctx(value, mask):
    size = lax.axis_size("ctx")
    return lax.ppermute(value, "ctx", [(i, i ^ mask) for i in range(size)])


def after(value, *others):
    return lax.optimization_barrier((value, others))[0]


def chip_masks():
    bits = lax.axis_size("fsdp").bit_length() - 2
    masks = [2 << i for i in range(bits)]
    x_masks, y_masks = masks[: bits // 2], masks[bits // 2 :]
    return (y_masks + x_masks, x_masks + y_masks)


def gather_first(blocks):
    half = len(blocks) // 2
    return [jnp.concatenate(blocks[:half], axis=0), jnp.concatenate(blocks[half:], axis=0)]


def gather_inner(parts, *hold):
    out = []
    for part, masks in zip(parts, chip_masks()):
        for mask in masks[:-1]:
            part = jnp.concatenate([part, after(swap(part, mask), *hold)], axis=0)
        out.append(part)
    return out


def gather_last(parts):
    return [swap(part, masks[-1]) for part, masks in zip(parts, chip_masks())]


def gather_core(parts, others):
    pieces = []
    for own in zip(parts, others):
        pieces += list(own) + [swap(piece, 1) for piece in own]
    return pieces


def piece_rows(width):
    devices = lax.axis_size("fsdp")
    block = width // (2 * devices)
    runs = []
    for half, masks in enumerate(chip_masks()):
        for core in (0, 1):
            for last in (0, 1):
                piece = half * 4 + core * 2 + last
                for inner in range(devices // 4):
                    chip = last * masks[-1]
                    for i, mask in enumerate(masks[:-1]):
                        chip += ((inner >> i) & 1) * mask
                    start = core * (width // 2) + half * (width // 4) + (chip >> 1) * block
                    runs.append((piece, inner * block, start, block))
    return runs


def plus(left, right):
    return (left.astype(jnp.float32) + right.astype(jnp.float32)).astype(jnp.bfloat16)


def total(values):
    result = values[0].astype(jnp.float32)
    for value in values[1:]:
        result = result + value.astype(jnp.float32)
    return result


def split_next(parts, stage):
    stay, go = [], []
    for terms, masks in zip(parts, chip_masks()):
        order = masks[::-1]
        axis = sorted(order[stage:], reverse=True).index(order[stage])
        stay.append([lax.index_in_dim(v, 0, axis, keepdims=False) for v in terms])
        go.append(
            total([lax.index_in_dim(v, 1, axis, keepdims=False) for v in terms]).astype(jnp.bfloat16)
        )
    return stay, go


def arrive(stay, go, stage, *hold):
    return [
        terms + [after(swap(value, masks[::-1][stage]), *hold)]
        for terms, value, masks in zip(stay, go, chip_masks())
    ]


def next_go(stay, go, *hold):
    parts = arrive(stay, go, 0, *hold)
    last = len(chip_masks()[0]) - 1
    for stage in range(1, last):
        stay, go = split_next(parts, stage)
        parts = arrive(stay, go, stage)
    return split_next(parts, last)


def low_total(terms):
    return total(terms).astype(jnp.bfloat16)


def scatter_near(stay, go, hold):
    pieces = lax.axis_size("ctx")
    blocks = []
    for terms in arrive(stay, go, len(chip_masks()[0]) - 1, hold):
        rows = terms[0].shape[0] // (pieces // 2)
        blocks += [[v[j * rows : (j + 1) * rows] for v in terms] for j in range(pieces // 2)]
    size = pieces
    while size > 4:
        size //= 2
        blocks = [blocks[j] + [swap_ctx(low_total(blocks[j + size]), size)] for j in range(size)]
    return blocks[0], blocks[2], [low_total(blocks[1]), low_total(blocks[3])]


def scatter_far(stay, through, go, *hold):
    one, far = after([swap_ctx(v, 1) for v in go], *hold)
    return stay + [one], low_total(through + [far])


def scatter_end(stay, two):
    return total(stay + [swap_ctx(two, 2)])


NT = (((1,), (1,)), ((), ()))
TN = (((0,), (0,)), ((), ()))
VMEM_BYTES = 58 * 1024 * 1024


def cost(microseconds):
    return pl.CostEstimate(
        flops=int(microseconds * 1e9), bytes_accessed=int(microseconds * 3e6), transcendentals=0
    )


def params():
    return pltpu.CompilerParams(vmem_limit_bytes=VMEM_BYTES)


def weight_kernel(edge, rows_one, rows_two, columns, out, turned):
    step = pl.program_id(0)

    @pl.when(step == 0)
    def _():
        turned[...] = rows_one[...].T

    @pl.when(step == edge)
    def _():
        turned[...] = rows_two[...].T

    out[...] = dot(turned[...], columns[...]).astype(jnp.bfloat16)


def weight_half(rows_one, rows_two, columns, edge, half, tile=512):
    tokens, width = rows_one.shape
    half_rows = pl.BlockSpec((tokens, width // 2), lambda j: (0, half))
    count = columns.shape[1]
    return pl.pallas_call(
        lambda *refs: weight_kernel(edge // tile, *refs),
        grid=(count // tile,),
        in_specs=[half_rows, half_rows, pl.BlockSpec((tokens, tile), lambda j: (0, j))],
        out_specs=pl.BlockSpec((width // 2, tile), lambda j: (0, j)),
        out_shape=jax.ShapeDtypeStruct((width // 2, count), jnp.bfloat16),
        scratch_shapes=[pltpu.VMEM((width // 2, tokens), jnp.bfloat16)],
        compiler_params=params(),
        name="weight_grad",
        cost_estimate=cost(0),
    )(rows_one, rows_two, columns)


def sum_rows(width):
    devices = lax.axis_size("fsdp")
    block = width // (2 * devices)
    runs = []
    for half, masks in enumerate(chip_masks()):
        bit = masks[-1] >> 1
        for value in (0, bit):
            chips = [c for c in range(devices // 2) if c & bit == value]
            runs.append([half * (width // 4) + c * block for c in chips])
    return runs, block


def weight_sum_kernel(edge, runs, block, rows_one, rows_two, columns, arrived, *refs):
    out, turned = refs[:4], refs[4]
    step = pl.program_id(0)

    @pl.when(step == 0)
    def _():
        turned[...] = rows_one[...].T

    @pl.when(step == edge)
    def _():
        turned[...] = rows_two[...].T

    value = dot(turned[...], columns[...]) + arrived[...].astype(jnp.float32)
    value = value.astype(jnp.bfloat16)
    for ref, starts in zip(out, runs):
        for i, start in enumerate(starts):
            ref[i * block : (i + 1) * block, :] = value[start : start + block]


def weight_sum(rows_one, rows_two, columns, edge, arrived, tile):
    tokens, width = rows_one.shape
    half_rows = pl.BlockSpec((tokens, width // 2), lambda j: (0, 0))
    count = columns.shape[1]
    runs, block = sum_rows(width)
    results = pl.pallas_call(
        lambda *refs: weight_sum_kernel(edge // tile, runs, block, *refs),
        grid=(count // tile,),
        in_specs=[
            half_rows,
            half_rows,
            pl.BlockSpec((tokens, tile), lambda j: (0, j)),
            pl.BlockSpec((width // 2, tile), lambda j: (0, j)),
        ],
        out_specs=[pl.BlockSpec((width // 8, tile), lambda j: (0, j))] * 4,
        out_shape=[jax.ShapeDtypeStruct((width // 8, count), jnp.bfloat16)] * 4,
        scratch_shapes=[pltpu.VMEM((width // 2, tokens), jnp.bfloat16)],
        compiler_params=params(),
        name="weight_sum",
        cost_estimate=cost(0),
    )(rows_one, rows_two, columns, arrived)
    shape = [2] * (len(chip_masks()[0]) - 1) + [block, count]
    stay_a, go_a, stay_b, go_b = (v.reshape(shape) for v in results)
    return [[stay_a], [stay_b]], [go_a, go_b]


def fetch(pieces, whole, semaphore, runs, start, stop):
    for piece, source, target, count in runs:
        pltpu.make_async_copy(
            pieces[piece].at[pl.ds(source, count), start:stop],
            whole.at[pl.ds(target, count), start:stop],
            semaphore,
        ).start()


def fetched(whole, semaphore, start, stop):
    view = whole.at[:, start:stop]
    pltpu.make_async_copy(view, view, semaphore).wait()


def dot(left, right):
    return jnp.dot(left, right, preferred_element_type=jnp.float32)


def dot_nt(left, right):
    return lax.dot_general(left, right, NT, preferred_element_type=jnp.float32)


def tiles(total, tile, body):
    for start in range(0, total, tile):
        body(slice(start, start + tile))


def looped(total, tile, body):
    @pl.loop(0, total // tile)
    def _(i):
        body(pl.ds(pl.multiple_of(i * tile, tile), tile))


def project_kernel(runs, hidden, gain, turn_cos, turn_sin, segment_row, *refs):
    pieces, refs = refs[:8], refs[8:]
    normed, project, queries, packed, whole, semaphore = refs
    columns, tokens = whole.shape[1], hidden.shape[0]
    fetch(pieces, whole, semaphore, runs, 0, columns)
    h = hidden[...].astype(jnp.float32)
    inverse = lax.rsqrt(jnp.mean(h * h, axis=-1, keepdims=True) + EPSILON)
    normed[...] = (h * inverse * gain[...]).astype(jnp.bfloat16)
    fetched(whole, semaphore, 0, columns)

    def body(at):
        project[:, at] = dot(normed[...], whole[:, at])

    tiles(columns, 384, body)
    start = SH * SP + 2 * NS
    turned = project[:, start : start + QUERY_HEADS * HEAD_SIZE].T
    queries[...] = (rotate(turned, turn_cos, turn_sin) * HEAD_SIZE ** (-0.5)).astype(jnp.bfloat16)
    start = start + QUERY_HEADS * HEAD_SIZE
    keys = rotate(project[:, start : start + KEY_WIDTH].T, turn_cos, turn_sin)
    packed[:tokens, :KEY_WIDTH] = keys.T.astype(jnp.bfloat16)
    start = start + KEY_WIDTH
    packed[:tokens, KEY_WIDTH:] = project[:, start : start + KEY_WIDTH].astype(jnp.bfloat16)
    packed[tokens:, :] = jnp.broadcast_to(segment_row[...], (16, 2 * KEY_WIDTH)).astype(jnp.bfloat16)


def rotate(turned, turn_cos, turn_sin, sign=1.0):
    half = HEAD_SIZE // 2
    c, s = turn_cos[...], turn_sin[...] * sign
    out = []
    for start in range(0, turned.shape[0], HEAD_SIZE):
        first, second = turned[start : start + half], turned[start + half : start + HEAD_SIZE]
        out += [first * c - second * s, second * c + first * s]
    return jnp.concatenate(out, axis=0)


def full_specs(count):
    return [pl.BlockSpec(memory_space=pltpu.VMEM)] * count


def any_specs(count):
    return [pl.BlockSpec(memory_space=pl.ANY)] * count


def project_in(hidden, gain, turn_cos, turn_sin, segment_row, pieces):
    tokens, width = hidden.shape
    columns = pieces[0].shape[1]
    runs = piece_rows(width)
    return pl.pallas_call(
        lambda *refs: project_kernel(runs, *refs),
        in_specs=full_specs(5) + any_specs(8),
        out_specs=full_specs(4),
        out_shape=[
            jax.ShapeDtypeStruct((tokens, width), jnp.bfloat16),
            jax.ShapeDtypeStruct((tokens, columns), jnp.float32),
            jax.ShapeDtypeStruct((QUERY_HEADS * HEAD_SIZE, tokens), jnp.bfloat16),
            jax.ShapeDtypeStruct((tokens + 16, 2 * KEY_WIDTH), jnp.bfloat16),
        ],
        scratch_shapes=[pltpu.VMEM((width, columns), jnp.bfloat16), pltpu.SemaphoreType.DMA],
        compiler_params=params(),
        name="project_in",
        cost_estimate=cost(0),
    )(hidden, gain[None], turn_cos, turn_sin, segment_row, *pieces)


def spread_heads():
    head = lax.broadcasted_iota(jnp.int32, (NS, SH * SP), 1) // SP
    return (lax.broadcasted_iota(jnp.int32, (NS, SH * SP), 0) == head).astype(jnp.float32)


def dot_exact(left, right):
    return jnp.dot(
        left, right, precision=lax.Precision.HIGHEST, preferred_element_type=jnp.float32
    )


def step_terms(project, bias, decay):
    tokens = project.shape[0]
    raw = project[:, project.shape[1] - NS :] + bias[...]
    step = jnp.maximum(raw, 0.0) + jnp.log1p(jnp.exp(-jnp.abs(raw)))
    rate = -jnp.exp(decay[...]) * step
    rows = lax.broadcasted_iota(jnp.int32, (tokens, tokens), 0)
    columns = lax.broadcasted_iota(jnp.int32, (tokens, tokens), 1)
    running = dot_exact((rows >= columns).astype(jnp.float32), rate)
    return raw, step, rate, running


def tail_terms(running, segment_column):
    tokens = running.shape[0]
    same = segment_column[...] == segment_column[tokens - 1 :, :]
    return jnp.where(same, jnp.exp(running[tokens - 1 :, :] - running), 0.0)


def split_low(values):
    high = values.astype(jnp.bfloat16)
    return high, (values - high.astype(jnp.float32)).astype(jnp.bfloat16)


def twice(values):
    return jnp.concatenate([values, values], axis=0)


def state_kernel(project, bias, decay, skip, spread, column, row, own, packed, running_out, bias_sum, turned):
    tokens, inner = own.shape
    _, step, _, running = step_terms(project, bias, decay)
    running_out[...] = running
    tail = tail_terms(running, column) * step
    tail = dot_exact(tail, spread[...])
    values = project[:, :inner]
    states = dot(project[:, inner : inner + NS].T.astype(jnp.bfloat16), (tail * values).astype(jnp.bfloat16))
    packed[:NS, :] = states.astype(jnp.bfloat16)
    last = dot_exact(jnp.broadcast_to(jnp.exp(running[tokens - 1 :, :]), (8, NS)), spread[...])
    packed[NS:, :] = jnp.concatenate([last, last], axis=0).astype(jnp.bfloat16)
    at_row = lax.broadcasted_iota(jnp.int32, (tokens, tokens), 0)
    at_column = lax.broadcasted_iota(jnp.int32, (tokens, tokens), 1)
    allowed = (at_row >= at_column) & (column[...] == row[...])
    turned[0] = running.T
    turned[1] = step.T
    bias_sum[...] = jnp.where(allowed, 0.0, -1e30)
    match = lax.dot_general(
        project[:, inner + NS : inner + 2 * NS],
        project[:, inner : inner + NS],
        NT,
        precision=lax.Precision.HIGHEST,
        preferred_element_type=jnp.float32,
    )
    lane = lax.broadcasted_iota(jnp.int32, (tokens, NS), 1)

    for pair in range(SH // 2):
        at = slice(pair * NS, (pair + 1) * NS)
        values = project[:, at]
        parts = []
        for k in (0, 1):
            head = 2 * pair + k
            gap = running_out[:, head : head + 1] - turned[0, slice(head, head + 1), :]
            weight = jnp.exp(jnp.minimum(gap, 0.0) + bias_sum[...])
            weight = weight * match * turned[1, slice(head, head + 1), :]
            parts.append(dot(weight.astype(jnp.bfloat16), values.astype(jnp.bfloat16)))
        own[:, at] = jnp.where(lane < SP, parts[0], parts[1]) + skip[:, at] * values


def state_forward(project, bias, decay, skip, spread, column, row):
    tokens, inner = project.shape[0], SH * SP
    return pl.pallas_call(
        state_kernel,
        in_specs=full_specs(7),
        out_specs=full_specs(3),
        out_shape=[
            jax.ShapeDtypeStruct((tokens, inner), jnp.float32),
            jax.ShapeDtypeStruct((NS + 16, inner), jnp.bfloat16),
            jax.ShapeDtypeStruct((tokens, NS), jnp.float32),
        ],
        scratch_shapes=[
            pltpu.VMEM((tokens, tokens), jnp.float32),
            pltpu.VMEM((2, NS, tokens), jnp.float32),
        ],
        compiler_params=params(),
        name="state_forward",
        cost_estimate=cost(0),
    )(project, bias, decay, skip, spread, column, row)


def key_masks(place, row, blocks, masks):
    tokens = row.shape[1]
    key = lax.broadcasted_iota(jnp.int32, (tokens, tokens), 0)
    query = lax.broadcasted_iota(jnp.int32, (tokens, tokens), 1)
    for j, block in enumerate(blocks):
        label = block[tokens : tokens + 16, :tokens].astype(jnp.float32).T[:, :1]
        ahead = ((place[0] ^ j) - place[0]) * tokens
        allowed = (key + ahead <= query) & (label == row[...])
        masks[j] = jnp.where(allowed, 0.0, -1e30)


def attend_kernel(count, place, queries, row, *refs):
    blocks, refs = refs[:count], refs[count:]
    attended, total, flags, masks, scores, turned, values = refs
    tokens = row.shape[1]
    ends = [block[tokens : tokens + 16, tokens - 1 : tokens].astype(jnp.float32)[:8] for block in blocks]

    def end_of(number):
        found = jnp.zeros((8, 1), jnp.float32)
        for j, end in enumerate(ends):
            found = found + jnp.where((place[0] ^ j) == number, end, 0.0)
        return found

    lane = lax.broadcasted_iota(jnp.int32, (8, NS), 1)
    known = jnp.where(lane == NS - 1, jnp.where(place[0] > 0, end_of(place[0] - 1), -1.0), 0.0)
    for k in range(count):
        same = (end_of(place[0] - k) == end_of(place[0] - k - 1)) & (place[0] > k)
        known = known + jnp.where((lane == k) & same, 1.0, 0.0)
    flags[...] = known
    key_masks(place, row, blocks, masks)
    for j, block in enumerate(blocks):
        values[j] = block[:tokens, KEY_WIDTH:].T
    for group in range(KEY_VALUE_HEADS):
        lanes = slice(group * HEAD_SIZE, (group + 1) * HEAD_SIZE)

        for r in range(REPEAT):
            head = group * REPEAT + r
            at = slice(head * HEAD_SIZE, (head + 1) * HEAD_SIZE)
            highest = None
            for j, block in enumerate(blocks):
                score = dot(block[:tokens, lanes], queries[at, :]) + masks[j]
                scores[j] = score
                top = jnp.max(score, axis=0, keepdims=True)
                highest = top if highest is None else jnp.maximum(highest, top)
            sums = 0.0
            for j in range(count):
                score = jnp.exp(scores[j] - highest)
                scores[j] = score
                sums = sums + jnp.sum(score, axis=0, keepdims=True)
            inverse = 1.0 / sums
            result = 0.0
            for j in range(count):
                result = result + dot(values[j, lanes, :], (scores[j] * inverse).astype(jnp.bfloat16))
            turned[at, :] = result
            total[slice(head, head + 1), :] = highest + jnp.log(sums)

    attended[...] = turned[...].T.astype(jnp.bfloat16)


def attend(place, queries, row, blocks):
    tokens, count = row.shape[1], len(blocks)
    return pl.pallas_call(
        lambda *refs: attend_kernel(count, *refs),
        in_specs=[pl.BlockSpec(memory_space=pltpu.SMEM)] + full_specs(2 + count),
        out_specs=full_specs(3),
        out_shape=[
            jax.ShapeDtypeStruct((tokens, QUERY_HEADS * HEAD_SIZE), jnp.bfloat16),
            jax.ShapeDtypeStruct((QUERY_HEADS, tokens), jnp.float32),
            jax.ShapeDtypeStruct((8, NS), jnp.float32),
        ],
        scratch_shapes=[
            pltpu.VMEM((count, tokens, tokens), jnp.float32),
            pltpu.VMEM((count, tokens, tokens), jnp.float32),
            pltpu.VMEM((QUERY_HEADS * HEAD_SIZE, tokens), jnp.float32),
            pltpu.VMEM((count, KEY_WIDTH, tokens), jnp.bfloat16),
        ],
        compiler_params=params(),
        name="attend",
        cost_estimate=cost(0),
    )(place, queries, row, *blocks)


def attend_back_kernel(count, place, queries, row, grad_att, total, turn_cos, turn_sin, *refs):
    blocks, refs = refs[:count], refs[count:]
    grad_query, grad_blocks, refs = refs[0], refs[1 : 1 + count], refs[1 + count :]
    masks, chances, slopes, turned_keys, turned_grad, grad_turned, key_sums, value_sums = refs
    tokens = row.shape[1]
    key_masks(place, row, blocks, masks)
    turned_grad[...] = grad_att[...].T
    for j, block in enumerate(blocks):
        turned_keys[j] = block[:tokens, :KEY_WIDTH].T
    for group in range(KEY_VALUE_HEADS):
        lanes = slice(group * HEAD_SIZE, (group + 1) * HEAD_SIZE)
        ahead = slice(KEY_WIDTH + group * HEAD_SIZE, KEY_WIDTH + (group + 1) * HEAD_SIZE)
        key_sums[...] = jnp.zeros_like(key_sums)
        value_sums[...] = jnp.zeros_like(value_sums)

        for r in range(REPEAT):
            head = group * REPEAT + r
            at = slice(head * HEAD_SIZE, (head + 1) * HEAD_SIZE)
            query, grad = queries[at, :], turned_grad[at, :]
            query_rows, grad_rows = query.T, grad.T
            inside = 0.0
            for j, block in enumerate(blocks):
                score = dot(block[:tokens, lanes], query) + masks[j]
                chance = jnp.exp(score - total[slice(head, head + 1), :])
                slope = dot(block[:tokens, ahead], grad)
                chances[j], slopes[j] = chance, slope
                inside = inside + jnp.sum(chance * slope, axis=0, keepdims=True)
                value_sums[j] = value_sums[j] + dot(chance.astype(jnp.bfloat16), grad_rows)
            result = 0.0
            for j in range(count):
                slope = (chances[j] * (slopes[j] - inside)).astype(jnp.bfloat16)
                key_sums[j] = key_sums[j] + dot(slope, query_rows)
                result = result + dot(turned_keys[j, lanes, :], slope)
            grad_turned[at, :] = result

        for j in range(count):
            grad_blocks[j][:, lanes] = key_sums[j].astype(jnp.bfloat16)
            grad_blocks[j][:, ahead] = value_sums[j].astype(jnp.bfloat16)
    turned = rotate(grad_turned[...], turn_cos, turn_sin, -1.0) * HEAD_SIZE ** (-0.5)
    grad_query[...] = turned.T.astype(jnp.bfloat16)


def attend_back(place, queries, row, grad_att, total, turn_cos, turn_sin, blocks):
    tokens, count = row.shape[1], len(blocks)
    square = pltpu.VMEM((count, tokens, tokens), jnp.float32)
    heads = QUERY_HEADS * HEAD_SIZE
    return pl.pallas_call(
        lambda *refs: attend_back_kernel(count, *refs),
        in_specs=[pl.BlockSpec(memory_space=pltpu.SMEM)] + full_specs(6 + count),
        out_specs=full_specs(1 + count),
        out_shape=[jax.ShapeDtypeStruct((tokens, heads), jnp.bfloat16)]
        + [jax.ShapeDtypeStruct((tokens, 2 * KEY_WIDTH), jnp.bfloat16)] * count,
        scratch_shapes=[
            square,
            square,
            square,
            pltpu.VMEM((count, KEY_WIDTH, tokens), jnp.bfloat16),
            pltpu.VMEM((heads, tokens), jnp.bfloat16),
            pltpu.VMEM((heads, tokens), jnp.float32),
            pltpu.VMEM((count, tokens, HEAD_SIZE), jnp.float32),
            pltpu.VMEM((count, tokens, HEAD_SIZE), jnp.float32),
        ],
        compiler_params=params(),
        name="attend_back",
        cost_estimate=cost(60),
    )(place, queries, row, grad_att, total, turn_cos, turn_sin, *blocks)


def state_back_kernel(
    project, bias, decay, skip, spread, column, row, grad_y, carried, entered, near, far,
    grad_query, grad_keys, turn_cos, turn_sin,
    grad_project, small, grad_state, bias_sum, turned, match_grad, column_sums, row_sums, running_keep, step_keep,
):
    tokens, inner = grad_y.shape
    raw, step, rate, running = step_terms(project, bias, decay)
    running_keep[...], step_keep[...] = running, step
    grad_state[...] = entered_state(jnp.ones((8, NS), jnp.float32), near, far)
    decayed = tail_terms(running, column)
    tail = decayed * step
    turned[...] = running.T
    values_b = project[:, inner : inner + NS]
    values_c = project[:, inner + NS : inner + 2 * NS]
    low_b, low_c = values_b.astype(jnp.bfloat16), values_c.astype(jnp.bfloat16)
    both_b = jnp.concatenate(split_low(values_b), axis=1)
    both_c = jnp.concatenate(split_low(values_c), axis=1)
    key = lax.broadcasted_iota(jnp.int32, (tokens, tokens), 0)
    query = lax.broadcasted_iota(jnp.int32, (tokens, tokens), 1)
    bias_sum[...] = jnp.where((query >= key) & (column[...] == row[...]), 0.0, -1e30)
    match = lax.dot_general(
        values_b, values_c, NT, precision=lax.Precision.HIGHEST, preferred_element_type=jnp.float32
    )
    match_grad[...] = jnp.zeros_like(match_grad)
    column_sums[...] = jnp.zeros_like(column_sums)
    row_sums[...] = jnp.zeros_like(row_sums)
    lane = lax.broadcasted_iota(jnp.int32, (tokens, NS), 1)

    for pair in range(SH // 2):
        at = slice(pair * NS, (pair + 1) * NS)
        low, rest = split_low(project[:, at])
        low_grad, rest_grad = split_low(grad_y[:, at])
        turned_grad, turned_rest = low_grad.T, rest_grad.T
        parts = []
        for k in (0, 1):
            head = 2 * pair + k
            rows = slice(k * SP, (k + 1) * SP)
            gap = turned[slice(head, head + 1), :] - running_keep[:, head : head + 1]
            weight = jnp.exp(jnp.minimum(gap, 0.0) + bias_sum[...])
            step_column = step_keep[:, head : head + 1]
            slope = dot(
                jnp.concatenate([low[:, rows], rest[:, rows], low[:, rows]], axis=1),
                jnp.concatenate([turned_grad[rows], turned_grad[rows], turned_rest[rows]], axis=0),
            )
            slope = slope * weight
            scaled = slope * step_column
            match_grad[...] = match_grad[...] + scaled
            row_sums[slice(head, head + 1), :] = jnp.sum(scaled * match, axis=0, keepdims=True)
            sums = jnp.sum(slope * match, axis=1, keepdims=True)
            column_sums[...] = column_sums[...] + jnp.where(lane == head, sums, 0.0)
            weight = weight * match * step_column
            parts.append(dot(weight.astype(jnp.bfloat16), low_grad))
        grad_x = jnp.where(lane < SP, parts[0], parts[1]) + skip[:, at] * grad_y[:, at]
        tail_wide = dot_exact(tail, spread[:, at])
        grad_x = grad_x + tail_wide * dot(low_b, grad_state[:, at])
        grad_project[:, at] = grad_x.astype(jnp.bfloat16)

    x, grad = project[:, :inner], grad_y[...]
    carried_wide = dot_exact(carried[...], spread[...])
    tail_wide = dot_exact(tail, spread[...])
    out_b = dot_nt((tail_wide * x).astype(jnp.bfloat16), grad_state[...])
    out_c = dot_nt((carried_wide * grad).astype(jnp.bfloat16), entered[...])
    low_match = match_grad[...].astype(jnp.bfloat16)
    out_b = out_b + dot(low_match, low_c)
    out_c = out_c + dot(match_grad[...].T.astype(jnp.bfloat16), low_b)
    grad_project[:, inner : inner + NS] = out_b.astype(jnp.bfloat16)
    grad_project[:, inner + NS : inner + 2 * NS] = out_c.astype(jnp.bfloat16)

    def per_head(wide):
        return lax.dot_general(
            wide, spread[...], NT, precision=lax.Precision.HIGHEST, preferred_element_type=jnp.float32
        )

    grad_tail = per_head(x * dot(both_b, twice(grad_state[...])))
    grad_carried = per_head(grad * dot(both_c, twice(entered[...])))
    kept = jnp.sum(grad_state[...].astype(jnp.float32) * entered[...].astype(jnp.float32), axis=0, keepdims=True)
    kept = per_head(jnp.broadcast_to(kept, (8, inner)))[:1]
    at_token = lax.broadcasted_iota(jnp.int32, (tokens, NS), 0)
    grad_carried = grad_carried + jnp.where(at_token == tokens - 1, kept, 0.0)
    grad_step = column_sums[...] + grad_tail * decayed
    through = grad_tail * tail
    grad_running = row_sums[...].T - step * column_sums[...] + grad_carried * carried[...] - through
    through = jnp.sum(through, axis=0, keepdims=True)
    grad_running = grad_running + jnp.where(at_token == tokens - 1, through, 0.0)
    grad_rate = dot_exact((query >= key).astype(jnp.float32), grad_running)
    grad_step = grad_step - grad_rate * jnp.exp(decay[...])
    grad_raw = grad_step * jax.nn.sigmoid(raw)
    grad_raw = jnp.where(lane < SH, grad_raw, 0.0)
    grad_skip = per_head(jnp.broadcast_to(jnp.sum(grad * x, axis=0, keepdims=True), (8, inner)))[:1]
    small[0:1, :] = jnp.sum(grad_raw, axis=0, keepdims=True)
    small[1:2, :] = jnp.sum(grad_rate * rate, axis=0, keepdims=True)
    small[2:3, :] = grad_skip
    small[3:, :] = jnp.zeros((5, NS), jnp.float32)
    start = inner + 2 * NS
    heads = QUERY_HEADS * HEAD_SIZE
    grad_project[:, start : start + heads] = grad_query[...]
    start = start + heads
    turned_key = rotate(grad_keys[:, :KEY_WIDTH].T, turn_cos, turn_sin, -1.0)
    grad_project[:, start : start + KEY_WIDTH] = turned_key.T.astype(jnp.bfloat16)
    start = start + KEY_WIDTH
    grad_project[:, start : start + KEY_WIDTH] = grad_keys[:, KEY_WIDTH:].astype(jnp.bfloat16)
    grad_project[:, start + KEY_WIDTH :] = grad_raw.astype(jnp.bfloat16)


def state_back(project, *others):
    tokens, inner = project.shape[0], SH * SP
    square = pltpu.VMEM((tokens, tokens), jnp.float32)
    narrow = pltpu.VMEM((tokens, NS), jnp.float32)
    return pl.pallas_call(
        state_back_kernel,
        in_specs=full_specs(1 + len(others)),
        out_specs=full_specs(2),
        out_shape=[
            jax.ShapeDtypeStruct(project.shape, jnp.bfloat16),
            jax.ShapeDtypeStruct((8, NS), jnp.float32),
        ],
        scratch_shapes=[
            pltpu.VMEM((NS, inner), jnp.bfloat16),
            square,
            pltpu.VMEM((NS, tokens), jnp.float32),
            square,
            narrow,
            pltpu.VMEM((NS, tokens), jnp.float32),
            narrow,
            narrow,
        ],
        compiler_params=params(),
        name="state_back",
        cost_estimate=cost(60),
    )(project, *others)


def shift_ctx(value, by, reverse):
    size = lax.axis_size("ctx")
    pairs = [(i, i + by) for i in range(size - by)]
    return lax.ppermute(value, "ctx", [(j, i) for i, j in pairs] if reverse else pairs)


def join_kernel(flags, own, near, both):
    keep = own[NS : NS + 1, :].astype(jnp.float32) * flags[0:1, 0:1]
    both[...] = (own[:NS, :].astype(jnp.float32) + keep * near[:NS, :].astype(jnp.float32)).astype(
        jnp.bfloat16
    )


def entering_near(packed, same, reverse):
    near = shift_ctx(packed, 1, reverse)
    if lax.axis_size("ctx") != 4:
        return near, packed
    both = pl.pallas_call(
        join_kernel,
        in_specs=full_specs(3),
        out_specs=full_specs(1)[0],
        out_shape=jax.ShapeDtypeStruct((NS, packed.shape[1]), jnp.bfloat16),
        compiler_params=params(),
        name="join",
        cost_estimate=cost(0),
    )(same, packed, near)
    return near, both


def entering_far(both, same, reverse):
    if lax.axis_size("ctx") == 4:
        return shift_ctx(both, 2, reverse)
    total, decay = 0.0, 1.0
    for shift in range(2, lax.axis_size("ctx")):
        part = shift_ctx(both, shift, reverse).astype(jnp.float32)
        total = total + decay * part[:NS]
        decay = decay * same[0, shift] * part[NS : NS + 1]
    return total.astype(jnp.bfloat16)


def entered_state(flags, near, far):
    keep = near[NS : NS + 1, :].astype(jnp.float32) * flags[0:1, 1:2]
    state = near[:NS, :].astype(jnp.float32) + keep * far[...].astype(jnp.float32)
    return state.astype(jnp.bfloat16)


def project_back_kernel(runs, hidden, gain, grad_project, partial, grad_residual, *refs):
    pieces, (grad_hidden, gain_grad, whole, grad_normed, semaphore) = refs[:8], refs[8:]
    columns = whole.shape[1]
    fetch(pieces, whole, semaphore, runs, 0, columns)
    h = hidden[...].astype(jnp.float32)
    inverse = lax.rsqrt(jnp.mean(h * h, axis=-1, keepdims=True) + EPSILON)
    fetched(whole, semaphore, 0, columns)

    def body(at):
        grad_normed[:, at] = partial[:, at] + dot_nt(grad_project[...], whole[at, :])

    tiles(whole.shape[0], 256, body)
    grad = grad_normed[...]
    gain_grad[...] = jnp.sum(grad * h * inverse, axis=0, keepdims=True)
    scaled = grad * gain[...]
    mean = jnp.mean(scaled * h, axis=-1, keepdims=True)
    grad_hidden[...] = (
        grad_residual[...] + inverse * scaled - h * (inverse * inverse * inverse) * mean
    ).astype(jnp.bfloat16)


def project_back(hidden, gain, grad_project, partial, grad_residual, pieces):
    tokens, width = hidden.shape
    columns = pieces[0].shape[1]
    runs = piece_rows(width)
    return pl.pallas_call(
        lambda *refs: project_back_kernel(runs, *refs),
        in_specs=full_specs(5) + any_specs(8),
        out_specs=full_specs(2),
        out_shape=[
            jax.ShapeDtypeStruct((tokens, width), jnp.bfloat16),
            jax.ShapeDtypeStruct((1, width), jnp.float32),
        ],
        scratch_shapes=[
            pltpu.VMEM((width, columns), jnp.bfloat16),
            pltpu.VMEM((tokens, width), jnp.float32),
            pltpu.SemaphoreType.DMA,
        ],
        compiler_params=params(),
        name="project_back",
        cost_estimate=cost(60),
    )(hidden, gain[None], grad_project, partial, grad_residual, *pieces)


def middle_kernel(
    runs, flags, hidden, normed, cotangent, own, project, near, far, running, column, spread, attended, gain, *refs
):
    mid_pieces, feed_pieces, refs = refs[:8], refs[8:16], refs[16:]
    layer_out, normed_two, feed_columns, grad_mix, mid_columns = refs[:5]
    grad_residual, grad_y, grad_att, grad_normed, gain_grad, pulled, entered, carried = refs[5:13]
    mid, feed, gate_z, ssm_out, gate, up, residual, grad_two, semaphores = refs[13:]
    width, inner = hidden.shape[1], own.shape[1]
    reads = project[:, inner + NS : inner + 2 * NS]
    low_reads = jnp.concatenate(split_low(reads), axis=1)
    turned_reads = reads.T.astype(jnp.bfloat16)
    middle_width = inner + attended.shape[1]
    edges = [0, inner, inner + middle_width]
    hidden_units = feed.shape[1] // 3
    tile, rows = 512, 256
    mid_runs = [(0, edges[1]), (edges[1], edges[2])]
    for i, (start, stop) in enumerate(mid_runs):
        fetch(mid_pieces, mid, semaphores.at[i], runs, start, stop)
    feed_runs = [(0, 2 * hidden_units), (2 * hidden_units, 3 * hidden_units)]
    for i, (start, stop) in enumerate(feed_runs):
        fetch(feed_pieces, feed, semaphores.at[2 + i], runs, start, stop)
    entered[...] = entered_state(flags, near, far)
    carried[...] = jnp.where(column[...] == flags[0:1, NS - 1 : NS], jnp.exp(running[...]), 0.0)

    def shift(at, by):
        return pl.ds(pl.multiple_of(at.start + by, 128), at.size)

    fetched(mid, semaphores.at[0], 0, inner)

    def gating(at):
        z = dot(normed[...], mid[:, at])
        gate_z[:, at] = z
        wide = dot_exact(carried[...], spread[:, at])
        y = own[:, at] + wide * dot(low_reads, twice(entered[:, at]))
        ssm_out[:, at] = y
        gated = y * (z * jax.nn.sigmoid(z))
        mid_columns[:, shift(at, inner)] = gated.astype(jnp.bfloat16)

    looped(inner, tile, gating)
    mid_columns[:, 2 * inner :] = attended[...]
    fetched(mid, semaphores.at[1], inner, edges[2])

    def mixing(at):
        residual[:, at] = hidden[:, at].astype(jnp.float32) + dot_nt(
            mid_columns[:, inner:], mid[at, inner:]
        )

    looped(width, rows, mixing)
    value = residual[...]
    inverse = lax.rsqrt(jnp.mean(value * value, axis=-1, keepdims=True) + EPSILON)
    normed_two[...] = (value * inverse * gain[...]).astype(jnp.bfloat16)
    fetched(feed, semaphores.at[2], 0, 2 * hidden_units)

    def opening(at):
        g = dot(normed_two[...], feed[:, at])
        u = dot(normed_two[...], feed[:, shift(at, hidden_units)])
        gate[:, at] = g
        up[:, at] = u
        active = (g * jax.nn.sigmoid(g)) * u
        feed_columns[:, shift(at, 2 * hidden_units)] = active.astype(jnp.bfloat16)

    looped(hidden_units, tile, opening)
    fetched(feed, semaphores.at[3], 2 * hidden_units, 3 * hidden_units)

    def closing(at):
        layer_out[:, at] = (
            residual[:, at] + dot_nt(feed_columns[:, 2 * hidden_units :], feed[at, 2 * hidden_units :])
        ).astype(jnp.bfloat16)

    looped(width, rows, closing)

    def activation(at):
        grad_active = dot(cotangent[...], feed[:, shift(at, 2 * hidden_units)])
        g, u = gate[:, at], up[:, at]
        s = jax.nn.sigmoid(g)
        feed_columns[:, at] = (grad_active * u * (s * (1.0 + g * (1.0 - s)))).astype(jnp.bfloat16)
        feed_columns[:, shift(at, hidden_units)] = (grad_active * (g * s)).astype(jnp.bfloat16)

    looped(hidden_units, tile, activation)

    def opening_back(at):
        grad_two[:, at] = dot_nt(
            feed_columns[:, : 2 * hidden_units], feed[at, : 2 * hidden_units]
        )

    looped(width, rows, opening_back)
    value = residual[...]
    grad = grad_two[...]
    gain_grad[...] = jnp.sum(grad * value * inverse, axis=0, keepdims=True)
    scaled = grad * gain[...]
    mean = jnp.mean(scaled * value, axis=-1, keepdims=True)
    grad = (
        cotangent[...].astype(jnp.float32)
        + inverse * scaled
        - value * (inverse * inverse * inverse) * mean
    )
    grad_residual[...] = grad
    grad_mix[...] = grad.astype(jnp.bfloat16)

    def gating_back(at):
        grad_gated = dot(grad_mix[...], mid[:, shift(at, inner)])
        z = gate_z[:, at]
        s = jax.nn.sigmoid(z)
        grad = grad_gated * (z * s)
        grad_y[:, at] = grad
        wide = dot_exact(carried[...], spread[:, at])
        pulled[:NS, at] = dot(turned_reads, (wide * grad).astype(jnp.bfloat16)).astype(jnp.bfloat16)
        grad_z = grad_gated * ssm_out[:, at] * (s * (1.0 + z * (1.0 - s)))
        mid_columns[:, at] = grad_z.astype(jnp.bfloat16)

    looped(inner, tile, gating_back)
    grad_att[...] = dot(grad_mix[...], mid[:, 2 * inner :]).astype(jnp.bfloat16)

    def normed_back(at):
        grad_normed[:, at] = dot_nt(mid_columns[:, :inner], mid[at, :inner])

    looped(width, rows, normed_back)
    tokens = hidden.shape[0]
    last = jnp.broadcast_to(carried[tokens - 1 :, :], (8, NS))
    last = dot_exact(last, spread[...])
    pulled[NS:, :] = jnp.concatenate([last, last], axis=0).astype(jnp.bfloat16)


def middle(
    flags, hidden, normed, cotangent, own, project, near, far, running, column, spread, attended, gain,
    mid_pieces, feed_pieces
):
    tokens, width = hidden.shape
    inner, heads = own.shape[1], attended.shape[1]
    mid = 2 * inner + heads
    feed = feed_pieces[0].shape[1]
    runs = piece_rows(width)
    low = lambda n: jax.ShapeDtypeStruct((tokens, n), jnp.bfloat16)
    high = lambda n: jax.ShapeDtypeStruct((tokens, n), jnp.float32)
    return pl.pallas_call(
        lambda *refs: middle_kernel(runs, *refs),
        in_specs=full_specs(13) + any_specs(16),
        out_specs=full_specs(13),
        out_shape=[
            low(width),
            low(width),
            low(feed),
            low(width),
            low(mid),
            high(width),
            high(inner),
            low(heads),
            high(width),
            jax.ShapeDtypeStruct((1, width), jnp.float32),
            jax.ShapeDtypeStruct((NS + 16, inner), jnp.bfloat16),
            jax.ShapeDtypeStruct((NS, inner), jnp.bfloat16),
            high(NS),
        ],
        scratch_shapes=[
            pltpu.VMEM((width, mid), jnp.bfloat16),
            pltpu.VMEM((width, feed), jnp.bfloat16),
            pltpu.VMEM((tokens, inner), jnp.float32),
            pltpu.VMEM((tokens, inner), jnp.float32),
            pltpu.VMEM((tokens, feed // 3), jnp.float32),
            pltpu.VMEM((tokens, feed // 3), jnp.float32),
            pltpu.VMEM((tokens, width), jnp.float32),
            pltpu.VMEM((tokens, width), jnp.float32),
            pltpu.SemaphoreType.DMA((4,)),
        ],
        compiler_params=params(),
        name="middle",
        cost_estimate=cost(29),
    )(
        flags, hidden, normed, cotangent, own, project, near, far, running, column, spread, attended, gain[None],
        *mid_pieces, *feed_pieces
    )


def width_order(width):
    devices, pieces = lax.axis_size("fsdp"), lax.axis_size("ctx")
    rows = width // (devices * pieces)
    block = rows * pieces // 2
    place = jnp.arange(width)
    core, half = place // (width // 2), (place // (width // 4)) % 2
    inner = place % (width // 4)
    device = lax.axis_index("fsdp") ^ (2 * (inner // block) + core)
    along = lax.axis_index("ctx") ^ ((inner % block) // rows + half * (pieces // 2))
    return (device * pieces + along) * rows + inner % rows


def gather_ctx(value, *hold):
    size = lax.axis_size("ctx")
    blocks = [value]
    if size == 4:
        one, two = swap_ctx(value, 1), swap_ctx(value, 2)
        return [value, one, two, swap_ctx(after(two, one, *hold), 1)]
    mask = 1
    while mask < size:
        blocks = blocks + [swap_ctx(block, mask) for block in blocks]
        mask *= 2
    return blocks


def scatter_ctx(blocks, early, late):
    size = lax.axis_size("ctx")
    if size == 4:
        far = after(swap_ctx(blocks[3], 1), early)
        one, two = after([swap_ctx(blocks[1], 1), swap_ctx(plus(blocks[2], far), 2)], late)
        return total([blocks[0], one, two])
    while size > 1:
        size //= 2
        blocks = [plus(blocks[j], swap_ctx(blocks[j + size], size)) for j in range(size)]
    return blocks[0].astype(jnp.float32)


def total_steps():
    return [
        (axis, 1 << i)
        for axis in ("fsdp", "ctx")
        for i in range(lax.axis_size(axis).bit_length() - 1)
    ]


def total_step(value, axis, mask):
    pairs = [(i, i ^ mask) for i in range(lax.axis_size(axis))]
    return value + lax.ppermute(value, axis, pairs)


def local(
    hidden_in,
    segments,
    cotangent,
    mixer_in,
    mixer_out,
    gate_up,
    down_weight,
    norm_gain,
    feed_gain,
    step_bias,
    decay_log,
    skip_gain,
):
    mixer_width = SH * SP
    width = hidden_in.shape[1]
    edges = [mixer_width, 2 * mixer_width, 2 * mixer_width + 2 * NS]
    edges += [edges[-1] + SH, mixer_in.shape[1]]
    in_z = mixer_in[:, : edges[0]]
    in_mix = jnp.concatenate(
        [
            mixer_in[:, edges[0] : edges[2]],
            mixer_in[:, edges[3] : edges[4]],
            mixer_in[:, edges[2] : edges[3]],
        ],
        axis=1,
    )
    in_mix = jnp.pad(in_mix, ((0, 0), (0, -in_mix.shape[1] % NS)))
    in_mid = jnp.concatenate([in_z, mixer_out.T], axis=1)
    in_feed = jnp.concatenate([gate_up, down_weight.T], axis=1)
    mix_blocks = gather_ctx(in_mix)
    mix_parts = gather_inner(gather_first(mix_blocks))
    mix_others = gather_last(mix_parts)
    mid_blocks = gather_ctx(after(in_mid, mix_blocks[-1]), mix_parts)
    mid_first = gather_first(after(mid_blocks, mix_others))
    feed_blocks = gather_ctx(after(in_feed, mid_blocks[1:3]), mid_first)
    mix_pieces = gather_core(mix_parts, mix_others)
    order = width_order(width)
    turn = (jnp.arange(width)[:, None] == order[None, :]).astype(jnp.bfloat16)

    def unturn(value):
        value = jnp.dot(value, turn.T, preferred_element_type=jnp.float32)
        return value.astype(jnp.bfloat16)

    hidden_in, cotangent = (
        jnp.dot(v, turn, preferred_element_type=jnp.float32).astype(jnp.bfloat16)
        for v in (hidden_in, cotangent)
    )
    gains = jnp.dot(
        jnp.stack([norm_gain, feed_gain]),
        turn.astype(jnp.float32),
        precision=lax.Precision.HIGHEST,
    )
    norm_gain, feed_gain = gains[0], gains[1]
    tokens = hidden_in.shape[0]
    piece = lax.axis_index("ctx")
    frequency = ROTARY_BASE ** (jnp.arange(HEAD_SIZE // 2, dtype=jnp.float32) * (-2.0 / HEAD_SIZE))
    token_position = (piece * tokens + jnp.arange(tokens)).astype(jnp.float32)
    angles = frequency[:, None] * token_position[None, :]
    turn_cos, turn_sin = jnp.cos(angles), jnp.sin(angles)
    segment_float = segments.astype(jnp.float32)
    row, column = segment_float[None, :], segment_float[:, None]
    place = piece.astype(jnp.int32)[None]
    spread = spread_heads()
    bias, decay = (jnp.pad(v, (0, NS - SH))[None] for v in (step_bias, decay_log))
    skip = jnp.repeat(skip_gain, SP)[None]
    normed, project, queries, packed = project_in(
        after(hidden_in, mid_first, feed_blocks[1:3]),
        norm_gain,
        turn_cos,
        turn_sin,
        jnp.pad(row, ((0, 0), (0, 2 * KEY_WIDTH - tokens))),
        mix_pieces,
    )
    mid_parts = gather_inner(mid_first, project)
    mid_others = gather_last(mid_parts)
    blocks = gather_ctx(packed)
    feed_first = gather_first(after(feed_blocks, project))
    own, states, running = state_forward(
        after(project, mid_parts, feed_first), bias, decay, skip, spread, column, row
    )
    feed_parts = gather_inner(feed_first, own)
    attended, total, flags = attend(
        place, after(queries, feed_parts, mid_others, cotangent), row, blocks
    )
    near, both = entering_near(states, flags, False)
    feed_others = gather_last(feed_parts)
    mid_pieces = gather_core(mid_parts, mid_others)
    feed_pieces = gather_core(feed_parts, feed_others)
    far = entering_far(both, flags, False)
    (
        layer_out,
        normed_two,
        feed_columns,
        grad_mix,
        mid_columns,
        grad_residual,
        grad_y,
        grad_att,
        grad_normed_part,
        grad_feed_gain,
        pulled,
        entered,
        carried,
    ) = middle(
        flags,
        hidden_in,
        normed,
        cotangent,
        own,
        project,
        near,
        far,
        running,
        column,
        spread,
        attended,
        feed_gain,
        mid_pieces,
        feed_pieces,
    )
    feed_args = (normed_two, cotangent, feed_columns, 2 * FF)
    mid_args = (normed, grad_mix, mid_columns, mixer_width)
    whole = jnp.ones((8, NS), jnp.float32)
    mid_sent = weight_half(*mid_args, 1, 512)
    mid_arrived = swap(mid_sent, 1)
    feed_sent = weight_half(*after(feed_args[:3], mid_sent), feed_args[3], 1, 2048)
    feed_arrived = swap(feed_sent, 1)
    mid_go = weight_sum(*after(mid_args[:3], feed_sent), mid_args[3], mid_arrived, 512)
    near, both = entering_near(pulled, after(whole, mid_go), True)
    grad_query, *grad_blocks = attend_back(
        place, queries, row, after(grad_att, both), total, turn_cos, turn_sin, blocks
    )
    far = entering_far(both, whole, True)
    feed_go = weight_sum(*after(feed_args[:3], grad_blocks), feed_args[3], feed_arrived, 2048)
    grad_keys = scatter_ctx(grad_blocks, feed_go, feed_go)
    mid_go = next_go(*mid_go, feed_go)
    grad_project, small = state_back(
        project,
        bias,
        decay,
        skip,
        spread,
        column,
        row,
        after(grad_y, feed_go, mid_go[1]),
        carried,
        entered,
        near,
        far,
        grad_query,
        grad_keys,
        turn_cos,
        turn_sin,
    )
    mix_args = (normed, normed, grad_project)
    mix_sent = weight_half(*mix_args, grad_project.shape[1], 1, 896)
    mix_arrived = swap(mix_sent, 1)
    layer_out = unturn(layer_out)
    feed_go = next_go(*feed_go, mix_sent, layer_out)
    mid_near = scatter_near(*mid_go, feed_go[1])
    mix_go = weight_sum(
        *after(mix_args, feed_go[1], mid_near[2]), grad_project.shape[1], mix_arrived, 896
    )
    mid_far = scatter_far(*mid_near, mix_go)
    feed_near = scatter_near(*feed_go, mix_go)
    grad_hidden, grad_norm_gain = project_back(
        hidden_in,
        norm_gain,
        after(grad_project, mid_far[1], feed_near[2]),
        grad_normed_part,
        grad_residual,
        mix_pieces,
    )
    grad_hidden = unturn(grad_hidden)
    gain_grads = jnp.dot(
        jnp.concatenate([grad_norm_gain, grad_feed_gain]),
        turn.T.astype(jnp.float32),
        precision=lax.Precision.HIGHEST,
    )
    packed = jnp.concatenate([gain_grads.reshape(-1, NS), small], axis=0)
    mix_go = next_go(*mix_go, packed, grad_hidden)
    packed = after(packed, mix_go[1])
    steps, along = total_steps(), len(chip_masks()[0]) + 1
    for step in steps[:along]:
        packed = total_step(packed, *step)
    feed_far = scatter_far(*feed_near, mix_go[1], packed)
    mix_near = scatter_near(*mix_go, feed_far[1])
    mix_far = scatter_far(*mix_near)
    packed = after(packed, mix_near[2])
    for step in steps[along:]:
        packed = total_step(packed, *step)
    owned_mid, owned_feed, owned_mix = (scatter_end(*v) for v in (mid_far, feed_far, mix_far))
    small, total_gain = packed[-small.shape[0] :], packed[: -small.shape[0]].reshape(2, width)
    total_norm, total_feed = total_gain[0], total_gain[1]
    total_bias, total_decay, total_skip = (small[i, :SH] for i in range(3))
    mix_edge = mixer_width + 2 * NS
    token_offset = grad_project.shape[1] - NS
    owned_in = jnp.concatenate(
        [
            owned_mid[:, :mixer_width],
            owned_mix[:, :mix_edge],
            owned_mix[:, token_offset : token_offset + SH],
            owned_mix[:, mix_edge:token_offset],
        ],
        axis=1,
    )
    owned_out = owned_mid[:, mixer_width:]
    return (
        layer_out,
        grad_hidden,
        owned_in,
        owned_out.T,
        owned_feed[:, : 2 * FF],
        owned_feed[:, 2 * FF :].T,
        total_norm,
        total_feed,
        total_bias,
        total_decay,
        total_skip,
    )


def solution(mesh):
    return jax.shard_map(
        local,
        mesh=mesh,
        in_specs=(
            P(("fsdp", "ctx"), None),
            P(("fsdp", "ctx")),
            P(("fsdp", "ctx"), None),
            P(("fsdp", "ctx"), None),
            P(None, ("fsdp", "ctx")),
            P(("fsdp", "ctx"), None),
            P(None, ("fsdp", "ctx")),
            P(),
            P(),
            P(),
            P(),
            P(),
        ),
        out_specs=(
            P(("fsdp", "ctx"), None),
            P(("fsdp", "ctx"), None),
            P(("fsdp", "ctx"), None),
            P(None, ("fsdp", "ctx")),
            P(("fsdp", "ctx"), None),
            P(None, ("fsdp", "ctx")),
            P(),
            P(),
            P(),
            P(),
            P(),
        ),
        check_vma=False,
    )
```
